32 devices in a mesh: frame: 8 (over z, x), fsdp: 4 (over y, core).
Axes of the slice: x: 2, y: 2, z: 4, core: 2. Of those that a mesh axis runs over, the one named last changes fastest.
Arguments:
- queries: bfloat16 [32, 192, 3072], P(('frame', 'fsdp')), may hold values from -18 to 18
- keys: bfloat16 [32, 192, 3072], P(('frame', 'fsdp')), may hold values from -7 to 7
- values: bfloat16 [32, 192, 3072], P(('frame', 'fsdp')), may hold values from -6 to 6
- residual: bfloat16 [32, 192, 3072], P(('frame', 'fsdp')), may hold values from -6 to 6
- target: bfloat16 [32, 192, 3072], P(('frame', 'fsdp')), may hold values from -6 to 6
- output_weight: bfloat16 [3072, 3072], P('fsdp'), may hold values from -0.109375 to 0.109375
- down_adapter: bfloat16 [8, 64, 3072], P('frame', None, 'fsdp'), may hold values from -0.109375 to 0.109375
- up_adapter: bfloat16 [8, 64, 3072], P('frame', None, 'fsdp'), may hold values from -1.1953125 to 1.1953125
- scene_of_frame: int32 [32], P(('frame', 'fsdp')), may hold values from 0 to 7
- scene_adapter_row: int32 [8], replicated, may hold values from 0 to 7, each once
- valid_token_count: int32 [32], P(('frame', 'fsdp')), may hold values from 1 to 192, 3840 in all
Outputs:
- grad_down: float32 [8, 64, 3072], P('frame', None, 'fsdp')
- grad_up: float32 [8, 64, 3072], P('frame', None, 'fsdp')
- frame_loss: float32 [32], P(('frame', 'fsdp'))
The draws below stay inside these ranges and needn't reach their ends.
Inputs may be any that keep to these rules, and one draw needn't show every extreme that they name: `scene_adapter_row`: each scene has its own adapter row. `valid_token_count`: some frame has all 192 slots valid.
All inputs are finite; a program needn't handle non-finite values. No bound on the sum of `valid_token_count` on one device may be relied on, other than what follows from the above.
Results may differ from the reference program's by a relative error of at most 0.0053.
Values may be sent and summed in bfloat16 or wider, within the bound.
No kernel may reach another device: no remote copies, remote signals or barrier semaphores. Data moves between devices by JAX's collectives and lax.ppermute only.
A program may use at most 192 MiB of HBM per device.

```python
import math
import jax
import jax.numpy as jnp
import numpy as np
from jax import lax

MODEL_DIM = 3072
HEADS = 24
HD = 128
ADAPTER_RANK = 64
FT = 192
FRAMES = 32
SCENE_COUNT = 8


def key_field(key):
    field_base = jnp.clip(jax.random.normal(jax.random.fold_in(key, 31), (FRAMES, FT, MODEL_DIM), jnp.float32), -6.0, 6.0)
    return field_base


def draw_keys(key, part):
    return key_field(key).astype(jnp.bfloat16)


def draw_queries(key, part):
    query_base = jnp.clip(jax.random.normal(jax.random.fold_in(key, 41), (FRAMES, FT, MODEL_DIM), jnp.float32), -6.0, 6.0)
    return query_base.astype(jnp.bfloat16)


def with_ends(values, rng, smallest, top_value):
    longest = values.shape.index(max(values.shape))
    spots = []
    for shift in (0, 1):
        where = [jax.random.randint(jax.random.fold_in(rng, axis), (), 0, length) for axis, length in enumerate(values.shape)]
        where[longest] = (where[longest] + shift) % values.shape[longest]
        spots.append(tuple(where))
    return values.at[spots[0]].set(smallest).at[spots[1]].set(top_value)


def steps_of(rng, shape, cuts, least, largest):
    def one(axis_at, blocks):
        steps = jax.random.uniform(jax.random.fold_in(jax.random.fold_in(rng, 6), axis_at), (blocks,), jnp.float32, least / len(cuts), largest / len(cuts))
        return jnp.repeat(jnp.exp(steps), shape[axis_at] // blocks).reshape((-1,) + (1,) * (len(shape) - axis_at - 1))

    level = one(*cuts[0])
    for cut in cuts[1:]:
        level = level * one(*cut)
    return level


def rank_table(count, skew):
    portions = [(1 << 20) // math.isqrt(rank ** skew) + 1 for rank in range(1, count + 1)]
    deviation = 1 + sum(portions) // (1 << 30)
    return np.cumsum(np.array([max(1, weight // deviation) for weight in portions]))


def ranked(own_key, dims, amount, lean):
    grid = rank_table(amount, lean)
    ticket = jax.random.randint(jax.random.fold_in(own_key, 1), dims, 0, int(grid[amount - 1]))
    grade = jnp.searchsorted(jnp.asarray(grid, jnp.int32), ticket, side="right")
    return jax.random.permutation(jax.random.fold_in(own_key, 2), amount)[grade].astype(jnp.int32)


def length_profile(count, total, limit, skew):
    weights = [(1 << 20) // math.isqrt(grade ** skew) + 1 for grade in range(2, count + 1)]
    rest, counts = total - limit - (count - 1), [1] * (count - 1)
    while rest > 0:
        movable = [i for i in range(count - 1) if counts[i] < limit]
        mass, left = sum([weights[i] for i in movable]), rest
        for i in movable:
            addition = min(limit - counts[i], max(1, left * weights[i] // mass), rest)
            counts[i] = counts[i] + addition
            rest = rest - addition
    return np.array([limit] + counts)


def ragged(stream_key, count, total, bound, skew):
    if count == 2:
        one = jax.random.randint(stream_key, (), max(1, total - bound), min(bound, total - 1) + 1)
        return jnp.stack([one, total - one])
    sizes = jnp.asarray(length_profile(count, total, bound, skew), jnp.int32)
    twos = (count - 1) // 2
    giver, receiver = sizes[1:1 + 2 * twos:2], sizes[2:2 + 2 * twos:2]
    room = jnp.minimum(giver - 1, bound - receiver)
    passed = jax.random.randint(jax.random.fold_in(stream_key, 1), (twos,), 0, 1 << 20) % (room + 1)
    sizes = sizes.at[1:1 + 2 * twos:2].set(giver - passed).at[2:2 + 2 * twos:2].set(receiver + passed)
    return sizes[jax.random.permutation(jax.random.fold_in(stream_key, 2), count)]


def scatter_about(own_key, extent, width, bound, split=(), kind=jnp.bfloat16):
    drawn = width * jax.random.normal(own_key, extent, jnp.float32)
    if split:
        drawn = drawn * steps_of(own_key, extent, split, -0.22, 0.18)
    return jnp.clip(drawn, -bound, bound).astype(kind)


def setup_inputs(seed: int = 0) -> dict:
    arg_keys = jax.random.split(jax.random.key(seed), 12)
    return {
        "queries": draw_queries(jax.random.fold_in(arg_keys[11], 71), 0),
        "keys": draw_keys(jax.random.fold_in(arg_keys[11], 71), 0),
        "values": scatter_about(arg_keys[2], (FRAMES, FT, MODEL_DIM), 1.0, 6.0, ((0, 32),)),
        "residual": scatter_about(arg_keys[3], (FRAMES, FT, MODEL_DIM), 1.0, 6.0, ((0, 32),)),
        "target": scatter_about(arg_keys[4], (FRAMES, FT, MODEL_DIM), 1.0, 6.0, ((0, 32),)),
        "output_weight": scatter_about(arg_keys[5], (MODEL_DIM, MODEL_DIM), MODEL_DIM ** -0.5, 0.109375, ((0, 4),)),
        "down_adapter": scatter_about(arg_keys[6], (SCENE_COUNT, ADAPTER_RANK, MODEL_DIM), MODEL_DIM ** -0.5, 0.109375, ((0, 8), (2, 4))),
        "up_adapter": scatter_about(arg_keys[7], (SCENE_COUNT, ADAPTER_RANK, MODEL_DIM), 0.2, 1.1953125, ((0, 8), (2, 4))),
        "scene_of_frame": with_ends(ranked(arg_keys[8], (FRAMES,), SCENE_COUNT, 2), jax.random.fold_in(arg_keys[8], 3), 0, SCENE_COUNT - 1).astype(jnp.int32),
        "scene_adapter_row": jax.random.permutation(arg_keys[9], SCENE_COUNT).astype(jnp.int32),
        "valid_token_count": ragged(arg_keys[10], FRAMES, FRAMES * FT * 5 // 8, FT, 1).astype(jnp.int32),
    }


adapter_scale = 2.0

def attend_frame(query_frame, key_frame, value_frame, valid_mask):
    query_heads = query_frame.astype(jnp.float32).reshape(FT, HEADS, HD)
    key_heads = key_frame.astype(jnp.float32).reshape(FT, HEADS, HD)
    value_heads = value_frame.astype(jnp.float32).reshape(FT, HEADS, HD)
    scores = jnp.einsum('qhd,khd->hqk', query_heads, key_heads) * (1.0 / math.sqrt(HD))
    scores = jnp.where(valid_mask[None, None, :], scores, -jnp.inf)
    row_max = lax.optimization_barrier(jnp.max(scores, axis=-1, keepdims=True))
    exponent = jnp.exp(scores - row_max)
    weights = (exponent / lax.optimization_barrier(jnp.sum(exponent, axis=-1, keepdims=True))).astype(jnp.bfloat16)
    attended = jnp.einsum('hqk,khd->qhd', weights.astype(jnp.float32), value_heads)
    return attended.reshape(FT, MODEL_DIM).astype(jnp.bfloat16)

def reference(queries, keys, values, residual, target, output_weight, down_adapter, up_adapter, scene_of_frame, scene_adapter_row, valid_token_count):
    weight_wide = output_weight.astype(jnp.float32)
    slot_list = scene_adapter_row[scene_of_frame].astype(jnp.int32)

    def one_frame(running, inputs):
        query_frame, key_frame, value_frame, residual_frame, target_frame_value, token_total, adapter_slot_index = inputs
        valid_mask = jnp.arange(FT, dtype=jnp.int32) < token_total
        attended = attend_frame(query_frame, key_frame, value_frame, valid_mask)
        projected_tokens = jnp.dot(attended.astype(jnp.float32), weight_wide, preferred_element_type=jnp.float32)
        down_weight_rows = down_adapter[adapter_slot_index]
        up_weight_rows = up_adapter[adapter_slot_index]
        low_rank_state = jnp.dot(attended, down_weight_rows.T, preferred_element_type=jnp.float32).astype(jnp.bfloat16)
        adapter_output = jnp.dot(low_rank_state, up_weight_rows, preferred_element_type=jnp.float32)
        combined_output = residual_frame.astype(jnp.float32) + projected_tokens + adapter_scale * adapter_output - target_frame_value.astype(jnp.float32)
        residual_error = jnp.where(valid_mask[:, None], combined_output, jnp.zeros_like(combined_output))
        token_float = token_total.astype(jnp.float32)
        frame_loss = jnp.sum(residual_error * residual_error) / (token_float * MODEL_DIM)
        output_gradient = (2.0 * residual_error / token_float).astype(jnp.bfloat16)
        up_gradient_terms = adapter_scale * jnp.dot(low_rank_state.T, output_gradient, preferred_element_type=jnp.float32)
        backward_low_rank = (adapter_scale * jnp.dot(output_gradient, up_weight_rows.T, preferred_element_type=jnp.float32)).astype(jnp.bfloat16)
        down_terms = jnp.dot(backward_low_rank.T, attended, preferred_element_type=jnp.float32)
        sum_down, sum_up = running
        return ((sum_down.at[adapter_slot_index].add(down_terms), sum_up.at[adapter_slot_index].add(up_gradient_terms)), frame_loss)
    start_sums = (jnp.zeros((SCENE_COUNT, ADAPTER_RANK, MODEL_DIM), jnp.float32), jnp.zeros((SCENE_COUNT, ADAPTER_RANK, MODEL_DIM), jnp.float32))
    (grad_down, grad_up), frame_loss = lax.scan(one_frame, start_sums, (queries, keys, values, residual, target, valid_token_count, slot_list))
    return (grad_down, grad_up, frame_loss)
```

```python
import math

import jax
import jax.numpy as jnp
from jax import lax
from jax.sharding import PartitionSpec as P

HEADS = 24
ADAPTER_SCALE = 2.0
F32 = jnp.float32
BF16 = jnp.bfloat16


def xor_send(value, axis, size, offset):
    return lax.ppermute(value, axis, [(i, i ^ offset) for i in range(size)])


def split_axis(size):
    inner = 1 << ((size.bit_length() - 1) // 2)
    return size // inner, inner


def gather_scenes(block, size):
    outer, inner = split_axis(size)
    first = [block]
    for step in range(1, outer):
        first.append(xor_send(block, "frame", size, step * inner))
    out = [None] * size
    for step in range(outer):
        out[step * inner] = first[step]
    for step in range(1, inner):
        for lead in range(outer):
            out[lead * inner + step] = xor_send(first[lead], "frame", size, step)
    return jnp.stack(out)


def scatter_scenes(dense, size, inner_first):
    outer, inner = split_axis(size)
    near, far = (inner, outer) if inner_first else (outer, inner)
    near_mul, far_mul = (1, inner) if inner_first else (inner, 1)

    def at(f, s):
        return dense[f * far_mul + s * near_mul]

    staged = [at(f, 0) for f in range(far)]
    for step in range(1, near):
        sent = jnp.stack([at(f, step) for f in range(far)]).astype(BF16)
        got = xor_send(sent, "frame", size, step * near_mul)
        staged = [staged[f] + got[f].astype(F32) for f in range(far)]
    total = staged[0]
    for step in range(1, far):
        total = total + xor_send(staged[step].astype(BF16), "frame", size, step * far_mul).astype(F32)
    return total


def attend(queries, keys, values, valid):
    slots, width = queries.shape
    size = width // HEADS
    q = queries.reshape(slots, HEADS, size)
    k = keys.reshape(slots, HEADS, size)
    v = values.reshape(slots, HEADS, size)
    scores = jnp.einsum("qhd,khd->hqk", q, k, preferred_element_type=F32) * (1.0 / math.sqrt(size))
    scores = jnp.where(valid[None, None, :], scores, -jnp.inf)
    peak = jnp.max(scores, axis=-1, keepdims=True)
    exponent = jnp.exp(scores - peak)
    weights = (exponent / jnp.sum(exponent, axis=-1, keepdims=True)).astype(BF16)
    out = jnp.einsum("hqk,khd->qhd", weights, v, preferred_element_type=F32)
    return out.astype(BF16).reshape(slots, width)


def dot(a, b, ca, cb):
    return lax.dot_general(a, b, (((ca,), (cb,)), ((), ())), preferred_element_type=F32)


def make_per_device(frame_size, fsdp_size):
    chips = fsdp_size // 2

    def per_device(
        queries,
        keys,
        values,
        residual,
        target,
        output_weight,
        down_adapter,
        up_adapter,
        scene_of_frame,
        scene_adapter_row,
        valid_token_count,
    ):
        slots, width = queries.shape[1:]
        depth = output_weight.shape[0]
        shard = lax.axis_index("fsdp")
        group = lax.axis_index("frame")
        core = shard % 2
        chip = shard // 2

        weight_near = xor_send(output_weight, "fsdp", fsdp_size, 1)
        blocks = gather_scenes(jnp.concatenate([down_adapter, up_adapter], axis=0), frame_size)
        own_slot = scene_adapter_row[scene_of_frame[0]]
        offsets = [own_slot ^ group]
        for step in range(1, fsdp_size):
            offsets.append(xor_send(own_slot[None], "fsdp", fsdp_size, step)[0] ^ group)

        count = valid_token_count[0]
        valid = jnp.arange(slots, dtype=jnp.int32) < count
        attended = attend(queries[0], keys[0], values[0], valid)

        def partial(columns):
            mine = lax.dynamic_slice_in_dim(columns, core * depth, depth, 1)
            near = lax.dynamic_slice_in_dim(columns, (1 - core) * depth, depth, 1)
            return dot(mine, output_weight, 1, 0) + dot(near, weight_near, 1, 0)

        def chip_columns(which):
            return lax.dynamic_slice_in_dim(attended, which * 2 * depth, 2 * depth, 1)

        received = []
        for step in range(1, chips):
            theirs = xor_send(chip_columns(chip ^ step), "fsdp", fsdp_size, 2 * step)
            received.append(xor_send(partial(theirs).astype(BF16), "fsdp", fsdp_size, 2 * step))
        projected = partial(chip_columns(chip))
        for got in received:
            projected = projected + got.astype(F32)

        chosen = []
        for step in range(fsdp_size):
            pick = lax.dynamic_index_in_dim(blocks, offsets[step], 0, keepdims=False)
            chosen.append(pick if step == 0 else xor_send(pick, "fsdp", fsdp_size, step))
        adapters = jnp.zeros((2, down_adapter.shape[1], width), BF16)
        for step in range(fsdp_size):
            adapters = lax.dynamic_update_slice_in_dim(adapters, chosen[step], (shard ^ step) * depth, 2)
        down, up = adapters[0], adapters[1]

        low = dot(attended, down, 1, 1).astype(BF16)
        combined = (
            residual[0].astype(F32) + projected + ADAPTER_SCALE * dot(low, up, 1, 0) - target[0].astype(F32)
        )
        error = jnp.where(valid[:, None], combined, 0.0)
        tokens = count.astype(F32)
        loss = jnp.sum(error * error) / (tokens * width)
        cotangent = (2.0 * error / tokens).astype(BF16)
        up_terms = ADAPTER_SCALE * dot(low, cotangent, 0, 0)
        back = (ADAPTER_SCALE * dot(cotangent, up, 1, 1)).astype(BF16)
        down_terms = dot(back, attended, 0, 0)
        terms = jnp.concatenate([down_terms, up_terms], axis=0)

        pieces = []
        for step in range(fsdp_size):
            piece = lax.dynamic_slice_in_dim(terms, (shard ^ step) * depth, depth, 1)
            pieces.append(piece if step == 0 else xor_send(piece.astype(BF16), "fsdp", fsdp_size, step).astype(F32))
        dense = []
        for scene in range(frame_size):
            total = jnp.zeros_like(pieces[0])
            for offset, piece in zip(offsets, pieces):
                total = total + jnp.where(offset == scene, piece, 0.0)
            dense.append(total)
        dense = jnp.stack(dense)
        rank = down_adapter.shape[1]
        cut = 2 * rank * 5 // 8
        top = scatter_scenes(dense[:, :cut], frame_size, True)
        bottom = scatter_scenes(dense[:, cut:], frame_size, False)
        owned = jnp.concatenate([top, bottom], axis=0)
        return owned[None, :rank], owned[None, rank:], loss[None]

    return per_device


def solution(mesh):
    rows = P(("frame", "fsdp"), None, None)
    adapter = P("frame", None, "fsdp")
    vector = P(("frame", "fsdp"))
    placed = (rows, rows, rows, rows, rows, P("fsdp", None), adapter, adapter, vector, P(), vector)
    return jax.shard_map(
        make_per_device(mesh.shape["frame"], mesh.shape["fsdp"]),
        mesh=mesh,
        in_specs=placed,
        out_specs=(adapter, adapter, vector),
        check_vma=False,
    )
```

```python
import math

import jax
import jax.numpy as jnp
from jax import lax
from jax.experimental import pallas as pl
from jax.experimental.pallas import tpu as pltpu
from jax.sharding import PartitionSpec as P

HEADS = 24
ADAPTER_SCALE = 2.0
F32 = jnp.float32
BF16 = jnp.bfloat16


def xor_send(value, axis, size, offset):
    return lax.ppermute(value, axis, [(i, i ^ offset) for i in range(size)])


def split_axis(size):
    inner = 1 << ((size.bit_length() - 1) // 2)
    return size // inner, inner


def gather_scenes(block, size):
    outer, inner = split_axis(size)
    first = [block]
    for step in range(1, outer):
        first.append(xor_send(block, "frame", size, step * inner))
    out = [None] * size
    for step in range(outer):
        out[step * inner] = first[step]
    for step in range(1, inner):
        for lead in range(outer):
            out[lead * inner + step] = xor_send(first[lead], "frame", size, step)
    return jnp.stack(out)


def scatter_scenes(dense, size, inner_first):
    outer, inner = split_axis(size)
    near, far = (inner, outer) if inner_first else (outer, inner)
    near_mul, far_mul = (1, inner) if inner_first else (inner, 1)

    def at(f, s):
        return dense[f * far_mul + s * near_mul]

    staged = [at(f, 0) for f in range(far)]
    for step in range(1, near):
        sent = jnp.stack([at(f, step) for f in range(far)]).astype(BF16)
        got = xor_send(sent, "frame", size, step * near_mul)
        staged = [staged[f] + got[f].astype(F32) for f in range(far)]
    total = staged[0]
    for step in range(1, far):
        total = total + xor_send(staged[step].astype(BF16), "frame", size, step * far_mul).astype(F32)
    return total


def attend(queries, keys, values, valid):
    slots, width = queries.shape
    size = width // HEADS
    q = queries.reshape(slots, HEADS, size)
    k = keys.reshape(slots, HEADS, size)
    v = values.reshape(slots, HEADS, size)
    scores = jnp.einsum("qhd,khd->hqk", q, k, preferred_element_type=F32) * (1.0 / math.sqrt(size))
    scores = jnp.where(valid[None, None, :], scores, -jnp.inf)
    peak = jnp.max(scores, axis=-1, keepdims=True)
    exponent = jnp.exp(scores - peak)
    weights = (exponent / jnp.sum(exponent, axis=-1, keepdims=True)).astype(BF16)
    out = jnp.einsum("hqk,khd->qhd", weights, v, preferred_element_type=F32)
    return out.astype(BF16).reshape(slots, width)


def dot(a, b, ca, cb):
    return lax.dot_general(a, b, (((ca,), (cb,)), ((), ())), preferred_element_type=F32)


def make_general(frame_size, fsdp_size):
    chips = fsdp_size // 2

    def per_device(
        queries,
        keys,
        values,
        residual,
        target,
        output_weight,
        down_adapter,
        up_adapter,
        scene_of_frame,
        scene_adapter_row,
        valid_token_count,
    ):
        slots, width = queries.shape[1:]
        depth = output_weight.shape[0]
        shard = lax.axis_index("fsdp")
        group = lax.axis_index("frame")
        core = shard % 2
        chip = shard // 2

        weight_near = xor_send(output_weight, "fsdp", fsdp_size, 1)
        blocks = gather_scenes(jnp.concatenate([down_adapter, up_adapter], axis=0), frame_size)
        own_slot = scene_adapter_row[scene_of_frame[0]]
        offsets = [own_slot ^ group]
        for step in range(1, fsdp_size):
            offsets.append(xor_send(own_slot[None], "fsdp", fsdp_size, step)[0] ^ group)

        count = valid_token_count[0]
        valid = jnp.arange(slots, dtype=jnp.int32) < count
        attended = attend(queries[0], keys[0], values[0], valid)

        def partial(columns):
            mine = lax.dynamic_slice_in_dim(columns, core * depth, depth, 1)
            near = lax.dynamic_slice_in_dim(columns, (1 - core) * depth, depth, 1)
            return dot(mine, output_weight, 1, 0) + dot(near, weight_near, 1, 0)

        def chip_columns(which):
            return lax.dynamic_slice_in_dim(attended, which * 2 * depth, 2 * depth, 1)

        received = []
        for step in range(1, chips):
            theirs = xor_send(chip_columns(chip ^ step), "fsdp", fsdp_size, 2 * step)
            received.append(xor_send(partial(theirs).astype(BF16), "fsdp", fsdp_size, 2 * step))
        projected = partial(chip_columns(chip))
        for got in received:
            projected = projected + got.astype(F32)

        chosen = []
        for step in range(fsdp_size):
            pick = lax.dynamic_index_in_dim(blocks, offsets[step], 0, keepdims=False)
            chosen.append(pick if step == 0 else xor_send(pick, "fsdp", fsdp_size, step))
        adapters = jnp.zeros((2, down_adapter.shape[1], width), BF16)
        for step in range(fsdp_size):
            adapters = lax.dynamic_update_slice_in_dim(adapters, chosen[step], (shard ^ step) * depth, 2)
        down, up = adapters[0], adapters[1]

        low = dot(attended, down, 1, 1).astype(BF16)
        combined = (
            residual[0].astype(F32) + projected + ADAPTER_SCALE * dot(low, up, 1, 0) - target[0].astype(F32)
        )
        error = jnp.where(valid[:, None], combined, 0.0)
        tokens = count.astype(F32)
        loss = jnp.sum(error * error) / (tokens * width)
        cotangent = (2.0 * error / tokens).astype(BF16)
        up_terms = ADAPTER_SCALE * dot(low, cotangent, 0, 0)
        back = (ADAPTER_SCALE * dot(cotangent, up, 1, 1)).astype(BF16)
        down_terms = dot(back, attended, 0, 0)
        terms = jnp.concatenate([down_terms, up_terms], axis=0)

        pieces = []
        for step in range(fsdp_size):
            piece = lax.dynamic_slice_in_dim(terms, (shard ^ step) * depth, depth, 1)
            pieces.append(piece if step == 0 else xor_send(piece.astype(BF16), "fsdp", fsdp_size, step).astype(F32))
        dense = []
        for scene in range(frame_size):
            total = jnp.zeros_like(pieces[0])
            for offset, piece in zip(offsets, pieces):
                total = total + jnp.where(offset == scene, piece, 0.0)
            dense.append(total)
        dense = jnp.stack(dense)
        rank = down_adapter.shape[1]
        cut = 2 * rank * 5 // 8
        top = scatter_scenes(dense[:, :cut], frame_size, True)
        bottom = scatter_scenes(dense[:, cut:], frame_size, False)
        owned = jnp.concatenate([top, bottom], axis=0)
        return owned[None, :rank], owned[None, rank:], loss[None]

    return per_device


LANES = 128
CHUNKS = 2
VMEM = 48 * 1024 * 1024
SHARD, CORE, CHIP, COUNT, OFFSETS = 0, 1, 2, 3, 4


def kernel_call(body, name, scalars, operands, out_shape, grid=None, in_specs=None, out_specs=None, scratch=()):
    whole = lambda shape: pl.BlockSpec(shape, lambda *_: (0,) * len(shape))
    if in_specs is None:
        in_specs = [whole(x.shape) for x in operands]
    if out_specs is None:
        out_specs = jax.tree.map(lambda x: whole(x.shape), out_shape)
    return pl.pallas_call(
        body,
        out_shape=out_shape,
        grid_spec=pltpu.PrefetchScalarGridSpec(
            num_scalar_prefetch=1,
            grid=grid or (1,),
            in_specs=in_specs,
            out_specs=out_specs,
            scratch_shapes=list(scratch),
        ),
        compiler_params=pltpu.CompilerParams(vmem_limit_bytes=VMEM),
        name=name,
    )(scalars, *operands)


def shaped(shape, dtype=BF16):
    return jax.ShapeDtypeStruct(shape, dtype)


def attend_chip(scalars, queries, keys, values, chip_offset, depth):
    slots, width = queries.shape[1:]
    size = width // HEADS
    heads = max(h for h in (3, 2, 1) if depth % (h * size) == 0)
    parts = depth // (heads * size)

    def body(sc, q_ref, k_ref, v_ref, out_ref):
        seen = lax.broadcasted_iota(jnp.int32, (1, slots), 1) < sc[COUNT]
        for h in range(heads):
            at = slice(h * size, (h + 1) * size)
            scores = dot(q_ref[0, :, at], k_ref[0, :, at], 1, 1) * (1.0 / math.sqrt(size))
            scores = jnp.where(seen, scores, -1e30)
            exponent = jnp.exp(scores - jnp.max(scores, axis=1, keepdims=True))
            weights = exponent / jnp.sum(exponent, axis=1, keepdims=True)
            out_ref[0, :, at] = dot(weights.astype(BF16), v_ref[0, :, at], 1, 0).astype(BF16)

    def block(c, p, sc):
        return (0, 0, ((sc[CHIP] ^ chip_offset) * 2 + (sc[CORE] ^ c)) * parts + p)

    spec = pl.BlockSpec((1, slots, heads * size), block)
    return kernel_call(
        body,
        "attend",
        scalars,
        (queries, keys, values),
        shaped((2, slots, depth)),
        grid=(2, parts),
        in_specs=[spec] * 3,
        out_specs=pl.BlockSpec((1, slots, heads * size), lambda c, p, sc: (c, 0, p)),
    )


def project_chunk(scalars, columns, weight, weight_near, chip_offset, chunk, size):
    _, slots, depth = columns.shape
    w = depth // CHUNKS

    def body(sc, x_ref, own_ref, near_ref, out_ref):
        out_ref[0] = (dot(x_ref[0], own_ref[...], 1, 0) + dot(x_ref[1], near_ref[...], 1, 0)).astype(BF16)

    cols = pl.BlockSpec((depth, w), lambda k, sc: (0, (sc[SHARD] ^ (2 * chip_offset) ^ k) * CHUNKS + chunk))
    return kernel_call(
        body,
        "project",
        scalars,
        (columns, weight, weight_near),
        shaped((size, slots, w)),
        grid=(size,),
        in_specs=[pl.BlockSpec(columns.shape, lambda k, sc: (0, 0, 0)), cols, cols],
        out_specs=pl.BlockSpec((1, slots, w), lambda k, sc: (k, 0, 0)),
    )


def low_rank(scalars, attended, adapters):
    slots = attended[0].shape[1]
    rank = adapters[0].shape[0] // 2
    chips = len(attended)

    def body(sc, *refs):
        total = 0.0
        for k in range(2 * chips):
            total = total + dot(refs[k // 2][k % 2], refs[chips + k][:rank, :], 1, 1)
        refs[-1][...] = total.astype(BF16)

    return kernel_call(body, "low_rank", scalars, (*attended, *adapters), shaped((slots, rank)))


def base_chunk(scalars, columns, weight, weight_near, low, adapters, residual, target, chunk):
    _, slots, depth = columns.shape
    size = len(adapters)
    rank = adapters[0].shape[0] // 2
    w = depth // CHUNKS

    def body(sc, x_ref, own_ref, near_ref, low_ref, r_ref, t_ref, *refs):
        k = pl.program_id(0)
        up = refs[0][...]
        for step in range(1, size):
            up = jnp.where(k == step, refs[step][...], up)
        total = dot(x_ref[0], own_ref[...], 1, 0) + dot(x_ref[1], near_ref[...], 1, 0)
        total = total + ADAPTER_SCALE * dot(low_ref[...], up, 1, 0)
        refs[-1][0] = total + r_ref[0].astype(F32) - t_ref[0].astype(F32)

    place = lambda k, sc: (sc[SHARD] ^ k) * CHUNKS + chunk
    cols = pl.BlockSpec((depth, w), lambda k, sc: (0, place(k, sc)))
    tokens = pl.BlockSpec((1, slots, w), lambda k, sc: (0, 0, place(k, sc)))
    return kernel_call(
        body,
        "base",
        scalars,
        (columns, weight, weight_near, low, residual, target, *adapters),
        shaped((size, slots, w), F32),
        grid=(size,),
        in_specs=[
            pl.BlockSpec(columns.shape, lambda k, sc: (0, 0, 0)),
            cols,
            cols,
            pl.BlockSpec(low.shape, lambda k, sc: (0, 0)),
            tokens,
            tokens,
        ]
        + [pl.BlockSpec((rank, w), lambda k, sc: (1, chunk))] * size,
        out_specs=pl.BlockSpec((1, slots, w), lambda k, sc: (k, 0, 0)),
    )


def error_chunk(scalars, base, received, low, adapters, before, chunk):
    size, slots, w = base.shape
    rank = low.shape[1]
    width = size * w * CHUNKS
    last = chunk == CHUNKS - 1
    back_lanes = -(-slots // LANES) * LANES
    ups = pl.BlockSpec((rank, w), lambda k, sc: (1, chunk))
    whole = lambda x: pl.BlockSpec(x.shape, lambda k, sc: (0,) * len(x.shape))
    scalar = pl.BlockSpec(memory_space=pltpu.SMEM)
    peers = len(received)

    def body(sc, base_ref, low_ref, *refs):
        got, refs = refs[:peers], refs[peers:]
        up_refs, refs = refs[:size], refs[size:]
        if before:
            (back_in, loss_in), refs = refs[:2], refs[2:]
        pieces, (back_out, loss_out) = refs[:size], refs[size:]
        count = sc[COUNT]
        tokens = count.astype(F32)
        valid = lax.broadcasted_iota(jnp.int32, (slots, 1), 0) < count
        low_state = low_ref[...]
        back = back_in[...] if before else jnp.zeros((rank, slots), F32)
        squares = jnp.zeros((slots, w), F32)
        for k in range(size):
            error = base_ref[k]
            for ref in got:
                error = error + ref[k].astype(F32)
            error = jnp.where(valid, error, 0.0)
            squares = squares + error * error
            cotangent = (2.0 * error / tokens).astype(BF16)
            back = back + dot(up_refs[k][...], cotangent, 1, 1)
            pieces[k][:, :w] = (ADAPTER_SCALE * dot(low_state, cotangent, 0, 0)).astype(BF16)
        loss = jnp.sum(squares)
        if before:
            loss = loss + loss_in[0, 0]
        if last:
            loss = loss / (tokens * width)
            lanes = (ADAPTER_SCALE * back).astype(BF16)
            lanes = jnp.concatenate([lanes, jnp.zeros((rank, back_lanes - slots), BF16)], axis=1)
            for k in range(size):
                pieces[k][:, w:] = lanes
        back_out[...] = back
        loss_out[0, 0] = loss

    operands = [base, low, *received, *adapters]
    specs = [whole(base), whole(low), *[whole(x) for x in received], *[ups] * size]
    if before:
        operands += list(before)
        specs += [whole(before[0]), scalar]
    piece = shaped((rank, w + (back_lanes if last else 0)))
    out_shape = [piece] * size + [shaped((rank, slots), F32), shaped((1, 1), F32)]
    out_specs = [whole(x) for x in out_shape[:-1]] + [scalar]
    out = kernel_call(body, "error", scalars, operands, out_shape, in_specs=specs, out_specs=out_specs)
    return out[:size], out[size:]


def join_adapters(scalars, down, up):
    _, rank, depth = down.shape

    def body(sc, down_ref, up_ref, out_ref):
        out_ref[:rank, :] = down_ref[0]
        out_ref[rank:, :] = up_ref[0]

    return kernel_call(body, "join_adapters", scalars, (down, up), shaped((2 * rank, depth)))


def choose_adapters(scalars, blocks, size):
    def body(sc, *refs):
        for k in range(size):
            for scene in range(len(blocks)):

                @pl.when(sc[OFFSETS + k] == scene)
                def _():
                    refs[len(blocks) + k][...] = refs[scene][...]

    return kernel_call(body, "choose_adapters", scalars, blocks, [shaped(blocks[0].shape)] * size)


def scene_sum(sc, pieces, scene):
    total = jnp.zeros(pieces[0].shape, F32)
    for k, piece in enumerate(pieces):
        total = total + jnp.where(sc[OFFSETS + k] == scene, piece, 0.0)
    return total


def first_refs(sc, pieces, keep, sends, near, far, near_mul, far_mul):
    for f in range(far):
        keep[f] = scene_sum(sc, pieces, f * far_mul)
        for s in range(1, near):
            sends[s - 1][f] = scene_sum(sc, pieces, f * far_mul + s * near_mul).astype(BF16)


def second_refs(keep, received, final, sends, far):
    for f in range(far):
        total = keep[f]
        for ref in received:
            total = total + ref[f].astype(F32)
        if f == 0:
            final[...] = total
        else:
            sends[f - 1][...] = total.astype(BF16)


def make_chunked(frame_size, fsdp_size):
    chips = fsdp_size // 2
    outer, inner = split_axis(frame_size)
    along_inner = (inner, outer, 1, inner)
    along_outer = (outer, inner, inner, 1)

    def send_frames(arrays, step):
        return [xor_send(x, "frame", frame_size, (i + 1) * step) for i, x in enumerate(arrays)]

    def send_shards(arrays):
        return [arrays[0]] + [xor_send(x, "fsdp", fsdp_size, k) for k, x in enumerate(arrays) if k]

    def first_shapes(rank, w, order):
        near, far = order[:2]
        return [shaped((far, rank, w), F32)] + [shaped((far, rank, w))] * (near - 1)

    def second_shapes(rank, w, order):
        far = order[1]
        return [shaped((rank, w), F32)] + [shaped((rank, w))] * (far - 1)

    def per_device(
        queries,
        keys,
        values,
        residual,
        target,
        output_weight,
        down_adapter,
        up_adapter,
        scene_of_frame,
        scene_adapter_row,
        valid_token_count,
    ):
        depth = output_weight.shape[0]
        rank = down_adapter.shape[1]
        slots = queries.shape[1]
        w = depth // CHUNKS
        shard = lax.axis_index("fsdp").astype(jnp.int32)
        group = lax.axis_index("frame").astype(jnp.int32)
        places = [shard, shard % 2, shard // 2, valid_token_count[0]]
        scalars = jnp.stack(places)

        attended = [attend_chip(scalars, queries, keys, values, c, depth) for c in range(1, chips)]
        theirs = [xor_send(x, "fsdp", fsdp_size, 2 * (c + 1)) for c, x in enumerate(attended)]
        own = attend_chip(scalars, queries, keys, values, 0, depth)
        attended = [own] + attended

        block = join_adapters(scalars, down_adapter, up_adapter)
        blocks = [block] + [xor_send(block, "frame", frame_size, o * inner) for o in range(1, outer)]
        blocks = {o * inner: x for o, x in enumerate(blocks)}
        for lead in range(0, frame_size, inner):
            for step in range(1, inner):
                blocks[lead + step] = xor_send(blocks[lead], "frame", frame_size, step)
        blocks = [blocks[o] for o in range(frame_size)]

        weight_near = xor_send(output_weight, "fsdp", fsdp_size, 1)
        own_slot = scene_adapter_row[scene_of_frame[0]]
        slot_list = [own_slot] + [
            xor_send(own_slot[None], "fsdp", fsdp_size, k)[0] for k in range(1, fsdp_size)
        ]
        scalars = jnp.stack(places + [s ^ group for s in slot_list])

        partials = []
        for chunk in range(CHUNKS):
            partials.append(
                [
                    xor_send(
                        project_chunk(scalars, x, output_weight, weight_near, c + 1, chunk, fsdp_size),
                        "fsdp",
                        fsdp_size,
                        2 * (c + 1),
                    )
                    for c, x in enumerate(theirs)
                ]
            )

        columns = [None] * fsdp_size
        for c, x in enumerate([own] + theirs):
            columns[2 * c] = x[0]
            columns[2 * c + 1] = xor_send(x[1], "fsdp", fsdp_size, 1)

        adapters = send_shards(choose_adapters(scalars, blocks, fsdp_size))
        low = low_rank(scalars, attended, adapters)

        before = None
        finals = []
        for chunk in range(CHUNKS):
            base = base_chunk(
                scalars, own, output_weight, weight_near, low, adapters, residual, target, chunk
            )
            pieces, before = error_chunk(scalars, base, partials[chunk], low, adapters, before, chunk)
            pieces = send_shards(pieces)
            if chunk < CHUNKS - 1:

                def first(sc, *refs):
                    got = [ref[...].astype(F32) for ref in refs[:fsdp_size]]
                    first_refs(sc, got, refs[fsdp_size], refs[fsdp_size + 1 :], *along_inner)

                keep, *sends = kernel_call(first, "first", scalars, pieces, first_shapes(rank, w, along_inner))
                got = send_frames(sends, 1)

                def second(sc, keep_ref, *refs):
                    second_refs(keep_ref, refs[: inner - 1], refs[inner - 1], refs[inner:], outer)

                keep, *sends = kernel_call(
                    second, "second", scalars, (keep, *got), second_shapes(rank, w, along_inner)
                )
                finals.append((keep, *send_frames(sends, inner)))

        down_shapes = first_shapes(rank, depth, along_inner)
        up_shapes = first_shapes(rank, w, along_outer)

        def first_last(sc, *refs):
            got, cols, outs = refs[:fsdp_size], refs[fsdp_size : 2 * fsdp_size], refs[2 * fsdp_size :]
            downs = [dot(p[:, w : w + slots], c[...], 1, 0) for p, c in zip(got, cols)]
            first_refs(sc, downs, outs[0], outs[1:inner], *along_inner)
            ups = [p[:, :w].astype(F32) for p in got]
            first_refs(sc, ups, outs[inner], outs[inner + 1 :], *along_outer)

        out = kernel_call(first_last, "first_last", scalars, (*pieces, *columns), down_shapes + up_shapes)
        down_keep, up_keep = out[0], out[inner]
        down_got = send_frames(out[1:inner], 1)
        up_got = send_frames(out[inner + 1 :], inner)

        def second_last(sc, down_ref, up_ref, *refs):
            downs, refs = refs[: inner - 1], refs[inner - 1 :]
            ups, refs = refs[: outer - 1], refs[outer - 1 :]
            second_refs(down_ref, downs, refs[0], refs[1:outer], outer)
            second_refs(up_ref, ups, refs[outer], refs[outer + 1 :], inner)

        out = kernel_call(
            second_last,
            "second_last",
            scalars,
            (down_keep, up_keep, *down_got, *up_got),
            second_shapes(rank, depth, along_inner) + second_shapes(rank, w, along_outer),
        )
        downs = (out[0], *send_frames(out[1:outer], inner))
        finals.append((out[outer], *send_frames(out[outer + 1 :], 1)))
        lengths = [len(downs)] + [len(x) for x in finals]

        def finish(sc, *refs):
            down_ref, up_ref = refs[-2:]
            start = 0
            for part, length in enumerate(lengths):
                total = refs[start][...]
                for ref in refs[start + 1 : start + length]:
                    total = total + ref[...].astype(F32)
                start += length
                if part == 0:
                    down_ref[0] = total
                else:
                    up_ref[0, :, (part - 1) * w : part * w] = total

        grad = shaped((1, rank, depth), F32)
        grad_down, grad_up = kernel_call(
            finish, "finish", scalars, (*downs, *[x for part in finals for x in part]), [grad, grad]
        )
        return grad_down, grad_up, before[1][0]

    return per_device


def solution(mesh):
    frame_size, fsdp_size = mesh.shape["frame"], mesh.shape["fsdp"]
    rows = P(("frame", "fsdp"), None, None)
    adapter = P("frame", None, "fsdp")
    vector = P(("frame", "fsdp"))
    placed = (rows, rows, rows, rows, rows, P("fsdp", None), adapter, adapter, vector, P(), vector)
    chunked = make_chunked(frame_size, fsdp_size)
    general = make_general(frame_size, fsdp_size)

    def per_device(*operands):
        depth = operands[5].shape[0]
        return (chunked if depth % (LANES * CHUNKS) == 0 else general)(*operands)

    return jax.shard_map(
        per_device,
        mesh=mesh,
        in_specs=placed,
        out_specs=(adapter, adapter, vector),
        check_vma=False,
    )
```

```python
import math

import jax
import jax.numpy as jnp
from jax import lax
from jax.experimental import pallas as pl
from jax.experimental.pallas import tpu as pltpu
from jax.sharding import PartitionSpec as P

HEADS = 24
ADAPTER_SCALE = 2.0
F32 = jnp.float32
BF16 = jnp.bfloat16


def xor_send(value, axis, size, offset):
    return lax.ppermute(value, axis, [(i, i ^ offset) for i in range(size)])


def split_axis(size):
    inner = 1 << ((size.bit_length() - 1) // 2)
    return size // inner, inner


def gather_scenes(block, size):
    outer, inner = split_axis(size)
    first = [block]
    for step in range(1, outer):
        first.append(xor_send(block, "frame", size, step * inner))
    out = [None] * size
    for step in range(outer):
        out[step * inner] = first[step]
    for step in range(1, inner):
        for lead in range(outer):
            out[lead * inner + step] = xor_send(first[lead], "frame", size, step)
    return jnp.stack(out)


def scatter_scenes(dense, size, inner_first):
    outer, inner = split_axis(size)
    near, far = (inner, outer) if inner_first else (outer, inner)
    near_mul, far_mul = (1, inner) if inner_first else (inner, 1)

    def at(f, s):
        return dense[f * far_mul + s * near_mul]

    staged = [at(f, 0) for f in range(far)]
    for step in range(1, near):
        sent = jnp.stack([at(f, step) for f in range(far)]).astype(BF16)
        got = xor_send(sent, "frame", size, step * near_mul)
        staged = [staged[f] + got[f].astype(F32) for f in range(far)]
    total = staged[0]
    for step in range(1, far):
        total = total + xor_send(staged[step].astype(BF16), "frame", size, step * far_mul).astype(F32)
    return total


def attend(queries, keys, values, valid):
    slots, width = queries.shape
    size = width // HEADS
    q = queries.reshape(slots, HEADS, size)
    k = keys.reshape(slots, HEADS, size)
    v = values.reshape(slots, HEADS, size)
    scores = jnp.einsum("qhd,khd->hqk", q, k, preferred_element_type=F32) * (1.0 / math.sqrt(size))
    scores = jnp.where(valid[None, None, :], scores, -jnp.inf)
    peak = jnp.max(scores, axis=-1, keepdims=True)
    exponent = jnp.exp(scores - peak)
    weights = (exponent / jnp.sum(exponent, axis=-1, keepdims=True)).astype(BF16)
    out = jnp.einsum("hqk,khd->qhd", weights, v, preferred_element_type=F32)
    return out.astype(BF16).reshape(slots, width)


def dot(a, b, ca, cb):
    return lax.dot_general(a, b, (((ca,), (cb,)), ((), ())), preferred_element_type=F32)


def make_general(frame_size, fsdp_size):
    chips = fsdp_size // 2

    def per_device(
        queries,
        keys,
        values,
        residual,
        target,
        output_weight,
        down_adapter,
        up_adapter,
        scene_of_frame,
        scene_adapter_row,
        valid_token_count,
    ):
        slots, width = queries.shape[1:]
        depth = output_weight.shape[0]
        shard = lax.axis_index("fsdp")
        group = lax.axis_index("frame")
        core = shard % 2
        chip = shard // 2

        weight_near = xor_send(output_weight, "fsdp", fsdp_size, 1)
        blocks = gather_scenes(jnp.concatenate([down_adapter, up_adapter], axis=0), frame_size)
        own_slot = scene_adapter_row[scene_of_frame[0]]
        offsets = [own_slot ^ group]
        for step in range(1, fsdp_size):
            offsets.append(xor_send(own_slot[None], "fsdp", fsdp_size, step)[0] ^ group)

        count = valid_token_count[0]
        valid = jnp.arange(slots, dtype=jnp.int32) < count
        attended = attend(queries[0], keys[0], values[0], valid)

        def partial(columns):
            mine = lax.dynamic_slice_in_dim(columns, core * depth, depth, 1)
            near = lax.dynamic_slice_in_dim(columns, (1 - core) * depth, depth, 1)
            return dot(mine, output_weight, 1, 0) + dot(near, weight_near, 1, 0)

        def chip_columns(which):
            return lax.dynamic_slice_in_dim(attended, which * 2 * depth, 2 * depth, 1)

        received = []
        for step in range(1, chips):
            theirs = xor_send(chip_columns(chip ^ step), "fsdp", fsdp_size, 2 * step)
            received.append(xor_send(partial(theirs).astype(BF16), "fsdp", fsdp_size, 2 * step))
        projected = partial(chip_columns(chip))
        for got in received:
            projected = projected + got.astype(F32)

        chosen = []
        for step in range(fsdp_size):
            pick = lax.dynamic_index_in_dim(blocks, offsets[step], 0, keepdims=False)
            chosen.append(pick if step == 0 else xor_send(pick, "fsdp", fsdp_size, step))
        adapters = jnp.zeros((2, down_adapter.shape[1], width), BF16)
        for step in range(fsdp_size):
            adapters = lax.dynamic_update_slice_in_dim(adapters, chosen[step], (shard ^ step) * depth, 2)
        down, up = adapters[0], adapters[1]

        low = dot(attended, down, 1, 1).astype(BF16)
        combined = (
            residual[0].astype(F32) + projected + ADAPTER_SCALE * dot(low, up, 1, 0) - target[0].astype(F32)
        )
        error = jnp.where(valid[:, None], combined, 0.0)
        tokens = count.astype(F32)
        loss = jnp.sum(error * error) / (tokens * width)
        cotangent = (2.0 * error / tokens).astype(BF16)
        up_terms = ADAPTER_SCALE * dot(low, cotangent, 0, 0)
        back = (ADAPTER_SCALE * dot(cotangent, up, 1, 1)).astype(BF16)
        down_terms = dot(back, attended, 0, 0)
        terms = jnp.concatenate([down_terms, up_terms], axis=0)

        pieces = []
        for step in range(fsdp_size):
            piece = lax.dynamic_slice_in_dim(terms, (shard ^ step) * depth, depth, 1)
            pieces.append(piece if step == 0 else xor_send(piece.astype(BF16), "fsdp", fsdp_size, step).astype(F32))
        dense = []
        for scene in range(frame_size):
            total = jnp.zeros_like(pieces[0])
            for offset, piece in zip(offsets, pieces):
                total = total + jnp.where(offset == scene, piece, 0.0)
            dense.append(total)
        dense = jnp.stack(dense)
        rank = down_adapter.shape[1]
        cut = 2 * rank * 5 // 8
        top = scatter_scenes(dense[:, :cut], frame_size, True)
        bottom = scatter_scenes(dense[:, cut:], frame_size, False)
        owned = jnp.concatenate([top, bottom], axis=0)
        return owned[None, :rank], owned[None, rank:], loss[None]

    return per_device


LANES = 128
CHUNKS = 2
VMEM = 20 * 1024 * 1024
COST = 1.5e9
ALONE = 52 * 1024 * 1024
SHARD, CORE, CHIP, COUNT, GROUP, OFFSETS = 0, 1, 2, 3, 4, 5


def kernel_call(
    body, name, scalars, operands, out_shape, micros, grid=None, in_specs=None, out_specs=None, after=(), scratch=(), vmem=VMEM
):
    whole = lambda shape: pl.BlockSpec(shape, lambda *_: (0,) * len(shape))
    inner_body = body
    ready = len(operands)

    def body(sc, *refs):
        inner_body(sc, *refs[:ready], *refs[ready + len(after) :])

    if in_specs is None:
        in_specs = [whole(x.shape) for x in operands]
    if out_specs is None:
        out_specs = jax.tree.map(lambda x: whole(x.shape), out_shape)
    return pl.pallas_call(
        body,
        out_shape=out_shape,
        grid_spec=pltpu.PrefetchScalarGridSpec(
            num_scalar_prefetch=1,
            grid=grid or (1,),
            in_specs=[*in_specs, *[pl.BlockSpec(memory_space=pl.ANY)] * len(after)],
            out_specs=out_specs,
            scratch_shapes=list(scratch),
        ),
        compiler_params=pltpu.CompilerParams(vmem_limit_bytes=vmem),
        cost_estimate=pl.CostEstimate(
            flops=int(micros * COST), bytes_accessed=0, transcendentals=0
        ),
        name=name,
    )(scalars, *operands, *after)


def shaped(shape, dtype=BF16):
    return jax.ShapeDtypeStruct(shape, dtype)


def attend_chip(scalars, queries, keys, values, chip_offset, depth, after=()):
    slots, width = queries.shape[1:]
    size = width // HEADS
    heads = depth // size
    scale = math.log2(math.e) / math.sqrt(size)

    def body(sc, q_ref, k_ref, v_ref, out_ref, held, sems):
        def copy(c, i):
            shard = (sc[CHIP] ^ chip_offset) * 2 + (sc[CORE] ^ c)
            lanes = pl.ds(pl.multiple_of(shard * depth, LANES), depth)
            return pltpu.make_async_copy((q_ref, k_ref, v_ref)[i].at[0, :, lanes], held.at[c, i], sems.at[c, i])

        for c in range(2):
            for i in range(3):
                copy(c, i).start()
        seen = lax.broadcasted_iota(jnp.int32, (1, slots), 1) < sc[COUNT]
        at = [slice(h * size, (h + 1) * size) for h in range(heads)]
        for c in range(2):
            for i in range(3):
                copy(c, i).wait()
            q, k, v = (held.at[c, i] for i in range(3))
            scores = [jnp.where(seen, dot(q[:, h], k[:, h], 1, 1), -1e30) for h in at]
            scores = [jnp.exp2((x - jnp.max(x, axis=1, keepdims=True)) * scale) for x in scores]
            weights = [(x * (1.0 / jnp.sum(x, axis=1, keepdims=True))).astype(BF16) for x in scores]
            for h, x in zip(at, weights):
                out_ref[c, :, h] = dot(x, v[:, h], 1, 0).astype(BF16)

    hbm, vmem = pl.BlockSpec(memory_space=pltpu.HBM), pl.BlockSpec(memory_space=pltpu.VMEM)
    return kernel_call(
        body,
        "attend",
        scalars,
        (queries, keys, values),
        shaped((2, slots, depth)),
        4.0,
        in_specs=[hbm] * 3,
        out_specs=vmem,
        after=after,
        scratch=[pltpu.VMEM((2, 3, slots, depth), BF16), pltpu.SemaphoreType.DMA((2, 3))],
        vmem=ALONE,
    )


def project_chunk(scalars, columns, weight, weight_near, chip_offset, chunk, size, after):
    _, slots, depth = columns.shape
    w = depth // CHUNKS

    def body(sc, x_ref, own_ref, near_ref, out_ref):
        for k in range(size):
            place = (sc[SHARD] ^ (2 * chip_offset) ^ k) * CHUNKS + chunk
            cols = pl.ds(pl.multiple_of(place * w, LANES), w)
            out_ref[k] = (dot(x_ref[0], own_ref[:, cols], 1, 0) + dot(x_ref[1], near_ref[:, cols], 1, 0)).astype(BF16)

    vmem = pl.BlockSpec(memory_space=pltpu.VMEM)
    return kernel_call(
        body,
        "project",
        scalars,
        (columns, weight, weight_near),
        shaped((size, slots, w)),
        4.0,
        in_specs=[vmem] * 3,
        out_specs=vmem,
        after=after,
    )


def base_error(scalars, columns, weight, weight_near, residual, target, size, after):
    _, slots, depth = columns.shape
    w = depth // CHUNKS

    def body(sc, x_ref, own_ref, near_ref, r_ref, t_ref, out_ref):
        place = (sc[SHARD] ^ pl.program_id(1)) * CHUNKS + pl.program_id(0)
        cols = pl.ds(pl.multiple_of(place * w, LANES), w)
        total = dot(x_ref[0], own_ref[:, cols], 1, 0) + dot(x_ref[1], near_ref[:, cols], 1, 0)
        out_ref[0, 0] = total + (r_ref[0].astype(F32) - t_ref[0].astype(F32))

    tokens = pl.BlockSpec((1, slots, w), lambda i, k, sc: (0, 0, (sc[SHARD] ^ k) * CHUNKS + i))
    vmem = pl.BlockSpec(memory_space=pltpu.VMEM)
    return kernel_call(
        body,
        "base",
        scalars,
        (columns, weight, weight_near, residual, target),
        shaped((CHUNKS, size, slots, w), F32),
        7.0,
        grid=(CHUNKS, size),
        in_specs=[vmem, vmem, vmem, tokens, tokens],
        out_specs=pl.BlockSpec((1, 1, slots, w), lambda i, k, sc: (i, k, 0, 0)),
        after=after,
    )


def low_rank(scalars, attended, adapters):
    slots = attended[0].shape[1]
    rank = adapters[0].shape[0] // 2
    chips = len(attended)

    def body(sc, *refs):
        total = 0.0
        for k in range(2 * chips):
            total = total + dot(refs[k // 2][k % 2], refs[chips + k][:rank, :], 1, 1)
        refs[-1][...] = total.astype(BF16)

    return kernel_call(body, "low_rank", scalars, (*attended, *adapters), shaped((slots, rank)), 2.0)


def error_terms(scalars, base, received, low, adapters):
    chunks, size, slots, w = base.shape
    rank = low.shape[1]
    depth = chunks * w
    back_lanes = -(-slots // LANES) * LANES
    peers = len(received[0])
    flat = [x for group in received for x in group]

    def body(sc, base_ref, low_ref, *refs):
        got, up_refs, refs = refs[: len(flat)], refs[len(flat) : len(flat) + size], refs[len(flat) + size :]
        pieces, loss_out = refs[:size], refs[size]
        count = sc[COUNT]
        tokens = count.astype(F32)
        valid = lax.broadcasted_iota(jnp.int32, (slots, 1), 0) < count
        low_state = low_ref[...]
        back = jnp.zeros((rank, slots), F32)
        squares = jnp.zeros((slots, w), F32)
        for i in range(chunks):
            at = slice(i * w, (i + 1) * w)
            for k in range(size):
                up = up_refs[k][:, at]
                error = base_ref[i, k] + ADAPTER_SCALE * dot(low_state, up, 1, 0)
                for ref in got[i * peers : (i + 1) * peers]:
                    error = error + ref[k].astype(F32)
                error = jnp.where(valid, error, 0.0)
                squares = squares + error * error
                cotangent = (2.0 * error / tokens).astype(BF16)
                back = back + dot(up, cotangent, 1, 1)
                pieces[k][:, at] = (ADAPTER_SCALE * dot(low_state, cotangent, 0, 0)).astype(BF16)
        loss_out[0, 0] = jnp.sum(squares) / (tokens * (size * depth))
        lanes = (ADAPTER_SCALE * back).astype(BF16)
        lanes = jnp.concatenate([lanes, jnp.zeros((rank, back_lanes - slots), BF16)], axis=1)
        for k in range(size):
            pieces[k][:, depth:] = lanes

    whole = lambda x: pl.BlockSpec(x.shape, lambda k, sc: (0,) * len(x.shape))
    ups = pl.BlockSpec((rank, depth), lambda k, sc: (1, 0))
    out_shape = [shaped((rank, depth + back_lanes))] * size + [shaped((1, 1), F32)]
    out = kernel_call(
        body,
        "error",
        scalars,
        (base, low, *flat, *adapters),
        out_shape,
        4.0,
        in_specs=[whole(base), whole(low), *[whole(x) for x in flat], *[ups] * size],
        out_specs=[whole(x) for x in out_shape[:-1]] + [pl.BlockSpec(memory_space=pltpu.SMEM)],
    )
    return out[:size], out[size]


def join_adapters(scalars, down, up, scene, rows, after):
    _, rank, depth = down.shape

    def body(sc, down_ref, up_ref, scene_ref, row_ref, out_ref, slot_ref):
        out_ref[:rank, :] = down_ref[0]
        out_ref[rank:, :] = up_ref[0]
        slot_ref[0] = row_ref[scene_ref[0]]

    vmem, smem = pl.BlockSpec(memory_space=pltpu.VMEM), pl.BlockSpec(memory_space=pltpu.SMEM)
    return kernel_call(
        body,
        "join",
        scalars,
        (down, up, scene, rows),
        [shaped((2 * rank, depth)), shaped((1,), jnp.int32)],
        1.0,
        in_specs=[vmem, vmem, smem, smem],
        out_specs=[vmem, smem],
        after=after,
    )


def pack_scalars(scalars, slots, after):
    def body(sc, *refs):
        for i in range(OFFSETS):
            refs[-1][i] = sc[i]
        for k in range(len(slots)):
            refs[-1][OFFSETS + k] = refs[k][0] ^ sc[GROUP]

    smem = pl.BlockSpec(memory_space=pltpu.SMEM)
    return kernel_call(
        body,
        "pack",
        scalars,
        slots,
        shaped((OFFSETS + len(slots),), jnp.int32),
        0.5,
        in_specs=[smem] * len(slots),
        out_specs=smem,
        after=after,
    )


def stack_blocks(scalars, blocks, after):
    def body(sc, *refs):
        for i in range(len(blocks)):
            refs[-1][i] = refs[i][...]

    return kernel_call(
        body, "stack", scalars, blocks, shaped((len(blocks), *blocks[0].shape)), 1.0, after=after
    )


def choose_adapters(scalars, blocks, size, after):
    arrays = []
    for x, _ in blocks:
        if all(x is not y for y in arrays):
            arrays.append(x)
    where = [next(i for i, y in enumerate(arrays) if x is y) for x, _ in blocks]
    shape = arrays[0].shape

    def body(sc, *refs):
        for k in range(size):
            for scene, (_, place) in enumerate(blocks):

                @pl.when(sc[OFFSETS + k] == scene)
                def _():
                    ref = refs[where[scene]]
                    refs[len(arrays) + k][...] = ref[...] if place is None else ref[place]

    return kernel_call(body, "choose", scalars, arrays, [shaped(shape)] * size, 2.0, after=after)


def scene_sum(sc, pieces, scene):
    total = jnp.zeros(pieces[0].shape, F32)
    for k, piece in enumerate(pieces):
        total = total + jnp.where(sc[OFFSETS + k] == scene, piece, 0.0)
    return total


def first_refs(sc, pieces, keep, sends, near, far, near_mul, far_mul):
    for f in range(far):
        keep[f] = scene_sum(sc, pieces, f * far_mul)
        for s in range(1, near):
            sends[s - 1][f] = scene_sum(sc, pieces, f * far_mul + s * near_mul).astype(BF16)


def second_refs(keep, received, final, sends, far):
    for f in range(far):
        total = keep[f]
        for ref in received:
            total = total + ref[f].astype(F32)
        if f == 0:
            final[...] = total
        else:
            sends[f - 1][...] = total.astype(BF16)


def make_chunked(frame_size, fsdp_size):
    chips = fsdp_size // 2
    outer, inner = split_axis(frame_size)
    along_inner = (inner, outer, 1, inner)
    along_outer = (outer, inner, inner, 1)

    def send_frames(arrays, step):
        return [xor_send(x, "frame", frame_size, (i + 1) * step) for i, x in enumerate(arrays)]

    def send_shards(arrays):
        return [arrays[0]] + [xor_send(x, "fsdp", fsdp_size, k) for k, x in enumerate(arrays) if k]

    def first_shapes(rank, w, order):
        near, far = order[:2]
        return [shaped((far, rank, w), F32)] + [shaped((far, rank, w))] * (near - 1)

    def second_shapes(rank, w, order):
        far = order[1]
        return [shaped((rank, w), F32)] + [shaped((rank, w))] * (far - 1)

    def per_device(
        queries,
        keys,
        values,
        residual,
        target,
        output_weight,
        down_adapter,
        up_adapter,
        scene_of_frame,
        scene_adapter_row,
        valid_token_count,
    ):
        depth = output_weight.shape[0]
        rank = down_adapter.shape[1]
        slots = queries.shape[1]
        shard = lax.axis_index("fsdp").astype(jnp.int32)
        group = lax.axis_index("frame").astype(jnp.int32)
        places = [shard, shard % 2, shard // 2, valid_token_count[0], group]
        scalars = jnp.stack(places)

        weight_near = xor_send(output_weight, "fsdp", fsdp_size, 1)

        attended = [attend_chip(scalars, queries, keys, values, c, depth) for c in range(1, chips)]
        theirs = [xor_send(x, "fsdp", fsdp_size, 2 * (c + 1)) for c, x in enumerate(attended)]
        block, own_slot = join_adapters(
            scalars, down_adapter, up_adapter, scene_of_frame, scene_adapter_row, attended[:1]
        )
        slot_list = send_shards([own_slot] * fsdp_size)
        outer_blocks = [xor_send(block, "frame", frame_size, o * inner) for o in range(1, outer)]
        inner_blocks = [xor_send(block, "frame", frame_size, s) for s in range(1, inner)]
        own = attend_chip(scalars, queries, keys, values, 0, depth, [block])
        attended = [own] + attended

        partials = []
        after = [own]
        for chunk in range(CHUNKS):
            sent = []
            for c, x in enumerate(theirs):
                part = project_chunk(
                    scalars, x, output_weight, weight_near, c + 1, chunk, fsdp_size, after
                )
                sent.append(xor_send(part, "fsdp", fsdp_size, 2 * (c + 1)))
            partials.append(sent)
            after = [part, *inner_blocks]

        stacked = stack_blocks(scalars, outer_blocks, [part])
        far_blocks = [xor_send(stacked, "frame", frame_size, s) for s in range(1, inner)]
        base = base_error(
            scalars, own, output_weight, weight_near, residual, target, fsdp_size, [stacked]
        )
        blocks = [None] * frame_size
        for o in range(outer):
            blocks[o * inner] = (stacked, o - 1) if o else (block, None)
            for s in range(1, inner):
                blocks[o * inner + s] = (far_blocks[s - 1], o - 1) if o else (inner_blocks[s - 1], None)

        scalars = pack_scalars(scalars, slot_list, [base])
        adapters = send_shards(choose_adapters(scalars, blocks, fsdp_size, [base]))

        columns = [None] * fsdp_size
        for c, x in enumerate([own] + theirs):
            columns[2 * c] = x[0]
            columns[2 * c + 1] = xor_send(x[1], "fsdp", fsdp_size, 1)

        low = low_rank(scalars, attended, adapters)
        pieces, loss = error_terms(scalars, base, partials, low, adapters)
        pieces = send_shards(pieces)

        cut = depth // 3 // LANES * LANES
        first_shape = first_shapes(rank, depth + cut, along_inner) + first_shapes(rank, depth - cut, along_outer)
        second_shape = second_shapes(rank, depth + cut, along_inner) + second_shapes(
            rank, depth - cut, along_outer
        )

        def first(sc, *refs):
            got, cols, outs = refs[:fsdp_size], refs[fsdp_size : 2 * fsdp_size], refs[2 * fsdp_size :]
            downs = [dot(p[:, depth : depth + slots], c[...], 1, 0) for p, c in zip(got, cols)]
            down_outs = [ref.at[:, :, :depth] for ref in outs[:inner]]
            first_refs(sc, downs, down_outs[0], down_outs[1:], *along_inner)
            ups = [p[:, :cut].astype(F32) for p in got]
            up_outs = [ref.at[:, :, depth:] for ref in outs[:inner]]
            first_refs(sc, ups, up_outs[0], up_outs[1:], *along_inner)
            ups = [p[:, cut:depth].astype(F32) for p in got]
            first_refs(sc, ups, outs[inner], outs[inner + 1 :], *along_outer)

        out = kernel_call(first, "first", scalars, (*pieces, *columns), first_shape, 2.0)
        keeps = out[0], out[inner]
        inner_got = send_frames(out[1:inner], 1)
        outer_got = send_frames(out[inner + 1 :], inner)

        def second(sc, inner_keep, outer_keep, *refs):
            inners, refs = refs[: inner - 1], refs[inner - 1 :]
            outers, refs = refs[: outer - 1], refs[outer - 1 :]
            second_refs(inner_keep, inners, refs[0], refs[1:outer], outer)
            second_refs(outer_keep, outers, refs[outer], refs[outer + 1 :], inner)

        out = kernel_call(second, "second", scalars, (*keeps, *inner_got, *outer_got), second_shape, 0.8)
        one = (out[0], *send_frames(out[1:outer], inner))
        two = (out[outer], *send_frames(out[outer + 1 :], 1))

        def finish(sc, *refs):
            down_ref, up_ref = refs[-2:]
            for part, which in ((0, refs[: len(one)]), (1, refs[len(one) : -2])):
                total = which[0][...]
                for ref in which[1:]:
                    total = total + ref[...].astype(F32)
                if part == 0:
                    down_ref[0] = total[:, :depth]
                    up_ref[0, :, :cut] = total[:, depth:]
                else:
                    up_ref[0, :, cut:] = total

        grad = shaped((1, rank, depth), F32)
        grad_down, grad_up = kernel_call(finish, "finish", scalars, (*one, *two), [grad, grad], 1.3)
        return grad_down, grad_up, loss[0]

    return per_device


def solution(mesh):
    frame_size, fsdp_size = mesh.shape["frame"], mesh.shape["fsdp"]
    rows = P(("frame", "fsdp"), None, None)
    adapter = P("frame", None, "fsdp")
    vector = P(("frame", "fsdp"))
    placed = (rows, rows, rows, rows, rows, P("fsdp", None), adapter, adapter, vector, P(), vector)
    chunked = make_chunked(frame_size, fsdp_size)
    general = make_general(frame_size, fsdp_size)

    def per_device(*operands):
        depth = operands[5].shape[0]
        return (chunked if depth % (LANES * CHUNKS) == 0 else general)(*operands)

    return jax.shard_map(
        per_device,
        mesh=mesh,
        in_specs=placed,
        out_specs=(adapter, adapter, vector),
        check_vma=False,
    )
```

```python
import math

import jax
import jax.numpy as jnp
from jax import lax
from jax.experimental import pallas as pl
from jax.experimental.pallas import tpu as pltpu
from jax.sharding import PartitionSpec as P

HEADS = 24
ADAPTER_SCALE = 2.0
F32 = jnp.float32
BF16 = jnp.bfloat16


def xor_send(value, axis, size, offset):
    return lax.ppermute(value, axis, [(i, i ^ offset) for i in range(size)])


def split_axis(size):
    inner = 1 << ((size.bit_length() - 1) // 2)
    return size // inner, inner


def gather_scenes(block, size):
    outer, inner = split_axis(size)
    first = [block]
    for step in range(1, outer):
        first.append(xor_send(block, "frame", size, step * inner))
    out = [None] * size
    for step in range(outer):
        out[step * inner] = first[step]
    for step in range(1, inner):
        for lead in range(outer):
            out[lead * inner + step] = xor_send(first[lead], "frame", size, step)
    return jnp.stack(out)


def scatter_scenes(dense, size, inner_first):
    outer, inner = split_axis(size)
    near, far = (inner, outer) if inner_first else (outer, inner)
    near_mul, far_mul = (1, inner) if inner_first else (inner, 1)

    def at(f, s):
        return dense[f * far_mul + s * near_mul]

    staged = [at(f, 0) for f in range(far)]
    for step in range(1, near):
        sent = jnp.stack([at(f, step) for f in range(far)]).astype(BF16)
        got = xor_send(sent, "frame", size, step * near_mul)
        staged = [staged[f] + got[f].astype(F32) for f in range(far)]
    total = staged[0]
    for step in range(1, far):
        total = total + xor_send(staged[step].astype(BF16), "frame", size, step * far_mul).astype(F32)
    return total


def attend(queries, keys, values, valid):
    slots, width = queries.shape
    size = width // HEADS
    q = queries.reshape(slots, HEADS, size)
    k = keys.reshape(slots, HEADS, size)
    v = values.reshape(slots, HEADS, size)
    scores = jnp.einsum("qhd,khd->hqk", q, k, preferred_element_type=F32) * (1.0 / math.sqrt(size))
    scores = jnp.where(valid[None, None, :], scores, -jnp.inf)
    peak = jnp.max(scores, axis=-1, keepdims=True)
    exponent = jnp.exp(scores - peak)
    weights = (exponent / jnp.sum(exponent, axis=-1, keepdims=True)).astype(BF16)
    out = jnp.einsum("hqk,khd->qhd", weights, v, preferred_element_type=F32)
    return out.astype(BF16).reshape(slots, width)


def dot(a, b, ca, cb):
    return lax.dot_general(a, b, (((ca,), (cb,)), ((), ())), preferred_element_type=F32)


def make_general(frame_size, fsdp_size):
    chips = fsdp_size // 2

    def per_device(
        queries,
        keys,
        values,
        residual,
        target,
        output_weight,
        down_adapter,
        up_adapter,
        scene_of_frame,
        scene_adapter_row,
        valid_token_count,
    ):
        slots, width = queries.shape[1:]
        depth = output_weight.shape[0]
        shard = lax.axis_index("fsdp")
        group = lax.axis_index("frame")
        core = shard % 2
        chip = shard // 2

        weight_near = xor_send(output_weight, "fsdp", fsdp_size, 1)
        blocks = gather_scenes(jnp.concatenate([down_adapter, up_adapter], axis=0), frame_size)
        own_slot = scene_adapter_row[scene_of_frame[0]]
        offsets = [own_slot ^ group]
        for step in range(1, fsdp_size):
            offsets.append(xor_send(own_slot[None], "fsdp", fsdp_size, step)[0] ^ group)

        count = valid_token_count[0]
        valid = jnp.arange(slots, dtype=jnp.int32) < count
        attended = attend(queries[0], keys[0], values[0], valid)

        def partial(columns):
            mine = lax.dynamic_slice_in_dim(columns, core * depth, depth, 1)
            near = lax.dynamic_slice_in_dim(columns, (1 - core) * depth, depth, 1)
            return dot(mine, output_weight, 1, 0) + dot(near, weight_near, 1, 0)

        def chip_columns(which):
            return lax.dynamic_slice_in_dim(attended, which * 2 * depth, 2 * depth, 1)

        received = []
        for step in range(1, chips):
            theirs = xor_send(chip_columns(chip ^ step), "fsdp", fsdp_size, 2 * step)
            received.append(xor_send(partial(theirs).astype(BF16), "fsdp", fsdp_size, 2 * step))
        projected = partial(chip_columns(chip))
        for got in received:
            projected = projected + got.astype(F32)

        chosen = []
        for step in range(fsdp_size):
            pick = lax.dynamic_index_in_dim(blocks, offsets[step], 0, keepdims=False)
            chosen.append(pick if step == 0 else xor_send(pick, "fsdp", fsdp_size, step))
        adapters = jnp.zeros((2, down_adapter.shape[1], width), BF16)
        for step in range(fsdp_size):
            adapters = lax.dynamic_update_slice_in_dim(adapters, chosen[step], (shard ^ step) * depth, 2)
        down, up = adapters[0], adapters[1]

        low = dot(attended, down, 1, 1).astype(BF16)
        combined = (
            residual[0].astype(F32) + projected + ADAPTER_SCALE * dot(low, up, 1, 0) - target[0].astype(F32)
        )
        error = jnp.where(valid[:, None], combined, 0.0)
        tokens = count.astype(F32)
        loss = jnp.sum(error * error) / (tokens * width)
        cotangent = (2.0 * error / tokens).astype(BF16)
        up_terms = ADAPTER_SCALE * dot(low, cotangent, 0, 0)
        back = (ADAPTER_SCALE * dot(cotangent, up, 1, 1)).astype(BF16)
        down_terms = dot(back, attended, 0, 0)
        terms = jnp.concatenate([down_terms, up_terms], axis=0)

        pieces = []
        for step in range(fsdp_size):
            piece = lax.dynamic_slice_in_dim(terms, (shard ^ step) * depth, depth, 1)
            pieces.append(piece if step == 0 else xor_send(piece.astype(BF16), "fsdp", fsdp_size, step).astype(F32))
        dense = []
        for scene in range(frame_size):
            total = jnp.zeros_like(pieces[0])
            for offset, piece in zip(offsets, pieces):
                total = total + jnp.where(offset == scene, piece, 0.0)
            dense.append(total)
        dense = jnp.stack(dense)
        rank = down_adapter.shape[1]
        cut = 2 * rank * 5 // 8
        top = scatter_scenes(dense[:, :cut], frame_size, True)
        bottom = scatter_scenes(dense[:, cut:], frame_size, False)
        owned = jnp.concatenate([top, bottom], axis=0)
        return owned[None, :rank], owned[None, rank:], loss[None]

    return per_device


LANES = 128
VMEM = 20 * 1024 * 1024
COST = 4e8
ALONE = 52 * 1024 * 1024
SHARD, CORE, CHIP, COUNT, GROUP = range(5)


def kernel_call(
    body, name, scalars, operands, out_shape, micros, grid=None, in_specs=None, out_specs=None, after=(), scratch=(), vmem=VMEM
):
    whole = lambda shape: pl.BlockSpec(shape, lambda *_: (0,) * len(shape))
    inner_body = body
    ready = len(operands)

    def body(sc, *refs):
        inner_body(sc, *refs[:ready], *refs[ready + len(after) :])

    if in_specs is None:
        in_specs = [whole(x.shape) for x in operands]
    if out_specs is None:
        out_specs = jax.tree.map(lambda x: whole(x.shape), out_shape)
    return pl.pallas_call(
        body,
        out_shape=out_shape,
        grid_spec=pltpu.PrefetchScalarGridSpec(
            num_scalar_prefetch=1,
            grid=grid or (1,),
            in_specs=[*in_specs, *[pl.BlockSpec(memory_space=pl.ANY)] * len(after)],
            out_specs=out_specs,
            scratch_shapes=list(scratch),
        ),
        compiler_params=pltpu.CompilerParams(vmem_limit_bytes=vmem),
        cost_estimate=pl.CostEstimate(
            flops=int(micros * COST), bytes_accessed=0, transcendentals=0
        ),
        name=name,
    )(scalars, *operands, *after)


def shaped(shape, dtype=BF16):
    return jax.ShapeDtypeStruct(shape, dtype)


def attend_chip(scalars, queries, keys, values, chip_offset, depth, after=()):
    slots, width = queries.shape[1:]
    size = width // HEADS
    heads = depth // size
    scale = math.log2(math.e) / math.sqrt(size)

    def body(sc, q_ref, k_ref, v_ref, out_ref, held, sems):
        def copy(c, i):
            shard = (sc[CHIP] ^ chip_offset) * 2 + (sc[CORE] ^ c)
            lanes = pl.ds(pl.multiple_of(shard * depth, LANES), depth)
            return pltpu.make_async_copy((q_ref, k_ref, v_ref)[i].at[0, :, lanes], held.at[c, i], sems.at[c, i])

        for c in range(2):
            for i in range(3):
                copy(c, i).start()
        seen = lax.broadcasted_iota(jnp.int32, (1, slots), 1) < sc[COUNT]
        at = [slice(h * size, (h + 1) * size) for h in range(heads)]
        for c in range(2):
            for i in range(3):
                copy(c, i).wait()
            q, k, v = (held.at[c, i] for i in range(3))
            scores = [jnp.where(seen, dot(q[:, h], k[:, h], 1, 1), -1e30) for h in at]
            scores = [jnp.exp2((x - jnp.max(x, axis=1, keepdims=True)) * scale) for x in scores]
            weights = [(x * (1.0 / jnp.sum(x, axis=1, keepdims=True))).astype(BF16) for x in scores]
            for h, x in zip(at, weights):
                out_ref[c, :, h] = dot(x, v[:, h], 1, 0).astype(BF16)

    hbm, vmem = pl.BlockSpec(memory_space=pltpu.HBM), pl.BlockSpec(memory_space=pltpu.VMEM)
    return kernel_call(
        body,
        "attend",
        scalars,
        (queries, keys, values),
        shaped((2, slots, depth)),
        4.0,
        in_specs=[hbm] * 3,
        out_specs=vmem,
        after=after,
        scratch=[pltpu.VMEM((2, 3, slots, depth), BF16), pltpu.SemaphoreType.DMA((2, 3))],
        vmem=ALONE,
    )


def chunk_lanes(depth):
    cut = depth // 3 // LANES * LANES
    return slice(0, cut), slice(cut, depth)


def project_chunk(scalars, columns, weight, weight_near, chip_offset, lanes, size, after):
    _, slots, depth = columns.shape
    w = lanes.stop - lanes.start

    def body(sc, x_ref, own_ref, near_ref, out_ref):
        for k in range(size):
            start = (sc[SHARD] ^ (2 * chip_offset) ^ k) * depth + lanes.start
            cols = pl.ds(pl.multiple_of(start, LANES), w)
            out_ref[k] = (dot(x_ref[0], own_ref[:, cols], 1, 0) + dot(x_ref[1], near_ref[:, cols], 1, 0)).astype(BF16)

    vmem = pl.BlockSpec(memory_space=pltpu.VMEM)
    return kernel_call(
        body,
        "project",
        scalars,
        (columns, weight, weight_near),
        shaped((size, slots, w)),
        8.0 * w / depth,
        in_specs=[vmem] * 3,
        out_specs=vmem,
        after=after,
    )


def base_error(scalars, columns, weight, weight_near, residual, target, received, lanes, size, after):
    _, slots, depth = columns.shape
    w = lanes.stop - lanes.start

    def body(sc, x_ref, own_ref, near_ref, r_ref, t_ref, *refs):
        cols = pl.ds(pl.multiple_of((sc[SHARD] ^ pl.program_id(0)) * depth, LANES), depth)
        total = dot(x_ref[0], own_ref[:, cols], 1, 0) + dot(x_ref[1], near_ref[:, cols], 1, 0)
        refs[-1][0] = total + (r_ref[0].astype(F32) - t_ref[0].astype(F32))
        for ref in refs[:-1]:
            refs[-1][0, :, lanes] += ref[0].astype(F32)

    tokens = pl.BlockSpec((1, slots, depth), lambda k, sc: (0, 0, sc[SHARD] ^ k))
    lead = lambda width: pl.BlockSpec((1, slots, width), lambda k, sc: (k, 0, 0))
    vmem = pl.BlockSpec(memory_space=pltpu.VMEM)
    return kernel_call(
        body,
        "base",
        scalars,
        (columns, weight, weight_near, residual, target, *received),
        shaped((size, slots, depth), F32),
        7.0,
        grid=(size,),
        in_specs=[vmem, vmem, vmem, tokens, tokens, *[lead(w)] * len(received)],
        out_specs=lead(depth),
        after=after,
    )


def error_terms(scalars, base, received, lanes, low_part, adapters):
    size, slots, depth = base.shape
    rank = low_part.shape[0]
    back_lanes = -(-slots // LANES) * LANES
    peers = len(received)
    step = math.gcd(lanes.start, depth)

    def body(sc, base_ref, low_ref, *refs):
        got, up_refs, pieces = refs[:peers], refs[peers : peers + size], refs[peers + size : -1]
        count = sc[COUNT]
        tokens = count.astype(F32)
        valid = lax.broadcasted_iota(jnp.int32, (slots, 1), 0) < count
        low_wide = low_ref[...]
        for ref in up_refs[1:]:
            low_wide = low_wide + ref[:, depth : depth + slots].astype(F32)
        low_turned = low_wide.astype(BF16)
        low_state = low_wide.T.astype(BF16)
        back = jnp.zeros((rank, slots), F32)
        squares = jnp.zeros((slots, step), F32)
        for k in range(size):
            for start in range(0, depth, step):
                at = slice(start, start + step)
                up = up_refs[k][:, at]
                error = base_ref[k, :, at] + ADAPTER_SCALE * dot(low_state, up, 1, 0)
                if start >= lanes.start:
                    for ref in got:
                        error = error + ref[k, :, start - lanes.start : start - lanes.start + step].astype(F32)
                error = jnp.where(valid, error, 0.0)
                squares = squares + error * error
                cotangent = (2.0 * error / tokens).astype(BF16)
                back = back + dot(up, cotangent, 1, 1)
                pieces[k][:, at] = (ADAPTER_SCALE * dot(low_turned, cotangent, 1, 0)).astype(BF16)
        refs[-1][0, 0] = jnp.sum(squares) / (tokens * (size * depth))
        padded = (ADAPTER_SCALE * back).astype(BF16)
        padded = jnp.concatenate([padded, jnp.zeros((rank, back_lanes - slots), BF16)], axis=1)
        for k in range(size):
            pieces[k][:, depth:] = padded

    whole = lambda x: pl.BlockSpec(x.shape, lambda k, sc: (0,) * len(x.shape))
    out_shape = [shaped((rank, depth + back_lanes))] * size + [shaped((1, 1), F32)]
    out = kernel_call(
        body,
        "error",
        scalars,
        (base, low_part, *received, *adapters),
        out_shape,
        3.0,
        in_specs=[whole(x) for x in (base, low_part, *received, *adapters)],
        out_specs=[whole(x) for x in out_shape[:-1]] + [pl.BlockSpec(memory_space=pltpu.SMEM)],
    )
    return out[:size], out[size]


def join_adapters(scalars, down, up, scene, rows, after):
    _, rank, depth = down.shape

    def body(sc, down_ref, up_ref, scene_ref, row_ref, out_ref, slot_ref):
        out_ref[:rank, :] = down_ref[0]
        out_ref[rank:, :] = up_ref[0]
        slot_ref[...] = jnp.full(slot_ref.shape, row_ref[scene_ref[0]].astype(F32))

    vmem, smem = pl.BlockSpec(memory_space=pltpu.VMEM), pl.BlockSpec(memory_space=pltpu.SMEM)
    return kernel_call(
        body,
        "join",
        scalars,
        (down, up, scene, rows),
        [shaped((2 * rank, depth)), shaped((8, LANES), F32)],
        1.0,
        in_specs=[vmem, vmem, smem, smem],
        out_specs=[vmem, vmem],
        after=after,
    )


def stack_blocks(scalars, blocks, after):
    def body(sc, *refs):
        for i in range(len(blocks)):
            refs[-1][i] = refs[i][...]

    return kernel_call(
        body, "stack", scalars, blocks, shaped((len(blocks), *blocks[0].shape)), 0.6, after=after
    )


def slot_offset(sc, slot_ref):
    return jnp.max(slot_ref[...]).astype(jnp.int32) ^ sc[GROUP]


def choose_adapters(scalars, slot_list, blocks, columns, after):
    arrays = []
    for x, _ in blocks:
        if all(x is not y for y in arrays):
            arrays.append(x)
    where = [next(i for i, y in enumerate(arrays) if x is y) for x, _ in blocks]
    rows, depth = arrays[0].shape
    rank = rows // 2
    size = len(slot_list)
    slots = columns[0].shape[0]
    padded = -(-slots // LANES) * LANES

    def body(sc, *refs):
        slot_refs, column_refs, refs = refs[:size], refs[size : 2 * size], refs[2 * size :]
        outs, low_ref, held = refs[len(arrays) : -2], refs[-2], refs[-1]
        for k in range(size):
            offset = slot_offset(sc, slot_refs[k])
            for scene, (_, place) in enumerate(blocks):

                @pl.when(offset == scene)
                def _():
                    ref = refs[where[scene]]
                    held[k] = ref[...] if place is None else ref[place]

        for k in range(size):
            part = dot(held[k, :rank, :], column_refs[k][...], 1, 1)
            if k == 0:
                low_ref[...] = part
            outs[k][:, :depth] = held[k, rank:, :]
            outs[k][:, depth:] = jnp.concatenate(
                [part.astype(BF16), jnp.zeros((rank, padded - slots), BF16)], axis=1
            )

    out = kernel_call(
        body,
        "choose",
        scalars,
        (*slot_list, *columns, *arrays),
        [shaped((rank, depth + padded))] * size + [shaped((rank, slots), F32)],
        2.0,
        after=after,
        scratch=[pltpu.VMEM((size, rows, depth), BF16)],
    )
    return out[:size], out[size]


def scene_sum(offsets, pieces, scene):
    total = jnp.zeros(pieces[0].shape, F32)
    for offset, piece in zip(offsets, pieces):
        total = total + jnp.where(offset == scene, piece, 0.0)
    return total


def first_refs(offsets, pieces, keep, sends, near, far, near_mul, far_mul):
    for f in range(far):
        keep[f] = scene_sum(offsets, pieces, f * far_mul)
        for s in range(1, near):
            sends[s - 1][f] = scene_sum(offsets, pieces, f * far_mul + s * near_mul).astype(BF16)


def second_refs(keep, received, final, sends, far):
    for f in range(far):
        total = keep[f]
        for ref in received:
            total = total + ref[f].astype(F32)
        if f == 0:
            final[...] = total
        else:
            sends[f - 1][...] = total.astype(BF16)


def make_chunked(frame_size, fsdp_size):
    chips = fsdp_size // 2
    outer, inner = split_axis(frame_size)
    along_inner = (inner, outer, 1, inner)
    along_outer = (outer, inner, inner, 1)

    def send_frames(arrays, step):
        return [xor_send(x, "frame", frame_size, (i + 1) * step) for i, x in enumerate(arrays)]

    def send_shards(arrays):
        return [arrays[0]] + [xor_send(x, "fsdp", fsdp_size, k) for k, x in enumerate(arrays) if k]

    def first_shapes(rank, w, order):
        near, far = order[:2]
        return [shaped((far, rank, w), F32)] + [shaped((far, rank, w))] * (near - 1)

    def second_shapes(rank, w, order):
        far = order[1]
        return [shaped((rank, w), F32)] + [shaped((rank, w))] * (far - 1)

    def per_device(
        queries,
        keys,
        values,
        residual,
        target,
        output_weight,
        down_adapter,
        up_adapter,
        scene_of_frame,
        scene_adapter_row,
        valid_token_count,
    ):
        depth = output_weight.shape[0]
        rank = down_adapter.shape[1]
        slots = queries.shape[1]
        shard = lax.axis_index("fsdp").astype(jnp.int32)
        group = lax.axis_index("frame").astype(jnp.int32)
        places = [shard, shard % 2, shard // 2, valid_token_count[0], group]
        scalars = jnp.stack(places)

        weight_near = xor_send(output_weight, "fsdp", fsdp_size, 1)

        attended = [attend_chip(scalars, queries, keys, values, c, depth) for c in range(1, chips)]
        theirs = [xor_send(x, "fsdp", fsdp_size, 2 * (c + 1)) for c, x in enumerate(attended)]
        own = attend_chip(scalars, queries, keys, values, 0, depth, attended[:1])
        block, own_slot = join_adapters(
            scalars, down_adapter, up_adapter, scene_of_frame, scene_adapter_row, [own, weight_near]
        )
        near_slots = [own_slot] + [xor_send(own_slot, "fsdp", fsdp_size, 2 * c) for c in range(1, chips)]
        outer_blocks = [xor_send(block, "frame", frame_size, o * inner) for o in range(1, outer)]
        attended = [own] + attended

        partials = []
        after = [block, *near_slots[1:]]
        parts = chunk_lanes(depth)
        for lanes in parts:
            sent = []
            for c, x in enumerate(theirs):
                part = project_chunk(
                    scalars, x, output_weight, weight_near, c + 1, lanes, fsdp_size, after
                )
                sent.append(xor_send(part, "fsdp", fsdp_size, 2 * (c + 1)))
            partials.append(sent)
            after = [part]
        slot_list = [x for slot in near_slots for x in (slot, xor_send(slot, "fsdp", fsdp_size, 1))]

        stacked = stack_blocks(scalars, outer_blocks, [part])
        inner_blocks = [xor_send(block, "frame", frame_size, s) for s in range(1, inner)]
        far_blocks = [xor_send(stacked, "frame", frame_size, s) for s in range(1, inner)]
        base = base_error(
            scalars,
            own,
            output_weight,
            weight_near,
            residual,
            target,
            partials[0],
            parts[0],
            fsdp_size,
            [stacked],
        )
        blocks = [None] * frame_size
        for o in range(outer):
            blocks[o * inner] = (stacked, o - 1) if o else (block, None)
            for s in range(1, inner):
                blocks[o * inner + s] = (far_blocks[s - 1], o - 1) if o else (inner_blocks[s - 1], None)

        columns = [None] * fsdp_size
        for c, x in enumerate([own] + theirs):
            columns[2 * c] = x[0]
            columns[2 * c + 1] = xor_send(x[1], "fsdp", fsdp_size, 1)

        chosen, low_part = choose_adapters(scalars, slot_list, blocks, columns, [base])
        adapters = send_shards(chosen)
        pieces, loss = error_terms(scalars, base, partials[1], parts[1], low_part, adapters)
        pieces = send_shards(pieces)

        cut = depth // 3 // LANES * LANES
        first_shape = first_shapes(rank, depth + cut, along_inner) + first_shapes(rank, depth - cut, along_outer)
        second_shape = second_shapes(rank, depth + cut, along_inner) + second_shapes(
            rank, depth - cut, along_outer
        )

        def first(sc, *refs):
            slot_refs, got, cols = (refs[i * fsdp_size : (i + 1) * fsdp_size] for i in range(3))
            outs = refs[3 * fsdp_size :]
            offsets = [slot_offset(sc, ref) for ref in slot_refs]
            downs = [dot(p[:, depth : depth + slots], c[...], 1, 0) for p, c in zip(got, cols)]
            down_outs = [ref.at[:, :, :depth] for ref in outs[:inner]]
            first_refs(offsets, downs, down_outs[0], down_outs[1:], *along_inner)
            ups = [p[:, :cut].astype(F32) for p in got]
            up_outs = [ref.at[:, :, depth:] for ref in outs[:inner]]
            first_refs(offsets, ups, up_outs[0], up_outs[1:], *along_inner)
            ups = [p[:, cut:depth].astype(F32) for p in got]
            first_refs(offsets, ups, outs[inner], outs[inner + 1 :], *along_outer)

        out = kernel_call(first, "first", scalars, (*slot_list, *pieces, *columns), first_shape, 2.0)
        keeps = out[0], out[inner]
        inner_got = send_frames(out[1:inner], 1)
        outer_got = send_frames(out[inner + 1 :], inner)

        def second(sc, inner_keep, outer_keep, *refs):
            inners, refs = refs[: inner - 1], refs[inner - 1 :]
            outers, refs = refs[: outer - 1], refs[outer - 1 :]
            second_refs(inner_keep, inners, refs[0], refs[1:outer], outer)
            second_refs(outer_keep, outers, refs[outer], refs[outer + 1 :], inner)

        out = kernel_call(second, "second", scalars, (*keeps, *inner_got, *outer_got), second_shape, 0.8)
        one = (out[0], *send_frames(out[1:outer], inner))
        two = (out[outer], *send_frames(out[outer + 1 :], 1))

        def finish(sc, *refs):
            down_ref, up_ref = refs[-2:]
            for part, which in ((0, refs[: len(one)]), (1, refs[len(one) : -2])):
                total = which[0][...]
                for ref in which[1:]:
                    total = total + ref[...].astype(F32)
                if part == 0:
                    down_ref[0] = total[:, :depth]
                    up_ref[0, :, :cut] = total[:, depth:]
                else:
                    up_ref[0, :, cut:] = total

        grad = shaped((1, rank, depth), F32)
        grad_down, grad_up = kernel_call(finish, "finish", scalars, (*one, *two), [grad, grad], 1.3)
        return grad_down, grad_up, loss[0]

    return per_device


def solution(mesh):
    frame_size, fsdp_size = mesh.shape["frame"], mesh.shape["fsdp"]
    rows = P(("frame", "fsdp"), None, None)
    adapter = P("frame", None, "fsdp")
    vector = P(("frame", "fsdp"))
    placed = (rows, rows, rows, rows, rows, P("fsdp", None), adapter, adapter, vector, P(), vector)
    chunked = make_chunked(frame_size, fsdp_size)
    general = make_general(frame_size, fsdp_size)

    def per_device(*operands):
        depth = operands[5].shape[0]
        return (chunked if depth % (3 * LANES) == 0 else general)(*operands)

    return jax.shard_map(
        per_device,
        mesh=mesh,
        in_specs=placed,
        out_specs=(adapter, adapter, vector),
        check_vma=False,
    )
```

```python
import math

import jax
import jax.numpy as jnp
from jax import lax
from jax.experimental import pallas as pl
from jax.experimental.pallas import tpu as pltpu
from jax.sharding import PartitionSpec as P

HEADS = 24
ADAPTER_SCALE = 2.0
F32 = jnp.float32
BF16 = jnp.bfloat16


def xor_send(value, axis, size, offset):
    return lax.ppermute(value, axis, [(i, i ^ offset) for i in range(size)])


def split_axis(size):
    inner = 1 << ((size.bit_length() - 1) // 2)
    return size // inner, inner


def gather_scenes(block, size):
    outer, inner = split_axis(size)
    first = [block]
    for step in range(1, outer):
        first.append(xor_send(block, "frame", size, step * inner))
    out = [None] * size
    for step in range(outer):
        out[step * inner] = first[step]
    for step in range(1, inner):
        for lead in range(outer):
            out[lead * inner + step] = xor_send(first[lead], "frame", size, step)
    return jnp.stack(out)


def scatter_scenes(dense, size, inner_first):
    outer, inner = split_axis(size)
    near, far = (inner, outer) if inner_first else (outer, inner)
    near_mul, far_mul = (1, inner) if inner_first else (inner, 1)

    def at(f, s):
        return dense[f * far_mul + s * near_mul]

    staged = [at(f, 0) for f in range(far)]
    for step in range(1, near):
        sent = jnp.stack([at(f, step) for f in range(far)]).astype(BF16)
        got = xor_send(sent, "frame", size, step * near_mul)
        staged = [staged[f] + got[f].astype(F32) for f in range(far)]
    total = staged[0]
    for step in range(1, far):
        total = total + xor_send(staged[step].astype(BF16), "frame", size, step * far_mul).astype(F32)
    return total


def attend(queries, keys, values, valid):
    slots, width = queries.shape
    size = width // HEADS
    q = queries.reshape(slots, HEADS, size)
    k = keys.reshape(slots, HEADS, size)
    v = values.reshape(slots, HEADS, size)
    scores = jnp.einsum("qhd,khd->hqk", q, k, preferred_element_type=F32) * (1.0 / math.sqrt(size))
    scores = jnp.where(valid[None, None, :], scores, -jnp.inf)
    peak = jnp.max(scores, axis=-1, keepdims=True)
    exponent = jnp.exp(scores - peak)
    weights = (exponent / jnp.sum(exponent, axis=-1, keepdims=True)).astype(BF16)
    out = jnp.einsum("hqk,khd->qhd", weights, v, preferred_element_type=F32)
    return out.astype(BF16).reshape(slots, width)


def dot(a, b, ca, cb):
    return lax.dot_general(a, b, (((ca,), (cb,)), ((), ())), preferred_element_type=F32)


def make_general(frame_size, fsdp_size):
    chips = fsdp_size // 2

    def per_device(
        queries,
        keys,
        values,
        residual,
        target,
        output_weight,
        down_adapter,
        up_adapter,
        scene_of_frame,
        scene_adapter_row,
        valid_token_count,
    ):
        slots, width = queries.shape[1:]
        depth = output_weight.shape[0]
        shard = lax.axis_index("fsdp")
        group = lax.axis_index("frame")
        core = shard % 2
        chip = shard // 2

        weight_near = xor_send(output_weight, "fsdp", fsdp_size, 1)
        blocks = gather_scenes(jnp.concatenate([down_adapter, up_adapter], axis=0), frame_size)
        own_slot = scene_adapter_row[scene_of_frame[0]]
        offsets = [own_slot ^ group]
        for step in range(1, fsdp_size):
            offsets.append(xor_send(own_slot[None], "fsdp", fsdp_size, step)[0] ^ group)

        count = valid_token_count[0]
        valid = jnp.arange(slots, dtype=jnp.int32) < count
        attended = attend(queries[0], keys[0], values[0], valid)

        def partial(columns):
            mine = lax.dynamic_slice_in_dim(columns, core * depth, depth, 1)
            near = lax.dynamic_slice_in_dim(columns, (1 - core) * depth, depth, 1)
            return dot(mine, output_weight, 1, 0) + dot(near, weight_near, 1, 0)

        def chip_columns(which):
            return lax.dynamic_slice_in_dim(attended, which * 2 * depth, 2 * depth, 1)

        received = []
        for step in range(1, chips):
            theirs = xor_send(chip_columns(chip ^ step), "fsdp", fsdp_size, 2 * step)
            received.append(xor_send(partial(theirs).astype(BF16), "fsdp", fsdp_size, 2 * step))
        projected = partial(chip_columns(chip))
        for got in received:
            projected = projected + got.astype(F32)

        chosen = []
        for step in range(fsdp_size):
            pick = lax.dynamic_index_in_dim(blocks, offsets[step], 0, keepdims=False)
            chosen.append(pick if step == 0 else xor_send(pick, "fsdp", fsdp_size, step))
        adapters = jnp.zeros((2, down_adapter.shape[1], width), BF16)
        for step in range(fsdp_size):
            adapters = lax.dynamic_update_slice_in_dim(adapters, chosen[step], (shard ^ step) * depth, 2)
        down, up = adapters[0], adapters[1]

        low = dot(attended, down, 1, 1).astype(BF16)
        combined = (
            residual[0].astype(F32) + projected + ADAPTER_SCALE * dot(low, up, 1, 0) - target[0].astype(F32)
        )
        error = jnp.where(valid[:, None], combined, 0.0)
        tokens = count.astype(F32)
        loss = jnp.sum(error * error) / (tokens * width)
        cotangent = (2.0 * error / tokens).astype(BF16)
        up_terms = ADAPTER_SCALE * dot(low, cotangent, 0, 0)
        back = (ADAPTER_SCALE * dot(cotangent, up, 1, 1)).astype(BF16)
        down_terms = dot(back, attended, 0, 0)
        terms = jnp.concatenate([down_terms, up_terms], axis=0)

        pieces = []
        for step in range(fsdp_size):
            piece = lax.dynamic_slice_in_dim(terms, (shard ^ step) * depth, depth, 1)
            pieces.append(piece if step == 0 else xor_send(piece.astype(BF16), "fsdp", fsdp_size, step).astype(F32))
        dense = []
        for scene in range(frame_size):
            total = jnp.zeros_like(pieces[0])
            for offset, piece in zip(offsets, pieces):
                total = total + jnp.where(offset == scene, piece, 0.0)
            dense.append(total)
        dense = jnp.stack(dense)
        rank = down_adapter.shape[1]
        cut = 2 * rank * 5 // 8
        top = scatter_scenes(dense[:, :cut], frame_size, True)
        bottom = scatter_scenes(dense[:, cut:], frame_size, False)
        owned = jnp.concatenate([top, bottom], axis=0)
        return owned[None, :rank], owned[None, rank:], loss[None]

    return per_device


LANES = 128
VMEM = 20 * 1024 * 1024
COST = 6.5e8
ALONE = 52 * 1024 * 1024
SHARD, CORE, CHIP, COUNT, GROUP = range(5)


def kernel_call(
    body, name, scalars, operands, out_shape, micros, grid=None, in_specs=None, out_specs=None, after=(), scratch=(), vmem=VMEM
):
    whole = lambda shape: pl.BlockSpec(shape, lambda *_: (0,) * len(shape))
    inner_body = body
    ready = len(operands)

    def body(sc, *refs):
        inner_body(sc, *refs[:ready], *refs[ready + len(after) :])

    if in_specs is None:
        in_specs = [whole(x.shape) for x in operands]
    if out_specs is None:
        out_specs = jax.tree.map(lambda x: whole(x.shape), out_shape)
    return pl.pallas_call(
        body,
        out_shape=out_shape,
        grid_spec=pltpu.PrefetchScalarGridSpec(
            num_scalar_prefetch=1,
            grid=grid or (1,),
            in_specs=[*in_specs, *[pl.BlockSpec(memory_space=pl.ANY)] * len(after)],
            out_specs=out_specs,
            scratch_shapes=list(scratch),
        ),
        compiler_params=pltpu.CompilerParams(vmem_limit_bytes=vmem),
        cost_estimate=pl.CostEstimate(
            flops=int(micros * COST), bytes_accessed=0, transcendentals=0
        ),
        name=name,
    )(scalars, *operands, *after)


def ordered_call(body, name, scalars, operands, out_shape, micros, order):
    def inner_body(sc, *refs):
        outs = refs[len(operands) :]
        body(sc, *refs[: len(operands)], *[outs[order.index(i)] for i in range(len(order))])

    out = kernel_call(inner_body, name, scalars, operands, [out_shape[i] for i in order], micros)
    return [out[order.index(i)] for i in range(len(order))]


def shaped(shape, dtype=BF16):
    return jax.ShapeDtypeStruct(shape, dtype)


def attend_chip(scalars, queries, keys, values, chip_offset, depth, after=()):
    slots, width = queries.shape[1:]
    size = width // HEADS
    heads = depth // size
    scale = math.log2(math.e) / math.sqrt(size)

    def body(sc, q_ref, k_ref, v_ref, out_ref, held, sems):
        def copy(c, i):
            shard = (sc[CHIP] ^ chip_offset) * 2 + (sc[CORE] ^ c)
            lanes = pl.ds(pl.multiple_of(shard * depth, LANES), depth)
            return pltpu.make_async_copy((q_ref, k_ref, v_ref)[i].at[0, :, lanes], held.at[c, i], sems.at[c, i])

        for i in range(3):
            copy(0, i).start()
        seen = lax.broadcasted_iota(jnp.int32, (1, slots), 1) < sc[COUNT]
        at = [slice(h * size, (h + 1) * size) for h in range(heads)]
        for c in range(2):
            for i in range(3):
                copy(c, i).wait()
            if c == 0:
                for i in range(3):
                    copy(1, i).start()
            q, k, v = (held.at[c, i] for i in range(3))
            scores = [jnp.where(seen, dot(q[:, h], k[:, h], 1, 1), -1e30) for h in at]
            scores = [jnp.exp2((x - jnp.max(x, axis=1, keepdims=True)) * scale) for x in scores]
            weights = [(x * (1.0 / jnp.sum(x, axis=1, keepdims=True))).astype(BF16) for x in scores]
            for h, x in zip(at, weights):
                out_ref[c, :, h] = dot(x, v[:, h], 1, 0).astype(BF16)

    hbm, vmem = pl.BlockSpec(memory_space=pltpu.HBM), pl.BlockSpec(memory_space=pltpu.VMEM)
    return kernel_call(
        body,
        "attend",
        scalars,
        (queries, keys, values),
        shaped((2, slots, depth)),
        4.0,
        in_specs=[hbm] * 3,
        out_specs=vmem,
        after=after,
        scratch=[pltpu.VMEM((2, 3, slots, depth), BF16), pltpu.SemaphoreType.DMA((2, 3))],
        vmem=ALONE,
    )


def chunk_lanes(depth):
    cut = depth // 3 // LANES * LANES
    return slice(0, cut), slice(cut, depth)


def project_chunk(scalars, columns, weight, weight_near, chip_offset, lanes, size, after):
    _, slots, depth = columns.shape
    w = lanes.stop - lanes.start

    def body(sc, x_ref, own_ref, near_ref, out_ref):
        for k in range(size):
            start = (sc[SHARD] ^ (2 * chip_offset) ^ k) * depth + lanes.start
            cols = pl.ds(pl.multiple_of(start, LANES), w)
            out_ref[k] = (dot(x_ref[0], own_ref[:, cols], 1, 0) + dot(x_ref[1], near_ref[:, cols], 1, 0)).astype(BF16)

    vmem = pl.BlockSpec(memory_space=pltpu.VMEM)
    return kernel_call(
        body,
        "project",
        scalars,
        (columns, weight, weight_near),
        shaped((size, slots, w)),
        8.0 * w / depth,
        in_specs=[vmem] * 3,
        out_specs=vmem,
        after=after,
    )


def base_error(scalars, columns, weight, weight_near, residual, target, received, lanes, size, after):
    _, slots, depth = columns.shape
    w = lanes.stop - lanes.start

    def body(sc, x_ref, own_ref, near_ref, r_ref, t_ref, *refs):
        cols = pl.ds(pl.multiple_of((sc[SHARD] ^ pl.program_id(0)) * depth, LANES), depth)
        total = dot(x_ref[0], own_ref[:, cols], 1, 0) + dot(x_ref[1], near_ref[:, cols], 1, 0)
        refs[-1][0] = total + (r_ref[0].astype(F32) - t_ref[0].astype(F32))
        for ref in refs[:-1]:
            refs[-1][0, :, lanes] += ref[0].astype(F32)

    tokens = pl.BlockSpec((1, slots, depth), lambda k, sc: (0, 0, sc[SHARD] ^ k))
    lead = lambda width: pl.BlockSpec((1, slots, width), lambda k, sc: (k, 0, 0))
    vmem = pl.BlockSpec(memory_space=pltpu.VMEM)
    return kernel_call(
        body,
        "base",
        scalars,
        (columns, weight, weight_near, residual, target, *received),
        shaped((size, slots, depth), F32),
        7.0,
        grid=(size,),
        in_specs=[vmem, vmem, vmem, tokens, tokens, *[lead(w)] * len(received)],
        out_specs=lead(depth),
        after=after,
    )


def error_terms(scalars, base, received, lanes, low_part, adapters):
    size, slots, depth = base.shape
    rank = low_part.shape[0]
    back_lanes = -(-slots // LANES) * LANES
    peers = len(received)
    step = math.gcd(lanes.start, depth)

    def body(sc, base_ref, low_ref, *refs):
        got, up_refs, pieces = refs[:peers], refs[peers : peers + size], refs[peers + size : -1]
        count = sc[COUNT]
        tokens = count.astype(F32)
        per_token = 2.0 / tokens
        valid = lax.broadcasted_iota(jnp.int32, (slots, 1), 0) < count
        low_wide = low_ref[...]
        for ref in up_refs[1:]:
            low_wide = low_wide + ref[:, depth : depth + slots].astype(F32)
        low_turned = ADAPTER_SCALE * low_wide.astype(BF16)
        low_state = ADAPTER_SCALE * low_wide.T.astype(BF16)
        back = jnp.zeros((rank, slots), F32)
        squares = jnp.zeros((slots, step), F32)
        for k in range(size):
            for start in range(0, depth, step):
                at = slice(start, start + step)
                up = up_refs[k][:, at]
                error = base_ref[k, :, at] + dot(low_state, up, 1, 0)
                if start >= lanes.start:
                    for ref in got:
                        error = error + ref[k, :, start - lanes.start : start - lanes.start + step].astype(F32)
                error = jnp.where(valid, error, 0.0)
                squares = squares + error * error
                cotangent = (error * per_token).astype(BF16)
                back = back + dot(up, cotangent, 1, 1)
                pieces[k][:, at] = dot(low_turned, cotangent, 1, 0).astype(BF16)
        refs[-1][0, 0] = jnp.sum(squares) / (tokens * (size * depth))
        padded = (ADAPTER_SCALE * back).astype(BF16)
        padded = jnp.concatenate([padded, jnp.zeros((rank, back_lanes - slots), BF16)], axis=1)
        for k in range(size):
            pieces[k][:, depth:] = padded

    whole = lambda x: pl.BlockSpec(x.shape, lambda k, sc: (0,) * len(x.shape))
    out_shape = [shaped((rank, depth + back_lanes))] * size + [shaped((1, 1), F32)]
    out = kernel_call(
        body,
        "error",
        scalars,
        (base, low_part, *received, *adapters),
        out_shape,
        3.0,
        in_specs=[whole(x) for x in (base, low_part, *received, *adapters)],
        out_specs=[whole(x) for x in out_shape[:-1]] + [pl.BlockSpec(memory_space=pltpu.SMEM)],
    )
    return out[:size], out[size]


def join_adapters(scalars, down, up, scene, rows, after):
    _, rank, depth = down.shape

    def body(sc, down_ref, up_ref, scene_ref, row_ref, out_ref, slot_ref):
        out_ref[:rank, :] = down_ref[0]
        out_ref[rank:, :] = up_ref[0]
        slot_ref[...] = jnp.full(slot_ref.shape, row_ref[scene_ref[0]].astype(F32))

    vmem, smem = pl.BlockSpec(memory_space=pltpu.VMEM), pl.BlockSpec(memory_space=pltpu.SMEM)
    return kernel_call(
        body,
        "join",
        scalars,
        (down, up, scene, rows),
        [shaped((2 * rank, depth)), shaped((8, LANES), F32)],
        1.0,
        in_specs=[vmem, vmem, smem, smem],
        out_specs=[vmem, vmem],
        after=after,
    )


def stack_blocks(scalars, blocks, columns, after):
    count = len(blocks)

    def body(sc, *refs):
        ins, out_ref, others = refs[: count + len(columns)], refs[count + len(columns)], refs[count + len(columns) + 1 :]
        for i in range(count):
            out_ref[i] = ins[i][...]
        for ref, other in zip(ins[count:], others):
            other[...] = ref[1]

    out = kernel_call(
        body,
        "stack",
        scalars,
        (*blocks, *columns),
        [shaped((count, *blocks[0].shape))] + [shaped(x.shape[1:]) for x in columns],
        0.8,
        after=after,
    )
    return out[0], out[1:]


def slot_offset(sc, slot_ref):
    return jnp.max(slot_ref[...]).astype(jnp.int32) ^ sc[GROUP]


def choose_adapters(scalars, slot_list, blocks, columns, after):
    arrays = []
    for x, _ in blocks:
        if all(x is not y for y in arrays):
            arrays.append(x)
    where = [next(i for i, y in enumerate(arrays) if x is y) for x, _ in blocks]
    rows, depth = arrays[0].shape
    rank = rows // 2
    size = len(slot_list)
    slots = columns[0].shape[0]
    padded = -(-slots // LANES) * LANES

    def body(sc, *refs):
        slot_refs, column_refs, refs = refs[:size], refs[size : 2 * size], refs[2 * size :]
        outs, low_ref, held = refs[len(arrays) : -2], refs[-2], refs[-1]
        for k in range(size):
            offset = slot_offset(sc, slot_refs[k])
            for scene, (_, place) in enumerate(blocks):

                @pl.when(offset == scene)
                def _():
                    ref = refs[where[scene]]
                    held[k] = ref[...] if place is None else ref[place]

        for k in range(size):
            part = dot(held[k, :rank, :], column_refs[k][...], 1, 1)
            if k == 0:
                low_ref[...] = part
            outs[k][:, :depth] = held[k, rank:, :]
            outs[k][:, depth:] = jnp.concatenate(
                [part.astype(BF16), jnp.zeros((rank, padded - slots), BF16)], axis=1
            )

    out = kernel_call(
        body,
        "choose",
        scalars,
        (*slot_list, *columns, *arrays),
        [shaped((rank, depth + padded))] * size + [shaped((rank, slots), F32)],
        2.0,
        after=after,
        scratch=[pltpu.VMEM((size, rows, depth), BF16)],
    )
    return out[:size], out[size]


def scene_sum(offsets, pieces, scene):
    total = jnp.zeros(pieces[0].shape, F32)
    for offset, piece in zip(offsets, pieces):
        total = total + jnp.where(offset == scene, piece, 0.0)
    return total


def first_refs(offsets, pieces, keep, sends, near, far, near_mul, far_mul):
    for f in range(far):
        keep[f] = scene_sum(offsets, pieces, f * far_mul)
        for s in range(1, near):
            sends[s - 1][f] = scene_sum(offsets, pieces, f * far_mul + s * near_mul).astype(BF16)


def second_refs(keep, received, final, sends, far):
    for f in range(far):
        total = keep[f]
        for ref in received:
            total = total + ref[f].astype(F32)
        if f == 0:
            final[...] = total
        else:
            sends[f - 1][...] = total.astype(BF16)


def make_chunked(frame_size, fsdp_size):
    chips = fsdp_size // 2
    outer, inner = split_axis(frame_size)
    along_inner = (inner, outer, 1, inner)
    along_outer = (outer, inner, inner, 1)

    def send_frames(arrays, step):
        return [xor_send(x, "frame", frame_size, (i + 1) * step) for i, x in enumerate(arrays)]

    def send_shards(arrays):
        return [arrays[0]] + [xor_send(x, "fsdp", fsdp_size, k) for k, x in enumerate(arrays) if k]

    def first_shapes(rank, w, order):
        near, far = order[:2]
        return [shaped((far, rank, w), F32)] + [shaped((far, rank, w))] * (near - 1)

    def second_shapes(rank, w, order):
        far = order[1]
        return [shaped((rank, w), F32)] + [shaped((rank, w))] * (far - 1)

    def per_device(
        queries,
        keys,
        values,
        residual,
        target,
        output_weight,
        down_adapter,
        up_adapter,
        scene_of_frame,
        scene_adapter_row,
        valid_token_count,
    ):
        depth = output_weight.shape[0]
        rank = down_adapter.shape[1]
        slots = queries.shape[1]
        shard = lax.axis_index("fsdp").astype(jnp.int32)
        group = lax.axis_index("frame").astype(jnp.int32)
        places = [shard, shard % 2, shard // 2, valid_token_count[0], group]
        scalars = jnp.stack(places)

        weight_near = xor_send(output_weight, "fsdp", fsdp_size, 1)

        attended = [attend_chip(scalars, queries, keys, values, c, depth) for c in range(1, chips)]
        theirs = [xor_send(x, "fsdp", fsdp_size, 2 * (c + 1)) for c, x in enumerate(attended)]
        own = attend_chip(scalars, queries, keys, values, 0, depth, attended[:1])
        block, own_slot = join_adapters(
            scalars, down_adapter, up_adapter, scene_of_frame, scene_adapter_row, [own, weight_near]
        )
        near_slots = [own_slot] + [xor_send(own_slot, "fsdp", fsdp_size, 2 * c) for c in range(1, chips)]
        outer_blocks = [xor_send(block, "frame", frame_size, o * inner) for o in range(1, outer)]
        attended = [own] + attended

        partials = []
        after = [block, *near_slots[1:]]
        parts = chunk_lanes(depth)
        for lanes in parts:
            sent = []
            for c, x in enumerate(theirs):
                part = project_chunk(
                    scalars, x, output_weight, weight_near, c + 1, lanes, fsdp_size, after
                )
                sent.append(xor_send(part, "fsdp", fsdp_size, 2 * (c + 1)))
            partials.append(sent)
            after = [part]
        slot_list = [x for slot in near_slots for x in (slot, xor_send(slot, "fsdp", fsdp_size, 1))]

        inner_blocks = [xor_send(block, "frame", frame_size, s) for s in range(1, inner)]
        stacked, others = stack_blocks(scalars, outer_blocks, [own, *theirs], [part, *inner_blocks])
        far_blocks = [xor_send(stacked, "frame", frame_size, s) for s in range(1, inner)]
        base = base_error(
            scalars,
            own,
            output_weight,
            weight_near,
            residual,
            target,
            partials[0],
            parts[0],
            fsdp_size,
            [stacked],
        )
        blocks = [None] * frame_size
        for o in range(outer):
            blocks[o * inner] = (stacked, o - 1) if o else (block, None)
            for s in range(1, inner):
                blocks[o * inner + s] = (far_blocks[s - 1], o - 1) if o else (inner_blocks[s - 1], None)

        columns = [None] * fsdp_size
        for c, (x, other) in enumerate(zip([own] + theirs, others)):
            columns[2 * c] = x[0]
            columns[2 * c + 1] = xor_send(other, "fsdp", fsdp_size, 1)

        chosen, low_part = choose_adapters(scalars, slot_list, blocks, columns, [base])
        adapters = send_shards(chosen)
        pieces, loss = error_terms(scalars, base, partials[1], parts[1], low_part, adapters)
        pieces = send_shards(pieces)

        cut = depth // 3 // LANES * LANES
        first_shape = first_shapes(rank, depth + cut, along_inner) + first_shapes(rank, depth - cut, along_outer)
        second_shape = second_shapes(rank, depth + cut, along_inner) + second_shapes(
            rank, depth - cut, along_outer
        )

        def first(sc, *refs):
            slot_refs, got, cols = (refs[i * fsdp_size : (i + 1) * fsdp_size] for i in range(3))
            outs = refs[3 * fsdp_size :]
            offsets = [slot_offset(sc, ref) for ref in slot_refs]
            downs = [dot(p[:, depth : depth + slots], c[...], 1, 0) for p, c in zip(got, cols)]
            down_outs = [ref.at[:, :, :depth] for ref in outs[:inner]]
            first_refs(offsets, downs, down_outs[0], down_outs[1:], *along_inner)
            ups = [p[:, :cut].astype(F32) for p in got]
            up_outs = [ref.at[:, :, depth:] for ref in outs[:inner]]
            first_refs(offsets, ups, up_outs[0], up_outs[1:], *along_inner)
            ups = [p[:, cut:depth].astype(F32) for p in got]
            first_refs(offsets, ups, outs[inner], outs[inner + 1 :], *along_outer)

        far = [o for o in range(1, outer) if 2 * o >= outer]
        near = [o for o in range(1, outer) if 2 * o < outer]
        order = [0, inner, *[inner + o for o in far], *range(1, inner), *[inner + o for o in near]]
        out = ordered_call(first, "first", scalars, (*slot_list, *pieces, *columns), first_shape, 2.0, order)
        keeps = out[0], out[inner]
        outer_got = send_frames(out[inner + 1 :], inner)
        inner_got = send_frames(out[1:inner], 1)

        def second(sc, inner_keep, outer_keep, *refs):
            inners, refs = refs[: inner - 1], refs[inner - 1 :]
            outers, refs = refs[: outer - 1], refs[outer - 1 :]
            second_refs(inner_keep, inners, refs[0], refs[1:outer], outer)
            second_refs(outer_keep, outers, refs[outer], refs[outer + 1 :], inner)

        order = [0, outer, *far, *near, *[outer + i for i in range(1, inner)]]
        operands = (*keeps, *inner_got, *outer_got)
        out = ordered_call(second, "second", scalars, operands, second_shape, 0.8, order)
        one = (out[0], *send_frames(out[1:outer], inner))
        two = (out[outer], *send_frames(out[outer + 1 :], 1))

        def finish(sc, *refs):
            down_ref, up_ref = refs[-2:]
            for part, which in ((0, refs[: len(one)]), (1, refs[len(one) : -2])):
                total = which[0][...]
                for ref in which[1:]:
                    total = total + ref[...].astype(F32)
                if part == 0:
                    down_ref[0] = total[:, :depth]
                    up_ref[0, :, :cut] = total[:, depth:]
                else:
                    up_ref[0, :, cut:] = total

        grad = shaped((1, rank, depth), F32)
        grad_down, grad_up = kernel_call(finish, "finish", scalars, (*one, *two), [grad, grad], 1.3)
        return grad_down, grad_up, loss[0]

    return per_device


def solution(mesh):
    frame_size, fsdp_size = mesh.shape["frame"], mesh.shape["fsdp"]
    rows = P(("frame", "fsdp"), None, None)
    adapter = P("frame", None, "fsdp")
    vector = P(("frame", "fsdp"))
    placed = (rows, rows, rows, rows, rows, P("fsdp", None), adapter, adapter, vector, P(), vector)
    chunked = make_chunked(frame_size, fsdp_size)
    general = make_general(frame_size, fsdp_size)

    def per_device(*operands):
        depth = operands[5].shape[0]
        return (chunked if depth % (3 * LANES) == 0 else general)(*operands)

    return jax.shard_map(
        per_device,
        mesh=mesh,
        in_specs=placed,
        out_specs=(adapter, adapter, vector),
        check_vma=False,
    )
```

```python
import math

import jax
import jax.numpy as jnp
from jax import lax
from jax.experimental import pallas as pl
from jax.experimental.pallas import tpu as pltpu
from jax.sharding import PartitionSpec as P

HEADS = 24
ADAPTER_SCALE = 2.0
F32 = jnp.float32
BF16 = jnp.bfloat16


def xor_send(value, axis, size, offset):
    return lax.ppermute(value, axis, [(i, i ^ offset) for i in range(size)])


def split_axis(size):
    inner = 1 << ((size.bit_length() - 1) // 2)
    return size // inner, inner


def gather_scenes(block, size):
    outer, inner = split_axis(size)
    first = [block]
    for step in range(1, outer):
        first.append(xor_send(block, "frame", size, step * inner))
    out = [None] * size
    for step in range(outer):
        out[step * inner] = first[step]
    for step in range(1, inner):
        for lead in range(outer):
            out[lead * inner + step] = xor_send(first[lead], "frame", size, step)
    return jnp.stack(out)


def scatter_scenes(dense, size, inner_first):
    outer, inner = split_axis(size)
    near, far = (inner, outer) if inner_first else (outer, inner)
    near_mul, far_mul = (1, inner) if inner_first else (inner, 1)

    def at(f, s):
        return dense[f * far_mul + s * near_mul]

    staged = [at(f, 0) for f in range(far)]
    for step in range(1, near):
        sent = jnp.stack([at(f, step) for f in range(far)]).astype(BF16)
        got = xor_send(sent, "frame", size, step * near_mul)
        staged = [staged[f] + got[f].astype(F32) for f in range(far)]
    total = staged[0]
    for step in range(1, far):
        total = total + xor_send(staged[step].astype(BF16), "frame", size, step * far_mul).astype(F32)
    return total


def attend(queries, keys, values, valid):
    slots, width = queries.shape
    size = width // HEADS
    q = queries.reshape(slots, HEADS, size)
    k = keys.reshape(slots, HEADS, size)
    v = values.reshape(slots, HEADS, size)
    scores = jnp.einsum("qhd,khd->hqk", q, k, preferred_element_type=F32) * (1.0 / math.sqrt(size))
    scores = jnp.where(valid[None, None, :], scores, -jnp.inf)
    peak = jnp.max(scores, axis=-1, keepdims=True)
    exponent = jnp.exp(scores - peak)
    weights = (exponent / jnp.sum(exponent, axis=-1, keepdims=True)).astype(BF16)
    out = jnp.einsum("hqk,khd->qhd", weights, v, preferred_element_type=F32)
    return out.astype(BF16).reshape(slots, width)


def dot(a, b, ca, cb):
    return lax.dot_general(a, b, (((ca,), (cb,)), ((), ())), preferred_element_type=F32)


def make_general(frame_size, fsdp_size):
    chips = fsdp_size // 2

    def per_device(
        queries,
        keys,
        values,
        residual,
        target,
        output_weight,
        down_adapter,
        up_adapter,
        scene_of_frame,
        scene_adapter_row,
        valid_token_count,
    ):
        slots, width = queries.shape[1:]
        depth = output_weight.shape[0]
        shard = lax.axis_index("fsdp")
        group = lax.axis_index("frame")
        core = shard % 2
        chip = shard // 2

        weight_near = xor_send(output_weight, "fsdp", fsdp_size, 1)
        blocks = gather_scenes(jnp.concatenate([down_adapter, up_adapter], axis=0), frame_size)
        own_slot = scene_adapter_row[scene_of_frame[0]]
        offsets = [own_slot ^ group]
        for step in range(1, fsdp_size):
            offsets.append(xor_send(own_slot[None], "fsdp", fsdp_size, step)[0] ^ group)

        count = valid_token_count[0]
        valid = jnp.arange(slots, dtype=jnp.int32) < count
        attended = attend(queries[0], keys[0], values[0], valid)

        def partial(columns):
            mine = lax.dynamic_slice_in_dim(columns, core * depth, depth, 1)
            near = lax.dynamic_slice_in_dim(columns, (1 - core) * depth, depth, 1)
            return dot(mine, output_weight, 1, 0) + dot(near, weight_near, 1, 0)

        def chip_columns(which):
            return lax.dynamic_slice_in_dim(attended, which * 2 * depth, 2 * depth, 1)

        received = []
        for step in range(1, chips):
            theirs = xor_send(chip_columns(chip ^ step), "fsdp", fsdp_size, 2 * step)
            received.append(xor_send(partial(theirs).astype(BF16), "fsdp", fsdp_size, 2 * step))
        projected = partial(chip_columns(chip))
        for got in received:
            projected = projected + got.astype(F32)

        chosen = []
        for step in range(fsdp_size):
            pick = lax.dynamic_index_in_dim(blocks, offsets[step], 0, keepdims=False)
            chosen.append(pick if step == 0 else xor_send(pick, "fsdp", fsdp_size, step))
        adapters = jnp.zeros((2, down_adapter.shape[1], width), BF16)
        for step in range(fsdp_size):
            adapters = lax.dynamic_update_slice_in_dim(adapters, chosen[step], (shard ^ step) * depth, 2)
        down, up = adapters[0], adapters[1]

        low = dot(attended, down, 1, 1).astype(BF16)
        combined = (
            residual[0].astype(F32) + projected + ADAPTER_SCALE * dot(low, up, 1, 0) - target[0].astype(F32)
        )
        error = jnp.where(valid[:, None], combined, 0.0)
        tokens = count.astype(F32)
        loss = jnp.sum(error * error) / (tokens * width)
        cotangent = (2.0 * error / tokens).astype(BF16)
        up_terms = ADAPTER_SCALE * dot(low, cotangent, 0, 0)
        back = (ADAPTER_SCALE * dot(cotangent, up, 1, 1)).astype(BF16)
        down_terms = dot(back, attended, 0, 0)
        terms = jnp.concatenate([down_terms, up_terms], axis=0)

        pieces = []
        for step in range(fsdp_size):
            piece = lax.dynamic_slice_in_dim(terms, (shard ^ step) * depth, depth, 1)
            pieces.append(piece if step == 0 else xor_send(piece.astype(BF16), "fsdp", fsdp_size, step).astype(F32))
        dense = []
        for scene in range(frame_size):
            total = jnp.zeros_like(pieces[0])
            for offset, piece in zip(offsets, pieces):
                total = total + jnp.where(offset == scene, piece, 0.0)
            dense.append(total)
        dense = jnp.stack(dense)
        rank = down_adapter.shape[1]
        cut = 2 * rank * 5 // 8
        top = scatter_scenes(dense[:, :cut], frame_size, True)
        bottom = scatter_scenes(dense[:, cut:], frame_size, False)
        owned = jnp.concatenate([top, bottom], axis=0)
        return owned[None, :rank], owned[None, rank:], loss[None]

    return per_device


LANES = 128
VMEM = 20 * 1024 * 1024
COST = 7e8
ALONE = 52 * 1024 * 1024
SHARD, CORE, CHIP, COUNT, GROUP = range(5)


def kernel_call(
    body, name, scalars, operands, out_shape, micros, grid=None, in_specs=None, out_specs=None, after=(), scratch=(), vmem=VMEM
):
    whole = lambda shape: pl.BlockSpec(shape, lambda *_: (0,) * len(shape))
    inner_body = body
    ready = len(operands)

    def body(sc, *refs):
        inner_body(sc, *refs[:ready], *refs[ready + len(after) :])

    if in_specs is None:
        in_specs = [whole(x.shape) for x in operands]
    if out_specs is None:
        out_specs = jax.tree.map(lambda x: whole(x.shape), out_shape)
    return pl.pallas_call(
        body,
        out_shape=out_shape,
        grid_spec=pltpu.PrefetchScalarGridSpec(
            num_scalar_prefetch=1,
            grid=grid or (1,),
            in_specs=[*in_specs, *[pl.BlockSpec(memory_space=pl.ANY)] * len(after)],
            out_specs=out_specs,
            scratch_shapes=list(scratch),
        ),
        compiler_params=pltpu.CompilerParams(vmem_limit_bytes=vmem),
        cost_estimate=pl.CostEstimate(
            flops=int(micros * COST), bytes_accessed=0, transcendentals=0
        ),
        name=name,
    )(scalars, *operands, *after)


def ordered_call(body, name, scalars, operands, out_shape, micros, order):
    def inner_body(sc, *refs):
        outs = refs[len(operands) :]
        body(sc, *refs[: len(operands)], *[outs[order.index(i)] for i in range(len(order))])

    out = kernel_call(inner_body, name, scalars, operands, [out_shape[i] for i in order], micros)
    return [out[order.index(i)] for i in range(len(order))]


def shaped(shape, dtype=BF16):
    return jax.ShapeDtypeStruct(shape, dtype)


def attend_chip(scalars, queries, keys, values, chip_offset, depth, after=()):
    slots, width = queries.shape[1:]
    size = width // HEADS
    heads = depth // size
    scale = math.log2(math.e) / math.sqrt(size)

    def body(sc, q_ref, k_ref, v_ref, out_ref, held, sems):
        def copy(c, i):
            shard = (sc[CHIP] ^ chip_offset) * 2 + (sc[CORE] ^ c)
            lanes = pl.ds(pl.multiple_of(shard * depth, LANES), depth)
            return pltpu.make_async_copy((q_ref, k_ref, v_ref)[i].at[0, :, lanes], held.at[c, i], sems.at[c, i])

        for i in range(3):
            copy(0, i).start()
        seen = lax.broadcasted_iota(jnp.int32, (1, slots), 1) < sc[COUNT]
        at = [slice(h * size, (h + 1) * size) for h in range(heads)]
        for c in range(2):
            for i in range(3):
                copy(c, i).wait()
            if c == 0:
                for i in range(3):
                    copy(1, i).start()
            q, k, v = (held.at[c, i] for i in range(3))
            scores = [jnp.where(seen, dot(q[:, h], k[:, h], 1, 1), -1e30) for h in at]
            scores = [jnp.exp2((x - jnp.max(x, axis=1, keepdims=True)) * scale) for x in scores]
            weights = [(x * (1.0 / jnp.sum(x, axis=1, keepdims=True))).astype(BF16) for x in scores]
            for h, x in zip(at, weights):
                out_ref[c, :, h] = dot(x, v[:, h], 1, 0).astype(BF16)

    hbm, vmem = pl.BlockSpec(memory_space=pltpu.HBM), pl.BlockSpec(memory_space=pltpu.VMEM)
    return kernel_call(
        body,
        "attend",
        scalars,
        (queries, keys, values),
        shaped((2, slots, depth)),
        4.0,
        in_specs=[hbm] * 3,
        out_specs=vmem,
        after=after,
        scratch=[pltpu.VMEM((2, 3, slots, depth), BF16), pltpu.SemaphoreType.DMA((2, 3))],
        vmem=ALONE,
    )


def bring_weight(scalars, weight, scene, rows_of, after):
    pieces = 4
    rows = weight.shape[0] // pieces

    def body(sc, in_ref, scene_ref, row_ref, out_ref, slot_ref, sems):
        copies = []
        for i in range(pieces):
            at = pl.ds(i * rows, rows)
            copies.append(pltpu.make_async_copy(in_ref.at[at], out_ref.at[at], sems.at[i]))
        for copy in copies:
            copy.start()
        slot_ref[...] = jnp.full(slot_ref.shape, row_ref[scene_ref[0]].astype(F32))
        for copy in copies:
            copy.wait()

    vmem, smem = pl.BlockSpec(memory_space=pltpu.VMEM), pl.BlockSpec(memory_space=pltpu.SMEM)
    return kernel_call(
        body,
        "bring_weight",
        scalars,
        (weight, scene, rows_of),
        [shaped(weight.shape), shaped((8, LANES), F32)],
        3.0,
        in_specs=[pl.BlockSpec(memory_space=pl.ANY), smem, smem],
        out_specs=[vmem, vmem],
        after=after,
        scratch=[pltpu.SemaphoreType.DMA((pieces,))],
    )


def project(scalars, columns, weight, weight_near, chip_offset, size, after):
    _, slots, depth = columns.shape

    def body(sc, x_ref, own_ref, near_ref, out_ref):
        for k in range(size):
            start = (sc[SHARD] ^ (2 * chip_offset) ^ k) * depth
            cols = pl.ds(pl.multiple_of(start, LANES), depth)
            out_ref[k] = (dot(x_ref[0], own_ref[:, cols], 1, 0) + dot(x_ref[1], near_ref[:, cols], 1, 0)).astype(BF16)

    vmem = pl.BlockSpec(memory_space=pltpu.VMEM)
    return kernel_call(
        body,
        "project",
        scalars,
        (columns, weight, weight_near),
        shaped((size, slots, depth)),
        3.0,
        in_specs=[vmem] * 3,
        out_specs=vmem,
        after=after,
    )


def base_error(scalars, columns, weight, weight_near, residual, target, size, after):
    _, slots, depth = columns.shape

    def body(sc, x_ref, own_ref, near_ref, r_ref, t_ref, out_ref):
        cols = pl.ds(pl.multiple_of((sc[SHARD] ^ pl.program_id(0)) * depth, LANES), depth)
        total = dot(x_ref[0], own_ref[:, cols], 1, 0) + dot(x_ref[1], near_ref[:, cols], 1, 0)
        out_ref[0] = total + (r_ref[0].astype(F32) - t_ref[0].astype(F32))

    tokens = pl.BlockSpec((1, slots, depth), lambda k, sc: (0, 0, sc[SHARD] ^ k))
    vmem = pl.BlockSpec(memory_space=pltpu.VMEM)
    return kernel_call(
        body,
        "base",
        scalars,
        (columns, weight, weight_near, residual, target),
        shaped((size, slots, depth), F32),
        7.0,
        grid=(size,),
        in_specs=[vmem, vmem, vmem, tokens, tokens],
        out_specs=pl.BlockSpec((1, slots, depth), lambda k, sc: (k, 0, 0)),
        after=after,
    )


def error_terms(scalars, base, received, low_part, adapters):
    size, slots, depth = base.shape
    rank = low_part.shape[0]
    back_lanes = -(-slots // LANES) * LANES
    peers = len(received)
    step = depth // 3

    def body(sc, base_ref, low_ref, *refs):
        got, up_refs, pieces = refs[:peers], refs[peers : peers + size][::-1], refs[peers + size : -1]
        count = sc[COUNT]
        tokens = count.astype(F32)
        per_token = 2.0 / tokens
        valid = lax.broadcasted_iota(jnp.int32, (slots, 1), 0) < count
        low_wide = low_ref[...]
        for ref in up_refs[1:]:
            low_wide = low_wide + ref[:, depth : depth + slots].astype(F32)
        low_turned = ADAPTER_SCALE * low_wide.astype(BF16)
        low_state = ADAPTER_SCALE * low_wide.T.astype(BF16)
        back = jnp.zeros((slots, rank), F32)
        squares = jnp.zeros((slots, step), F32)
        for k in range(size):
            for start in range(0, depth, step):
                at = slice(start, start + step)
                up = up_refs[k][:, at]
                error = base_ref[k, :, at] + dot(low_state, up, 1, 0)
                for ref in got:
                    error = error + ref[k, :, at].astype(F32)
                error = jnp.where(valid, error, 0.0)
                squares = squares + error * error
                cotangent = (error * per_token).astype(BF16)
                back = back + dot(cotangent, up, 1, 1)
                pieces[k][:, at] = dot(low_turned, cotangent, 1, 0).astype(BF16)
        refs[-1][0, 0] = jnp.sum(squares) / (tokens * (size * depth))
        padded = (ADAPTER_SCALE * back).T.astype(BF16)
        padded = jnp.concatenate([padded, jnp.zeros((rank, back_lanes - slots), BF16)], axis=1)
        for k in range(size):
            pieces[k][:, depth:] = padded

    whole = lambda x: pl.BlockSpec(x.shape, lambda k, sc: (0,) * len(x.shape))
    out_shape = [shaped((rank, depth + back_lanes))] * size + [shaped((1, 1), F32)]
    out = kernel_call(
        body,
        "error",
        scalars,
        (base, low_part, *received, *adapters[::-1]),
        out_shape,
        3.0,
        in_specs=[whole(x) for x in (base, low_part, *received, *adapters[::-1])],
        out_specs=[whole(x) for x in out_shape[:-1]] + [pl.BlockSpec(memory_space=pltpu.SMEM)],
    )
    return out[:size], out[size]


def join_adapters(scalars, down, up, after):
    _, rank, depth = down.shape

    def body(sc, down_ref, up_ref, out_ref):
        out_ref[:rank, :] = down_ref[0]
        out_ref[rank:, :] = up_ref[0]

    return kernel_call(body, "join", scalars, (down, up), shaped((2 * rank, depth)), 1.0, after=after)


def stack_blocks(scalars, blocks, places, columns, slot_tiles, after):
    count, chips = len(blocks), len(columns)

    def body(sc, *refs):
        ins, out_ref, others = refs[: count + 2 * chips], refs[count + 2 * chips], refs[count + 2 * chips + 1 :]
        for i in range(count):
            out_ref[places[i]] = ins[i][...]
        for i in range(chips):
            others[i][...] = ins[count + i][1]
            others[chips + i][...] = ins[count + chips + i][...]

    out = kernel_call(
        body,
        "stack",
        scalars,
        (*blocks, *columns, *slot_tiles),
        [shaped((count, *blocks[0].shape))]
        + [shaped(x.shape[1:]) for x in columns]
        + [shaped(x.shape, F32) for x in slot_tiles],
        0.8,
        after=after,
    )
    return out[0], out[1 : 1 + chips], out[1 + chips :]


def slot_offset(sc, slot_ref):
    return jnp.max(slot_ref[...]).astype(jnp.int32) ^ sc[GROUP]


def choose_adapters(scalars, slot_list, blocks, columns, after):
    arrays = []
    for x, _ in blocks:
        if all(x is not y for y in arrays):
            arrays.append(x)
    where = [next(i for i, y in enumerate(arrays) if x is y) for x, _ in blocks]
    _, rows, depth = arrays[0].shape
    rank = rows // 2
    size = len(slot_list)
    slots = columns[0].shape[0]
    padded = -(-slots // LANES) * LANES

    def body(sc, *refs):
        slot_refs, column_refs, refs = refs[:size], refs[size : 2 * size], refs[2 * size :]
        outs, low_ref, held = refs[len(arrays) : -2], refs[-2], refs[-1]
        for k in range(size):
            offset = slot_offset(sc, slot_refs[k])
            for scene, (_, place) in enumerate(blocks):

                @pl.when(offset == scene)
                def _():
                    held[k] = refs[where[scene]][place]

        for k in range(size):
            part = dot(held[k, :rank, :], column_refs[k][...], 1, 1)
            if k == 0:
                low_ref[...] = part
            outs[k][:, :depth] = held[k, rank:, :]
            outs[k][:, depth:] = jnp.concatenate(
                [part.astype(BF16), jnp.zeros((rank, padded - slots), BF16)], axis=1
            )

    out = kernel_call(
        body,
        "choose",
        scalars,
        (*slot_list, *columns, *arrays),
        [shaped((rank, depth + padded))] * size + [shaped((rank, slots), F32)],
        2.0,
        after=after,
        scratch=[pltpu.VMEM((size, rows, depth), BF16)],
    )
    return out[:size], out[size]


def scene_sum(offsets, pieces, scene):
    total = jnp.zeros(pieces[0].shape, F32)
    for offset, piece in zip(offsets, pieces):
        total = total + jnp.where(offset == scene, piece, 0.0)
    return total


def first_refs(offsets, pieces, keep, sends, near, far, near_mul, far_mul):
    for f in range(far):
        keep[f] = scene_sum(offsets, pieces, f * far_mul)
        for s in range(1, near):
            sends[s - 1][f] = scene_sum(offsets, pieces, f * far_mul + s * near_mul).astype(BF16)


def second_refs(keep, received, final, sends, far):
    for f in range(far):
        total = keep[f]
        for ref in received:
            total = total + ref[f].astype(F32)
        if f == 0:
            final[...] = total
        else:
            sends[f - 1][...] = total.astype(BF16)


def make_chunked(frame_size, fsdp_size):
    chips = fsdp_size // 2
    outer, inner = split_axis(frame_size)
    along_inner = (inner, outer, 1, inner)
    along_outer = (outer, inner, inner, 1)

    def send_frames(arrays, step):
        return [xor_send(x, "frame", frame_size, (i + 1) * step) for i, x in enumerate(arrays)]

    def send_shards(arrays):
        return [arrays[0]] + [xor_send(x, "fsdp", fsdp_size, k) for k, x in enumerate(arrays) if k]

    def first_shapes(rank, w, order):
        near, far = order[:2]
        return [shaped((far, rank, w), F32)] + [shaped((far, rank, w))] * (near - 1)

    def second_shapes(rank, w, order):
        far = order[1]
        return [shaped((rank, w), F32)] + [shaped((rank, w))] * (far - 1)

    def per_device(
        queries,
        keys,
        values,
        residual,
        target,
        output_weight,
        down_adapter,
        up_adapter,
        scene_of_frame,
        scene_adapter_row,
        valid_token_count,
    ):
        depth = output_weight.shape[0]
        rank = down_adapter.shape[1]
        slots = queries.shape[1]
        shard = lax.axis_index("fsdp").astype(jnp.int32)
        group = lax.axis_index("frame").astype(jnp.int32)
        places = [shard, shard % 2, shard // 2, valid_token_count[0], group]
        scalars = jnp.stack(places)

        weight_near = xor_send(output_weight, "fsdp", fsdp_size, 1)

        attended = [attend_chip(scalars, queries, keys, values, c, depth) for c in range(1, chips)]
        theirs = [xor_send(x, "fsdp", fsdp_size, 2 * (c + 1)) for c, x in enumerate(attended)]
        block = join_adapters(scalars, down_adapter, up_adapter, attended[:1])
        outer_blocks = {
            o: xor_send(block, "frame", frame_size, o * inner)
            for o in sorted(range(1, outer), key=lambda o: -o.bit_length())
        }
        own = attend_chip(scalars, queries, keys, values, 0, depth, [block, weight_near])
        attended = [own] + attended

        weight_near, own_slot = bring_weight(
            scalars, weight_near, scene_of_frame, scene_adapter_row, [own]
        )
        near_slots = [own_slot] + [xor_send(own_slot, "fsdp", fsdp_size, 2 * c) for c in range(1, chips)]
        partials = []
        after = [own]
        for c, x in enumerate(theirs):
            part = project(scalars, x, output_weight, weight_near, c + 1, fsdp_size, after)
            partials.append(xor_send(part, "fsdp", fsdp_size, 2 * (c + 1)))
        stacked, others, near_slots = stack_blocks(
            scalars,
            [*outer_blocks.values(), block],
            [*outer_blocks, 0],
            [own, *theirs],
            near_slots,
            [part],
        )
        slot_list = [x for slot in near_slots for x in (slot, xor_send(slot, "fsdp", fsdp_size, 1))]
        far_blocks = [xor_send(stacked, "frame", frame_size, s) for s in range(1, inner)]
        base = base_error(
            scalars,
            own,
            output_weight,
            weight_near,
            residual,
            target,
            fsdp_size,
            [stacked],
        )
        blocks = [((stacked, *far_blocks)[s], o) for o in range(outer) for s in range(inner)]

        columns = [None] * fsdp_size
        for c, (x, other) in enumerate(zip([own] + theirs, others)):
            columns[2 * c] = x[0]
            columns[2 * c + 1] = xor_send(other, "fsdp", fsdp_size, 1)

        chosen, low_part = choose_adapters(scalars, slot_list, blocks, columns, [base])
        adapters = send_shards(chosen)
        pieces, loss = error_terms(scalars, base, partials, low_part, adapters)
        pieces = send_shards(pieces)

        cut = depth // 3 // LANES * LANES
        first_shape = first_shapes(rank, depth + cut, along_inner) + first_shapes(rank, depth - cut, along_outer)
        second_shape = second_shapes(rank, depth + cut, along_inner) + second_shapes(
            rank, depth - cut, along_outer
        )

        def first(sc, *refs):
            slot_refs, got, cols = (refs[i * fsdp_size : (i + 1) * fsdp_size] for i in range(3))
            got = got[::-1]
            outs = refs[3 * fsdp_size :]
            offsets = [slot_offset(sc, ref) for ref in slot_refs]
            downs = [dot(p[:, depth : depth + slots], c[...], 1, 0) for p, c in zip(got, cols)]
            down_outs = [ref.at[:, :, :depth] for ref in outs[:inner]]
            first_refs(offsets, downs, down_outs[0], down_outs[1:], *along_inner)
            ups = [p[:, :cut].astype(F32) for p in got]
            up_outs = [ref.at[:, :, depth:] for ref in outs[:inner]]
            first_refs(offsets, ups, up_outs[0], up_outs[1:], *along_inner)
            ups = [p[:, cut:depth].astype(F32) for p in got]
            first_refs(offsets, ups, outs[inner], outs[inner + 1 :], *along_outer)

        far = [o for o in range(1, outer) if 2 * o >= outer]
        near = [o for o in range(1, outer) if 2 * o < outer]
        order = [0, inner, *[inner + o for o in far], *range(1, inner), *[inner + o for o in near]]
        out = ordered_call(first, "first", scalars, (*slot_list, *pieces[::-1], *columns), first_shape, 2.0, order)
        keeps = out[0], out[inner]
        outer_got = send_frames(out[inner + 1 :], inner)
        inner_got = send_frames(out[1:inner], 1)

        ways = [("outer", o) for o in far] + [("inner", i) for i in range(1, inner)] + [("outer", o) for o in near]

        def second(sc, inner_keep, outer_keep, *refs):
            got = dict(zip(ways, refs))
            outs = refs[len(ways) :]
            inners = [got["inner", i] for i in range(1, inner)]
            outers = [got["outer", o] for o in range(1, outer)]
            second_refs(inner_keep, inners, outs[0], outs[1:outer], outer)
            second_refs(outer_keep, outers, outs[outer], outs[outer + 1 :], inner)

        order = [0, outer, *far, *near, *[outer + i for i in range(1, inner)]]
        sent = {"inner": inner_got, "outer": outer_got}
        operands = (*keeps, *[sent[way][i - 1] for way, i in ways])
        out = ordered_call(second, "second", scalars, operands, second_shape, 0.8, order)
        sent = send_frames(out[1:outer], inner)
        one = (out[0], *[sent[o - 1] for o in far + near])
        two = (out[outer], *send_frames(out[outer + 1 :], 1))

        def finish(sc, *refs):
            down_ref, up_ref = refs[-2:]
            for part, which in ((0, refs[: len(one)]), (1, refs[len(one) : -2])):
                total = which[0][...]
                for ref in which[1:]:
                    total = total + ref[...].astype(F32)
                if part == 0:
                    down_ref[0] = total[:, :depth]
                    up_ref[0, :, :cut] = total[:, depth:]
                else:
                    up_ref[0, :, cut:] = total

        grad = shaped((1, rank, depth), F32)
        grad_down, grad_up = kernel_call(finish, "finish", scalars, (*one, *two), [grad, grad], 1.3)
        return grad_down, grad_up, loss[0]

    return per_device


def solution(mesh):
    frame_size, fsdp_size = mesh.shape["frame"], mesh.shape["fsdp"]
    rows = P(("frame", "fsdp"), None, None)
    adapter = P("frame", None, "fsdp")
    vector = P(("frame", "fsdp"))
    placed = (rows, rows, rows, rows, rows, P("fsdp", None), adapter, adapter, vector, P(), vector)
    chunked = make_chunked(frame_size, fsdp_size)
    general = make_general(frame_size, fsdp_size)

    def per_device(*operands):
        depth = operands[5].shape[0]
        return (chunked if depth % (3 * LANES) == 0 else general)(*operands)

    return jax.shard_map(
        per_device,
        mesh=mesh,
        in_specs=placed,
        out_specs=(adapter, adapter, vector),
        check_vma=False,
    )
```

```python
import math

import jax
import jax.numpy as jnp
from jax import lax
from jax.experimental import pallas as pl
from jax.experimental.pallas import tpu as pltpu
from jax.sharding import PartitionSpec as P

HEADS = 24
ADAPTER_SCALE = 2.0
F32 = jnp.float32
BF16 = jnp.bfloat16


def xor_send(value, axis, size, offset):
    return lax.ppermute(value, axis, [(i, i ^ offset) for i in range(size)])


def split_axis(size):
    inner = 1 << ((size.bit_length() - 1) // 2)
    return size // inner, inner


def gather_scenes(block, size):
    outer, inner = split_axis(size)
    first = [block]
    for step in range(1, outer):
        first.append(xor_send(block, "frame", size, step * inner))
    out = [None] * size
    for step in range(outer):
        out[step * inner] = first[step]
    for step in range(1, inner):
        for lead in range(outer):
            out[lead * inner + step] = xor_send(first[lead], "frame", size, step)
    return jnp.stack(out)


def scatter_scenes(dense, size, inner_first):
    outer, inner = split_axis(size)
    near, far = (inner, outer) if inner_first else (outer, inner)
    near_mul, far_mul = (1, inner) if inner_first else (inner, 1)

    def at(f, s):
        return dense[f * far_mul + s * near_mul]

    staged = [at(f, 0) for f in range(far)]
    for step in range(1, near):
        sent = jnp.stack([at(f, step) for f in range(far)]).astype(BF16)
        got = xor_send(sent, "frame", size, step * near_mul)
        staged = [staged[f] + got[f].astype(F32) for f in range(far)]
    total = staged[0]
    for step in range(1, far):
        total = total + xor_send(staged[step].astype(BF16), "frame", size, step * far_mul).astype(F32)
    return total


def attend(queries, keys, values, valid):
    slots, width = queries.shape
    size = width // HEADS
    q = queries.reshape(slots, HEADS, size)
    k = keys.reshape(slots, HEADS, size)
    v = values.reshape(slots, HEADS, size)
    scores = jnp.einsum("qhd,khd->hqk", q, k, preferred_element_type=F32) * (1.0 / math.sqrt(size))
    scores = jnp.where(valid[None, None, :], scores, -jnp.inf)
    peak = jnp.max(scores, axis=-1, keepdims=True)
    exponent = jnp.exp(scores - peak)
    weights = (exponent / jnp.sum(exponent, axis=-1, keepdims=True)).astype(BF16)
    out = jnp.einsum("hqk,khd->qhd", weights, v, preferred_element_type=F32)
    return out.astype(BF16).reshape(slots, width)


def dot(a, b, ca, cb):
    return lax.dot_general(a, b, (((ca,), (cb,)), ((), ())), preferred_element_type=F32)


def make_general(frame_size, fsdp_size):
    chips = fsdp_size // 2

    def per_device(
        queries,
        keys,
        values,
        residual,
        target,
        output_weight,
        down_adapter,
        up_adapter,
        scene_of_frame,
        scene_adapter_row,
        valid_token_count,
    ):
        slots, width = queries.shape[1:]
        depth = output_weight.shape[0]
        shard = lax.axis_index("fsdp")
        group = lax.axis_index("frame")
        core = shard % 2
        chip = shard // 2

        weight_near = xor_send(output_weight, "fsdp", fsdp_size, 1)
        blocks = gather_scenes(jnp.concatenate([down_adapter, up_adapter], axis=0), frame_size)
        own_slot = scene_adapter_row[scene_of_frame[0]]
        offsets = [own_slot ^ group]
        for step in range(1, fsdp_size):
            offsets.append(xor_send(own_slot[None], "fsdp", fsdp_size, step)[0] ^ group)

        count = valid_token_count[0]
        valid = jnp.arange(slots, dtype=jnp.int32) < count
        attended = attend(queries[0], keys[0], values[0], valid)

        def partial(columns):
            mine = lax.dynamic_slice_in_dim(columns, core * depth, depth, 1)
            near = lax.dynamic_slice_in_dim(columns, (1 - core) * depth, depth, 1)
            return dot(mine, output_weight, 1, 0) + dot(near, weight_near, 1, 0)

        def chip_columns(which):
            return lax.dynamic_slice_in_dim(attended, which * 2 * depth, 2 * depth, 1)

        received = []
        for step in range(1, chips):
            theirs = xor_send(chip_columns(chip ^ step), "fsdp", fsdp_size, 2 * step)
            received.append(xor_send(partial(theirs).astype(BF16), "fsdp", fsdp_size, 2 * step))
        projected = partial(chip_columns(chip))
        for got in received:
            projected = projected + got.astype(F32)

        chosen = []
        for step in range(fsdp_size):
            pick = lax.dynamic_index_in_dim(blocks, offsets[step], 0, keepdims=False)
            chosen.append(pick if step == 0 else xor_send(pick, "fsdp", fsdp_size, step))
        adapters = jnp.zeros((2, down_adapter.shape[1], width), BF16)
        for step in range(fsdp_size):
            adapters = lax.dynamic_update_slice_in_dim(adapters, chosen[step], (shard ^ step) * depth, 2)
        down, up = adapters[0], adapters[1]

        low = dot(attended, down, 1, 1).astype(BF16)
        combined = (
            residual[0].astype(F32) + projected + ADAPTER_SCALE * dot(low, up, 1, 0) - target[0].astype(F32)
        )
        error = jnp.where(valid[:, None], combined, 0.0)
        tokens = count.astype(F32)
        loss = jnp.sum(error * error) / (tokens * width)
        cotangent = (2.0 * error / tokens).astype(BF16)
        up_terms = ADAPTER_SCALE * dot(low, cotangent, 0, 0)
        back = (ADAPTER_SCALE * dot(cotangent, up, 1, 1)).astype(BF16)
        down_terms = dot(back, attended, 0, 0)
        terms = jnp.concatenate([down_terms, up_terms], axis=0)

        pieces = []
        for step in range(fsdp_size):
            piece = lax.dynamic_slice_in_dim(terms, (shard ^ step) * depth, depth, 1)
            pieces.append(piece if step == 0 else xor_send(piece.astype(BF16), "fsdp", fsdp_size, step).astype(F32))
        dense = []
        for scene in range(frame_size):
            total = jnp.zeros_like(pieces[0])
            for offset, piece in zip(offsets, pieces):
                total = total + jnp.where(offset == scene, piece, 0.0)
            dense.append(total)
        dense = jnp.stack(dense)
        rank = down_adapter.shape[1]
        cut = 2 * rank * 5 // 8
        top = scatter_scenes(dense[:, :cut], frame_size, True)
        bottom = scatter_scenes(dense[:, cut:], frame_size, False)
        owned = jnp.concatenate([top, bottom], axis=0)
        return owned[None, :rank], owned[None, rank:], loss[None]

    return per_device


LANES = 128
VMEM = 20 * 1024 * 1024
COST = 7e8
ALONE = 52 * 1024 * 1024
SHARD, CORE, CHIP, COUNT, GROUP = range(5)


def kernel_call(
    body, name, scalars, operands, out_shape, micros, grid=None, in_specs=None, out_specs=None, after=(), scratch=(), vmem=VMEM
):
    whole = lambda shape: pl.BlockSpec(shape, lambda *_: (0,) * len(shape))
    inner_body = body
    ready = len(operands)

    def body(sc, *refs):
        inner_body(sc, *refs[:ready], *refs[ready + len(after) :])

    if in_specs is None:
        in_specs = [whole(x.shape) for x in operands]
    if out_specs is None:
        out_specs = jax.tree.map(lambda x: whole(x.shape), out_shape)
    return pl.pallas_call(
        body,
        out_shape=out_shape,
        grid_spec=pltpu.PrefetchScalarGridSpec(
            num_scalar_prefetch=1,
            grid=grid or (1,),
            in_specs=[*in_specs, *[pl.BlockSpec(memory_space=pl.ANY)] * len(after)],
            out_specs=out_specs,
            scratch_shapes=list(scratch),
        ),
        compiler_params=pltpu.CompilerParams(vmem_limit_bytes=vmem),
        cost_estimate=pl.CostEstimate(
            flops=int(micros * COST), bytes_accessed=0, transcendentals=0
        ),
        name=name,
    )(scalars, *operands, *after)


def ordered_call(body, name, scalars, operands, out_shape, micros, order):
    def inner_body(sc, *refs):
        outs = refs[len(operands) :]
        body(sc, *refs[: len(operands)], *[outs[order.index(i)] for i in range(len(order))])

    out = kernel_call(inner_body, name, scalars, operands, [out_shape[i] for i in order], micros)
    return [out[order.index(i)] for i in range(len(order))]


def shaped(shape, dtype=BF16):
    return jax.ShapeDtypeStruct(shape, dtype)


def attend_chip(counts, queries, keys, values, chip_offset, depth, after=()):
    slots, width = queries.shape[1:]
    size = width // HEADS
    heads = depth // size
    scale = math.log2(math.e) / math.sqrt(size)

    def body(sc, q_ref, k_ref, v_ref, out_ref, held, sems):
        def copy(c, i):
            shard = lax.axis_index("fsdp") ^ (2 * chip_offset + c)
            lanes = pl.ds(pl.multiple_of(shard * depth, LANES), depth)
            return pltpu.make_async_copy((q_ref, k_ref, v_ref)[i].at[0, :, lanes], held.at[c, i], sems.at[c, i])

        for i in range(3):
            copy(0, i).start()
        seen = lax.broadcasted_iota(jnp.int32, (1, slots), 1) < sc[0]
        at = [slice(h * size, (h + 1) * size) for h in range(heads)]
        for c in range(2):
            for i in range(3):
                copy(c, i).wait()
            if c == 0:
                for i in range(3):
                    copy(1, i).start()
            q, k, v = (held.at[c, i] for i in range(3))
            scores = [jnp.where(seen, dot(q[:, h], k[:, h], 1, 1), -1e30) for h in at]
            scores = [jnp.exp2((x - jnp.max(x, axis=1, keepdims=True)) * scale) for x in scores]
            weights = [(x * (1.0 / jnp.sum(x, axis=1, keepdims=True))).astype(BF16) for x in scores]
            for h, x in zip(at, weights):
                out_ref[c, :, h] = dot(x, v[:, h], 1, 0).astype(BF16)

    hbm, vmem = pl.BlockSpec(memory_space=pltpu.HBM), pl.BlockSpec(memory_space=pltpu.VMEM)
    return kernel_call(
        body,
        "attend",
        counts,
        (queries, keys, values),
        shaped((2, slots, depth)),
        4.0,
        in_specs=[hbm] * 3,
        out_specs=vmem,
        after=after,
        scratch=[pltpu.VMEM((2, 3, slots, depth), BF16), pltpu.SemaphoreType.DMA((2, 3))],
        vmem=ALONE,
    )


def bring_weight(scalars, weight, scene, rows_of, after):
    pieces = 4
    rows = weight.shape[0] // pieces

    def body(sc, in_ref, scene_ref, row_ref, out_ref, slot_ref, sems):
        copies = []
        for i in range(pieces):
            at = pl.ds(i * rows, rows)
            copies.append(pltpu.make_async_copy(in_ref.at[at], out_ref.at[at], sems.at[i]))
        for copy in copies:
            copy.start()
        slot_ref[...] = jnp.full(slot_ref.shape, row_ref[scene_ref[0]].astype(F32))
        for copy in copies:
            copy.wait()

    vmem, smem = pl.BlockSpec(memory_space=pltpu.VMEM), pl.BlockSpec(memory_space=pltpu.SMEM)
    return kernel_call(
        body,
        "bring_weight",
        scalars,
        (weight, scene, rows_of),
        [shaped(weight.shape), shaped((8, LANES), F32)],
        3.0,
        in_specs=[pl.BlockSpec(memory_space=pl.ANY), smem, smem],
        out_specs=[vmem, vmem],
        after=after,
        scratch=[pltpu.SemaphoreType.DMA((pieces,))],
    )


def project(scalars, columns, weight, weight_near, chip_offset, size, after):
    _, slots, depth = columns.shape

    def body(sc, x_ref, own_ref, near_ref, out_ref):
        for k in range(size):
            start = (sc[SHARD] ^ (2 * chip_offset) ^ k) * depth
            cols = pl.ds(pl.multiple_of(start, LANES), depth)
            out_ref[k] = (dot(x_ref[0], own_ref[:, cols], 1, 0) + dot(x_ref[1], near_ref[:, cols], 1, 0)).astype(BF16)

    vmem = pl.BlockSpec(memory_space=pltpu.VMEM)
    return kernel_call(
        body,
        "project",
        scalars,
        (columns, weight, weight_near),
        shaped((size, slots, depth)),
        3.0,
        in_specs=[vmem] * 3,
        out_specs=vmem,
        after=after,
    )


def base_error(scalars, columns, weight, weight_near, residual, target, size, after):
    _, slots, depth = columns.shape

    def body(sc, x_ref, own_ref, near_ref, r_ref, t_ref, out_ref):
        cols = pl.ds(pl.multiple_of((sc[SHARD] ^ pl.program_id(0)) * depth, LANES), depth)
        total = dot(x_ref[0], own_ref[:, cols], 1, 0) + dot(x_ref[1], near_ref[:, cols], 1, 0)
        out_ref[0] = total + (r_ref[0].astype(F32) - t_ref[0].astype(F32))

    tokens = pl.BlockSpec((1, slots, depth), lambda k, sc: (0, 0, sc[SHARD] ^ k))
    vmem = pl.BlockSpec(memory_space=pltpu.VMEM)
    return kernel_call(
        body,
        "base",
        scalars,
        (columns, weight, weight_near, residual, target),
        shaped((size, slots, depth), F32),
        7.0,
        grid=(size,),
        in_specs=[vmem, vmem, vmem, tokens, tokens],
        out_specs=pl.BlockSpec((1, slots, depth), lambda k, sc: (k, 0, 0)),
        after=after,
    )


def error_terms(scalars, base, received, low_part, adapters):
    size, slots, depth = base.shape
    rank = low_part.shape[0]
    back_lanes = -(-slots // LANES) * LANES
    peers = len(received)

    def body(sc, base_ref, low_ref, *refs):
        got, up_refs, pieces = refs[:peers], refs[peers : peers + size][::-1], refs[peers + size : -1]
        count = sc[COUNT]
        tokens = count.astype(F32)
        per_token = 2.0 / tokens
        valid = lax.broadcasted_iota(jnp.int32, (slots, 1), 0) < count
        low_wide = low_ref[...]
        for ref in up_refs[1:]:
            low_wide = low_wide + ref[:, depth : depth + slots].astype(F32)
        low_turned = ADAPTER_SCALE * low_wide.astype(BF16)
        low_state = ADAPTER_SCALE * low_wide.T.astype(BF16)
        back = jnp.zeros((slots, rank), F32)
        squares = jnp.zeros((slots, depth), F32)
        for k in range(size):
            up = up_refs[k][:, :depth]
            error = base_ref[k] + dot(low_state, up, 1, 0)
            for ref in got:
                error = error + ref[k].astype(F32)
            error = jnp.where(valid, error, 0.0)
            squares = squares + error * error
            cotangent = (error * per_token).astype(BF16)
            back = back + dot(cotangent, up, 1, 1)
            pieces[k][:, :depth] = dot(low_turned, cotangent, 1, 0).astype(BF16)
        refs[-1][0, 0] = jnp.sum(squares) / (tokens * (size * depth))
        padded = (ADAPTER_SCALE * back).T.astype(BF16)
        padded = jnp.concatenate([padded, jnp.zeros((rank, back_lanes - slots), BF16)], axis=1)
        for k in range(size):
            pieces[k][:, depth:] = padded

    whole = lambda x: pl.BlockSpec(x.shape, lambda k, sc: (0,) * len(x.shape))
    out_shape = [shaped((rank, depth + back_lanes))] * size + [shaped((1, 1), F32)]
    out = kernel_call(
        body,
        "error",
        scalars,
        (base, low_part, *received, *adapters[::-1]),
        out_shape,
        3.0,
        in_specs=[whole(x) for x in (base, low_part, *received, *adapters[::-1])],
        out_specs=[whole(x) for x in out_shape[:-1]] + [pl.BlockSpec(memory_space=pltpu.SMEM)],
    )
    return out[:size], out[size]


def join_adapters(scalars, down, up, after):
    _, rank, depth = down.shape

    def body(sc, down_ref, up_ref, out_ref):
        out_ref[:rank, :] = down_ref[0]
        out_ref[rank:, :] = up_ref[0]

    return kernel_call(body, "join", scalars, (down, up), shaped((2 * rank, depth)), 1.0, after=after)


def stack_blocks(scalars, blocks, places, columns, slot_tiles, after):
    count, chips = len(blocks), len(columns)

    def body(sc, *refs):
        ins, out_ref, others = refs[: count + 2 * chips], refs[count + 2 * chips], refs[count + 2 * chips + 1 :]
        for i in range(count):
            out_ref[places[i]] = ins[i][...]
        for i in range(chips):
            others[i][...] = ins[count + i][1]
            others[chips + i][...] = ins[count + chips + i][...]

    out = kernel_call(
        body,
        "stack",
        scalars,
        (*blocks, *columns, *slot_tiles),
        [shaped((count, *blocks[0].shape))]
        + [shaped(x.shape[1:]) for x in columns]
        + [shaped(x.shape, F32) for x in slot_tiles],
        0.8,
        after=after,
    )
    return out[0], out[1 : 1 + chips], out[1 + chips :]


def slot_offset(sc, slot_ref):
    return jnp.max(slot_ref[...]).astype(jnp.int32) ^ sc[GROUP]


def choose_adapters(scalars, slot_list, blocks, columns, after):
    arrays = []
    for x, _ in blocks:
        if all(x is not y for y in arrays):
            arrays.append(x)
    where = [next(i for i, y in enumerate(arrays) if x is y) for x, _ in blocks]
    _, rows, depth = arrays[0].shape
    rank = rows // 2
    size = len(slot_list)
    slots = columns[0].shape[0]
    padded = -(-slots // LANES) * LANES

    def body(sc, *refs):
        slot_refs, column_refs, refs = refs[:size], refs[size : 2 * size], refs[2 * size :]
        outs, low_ref, held = refs[len(arrays) : -2], refs[-2], refs[-1]
        for k in range(size):
            offset = slot_offset(sc, slot_refs[k])
            for scene, (_, place) in enumerate(blocks):

                @pl.when(offset == scene)
                def _():
                    held[k] = refs[where[scene]][place]

        for k in range(size):
            part = dot(held[k, :rank, :], column_refs[k][...], 1, 1)
            if k == 0:
                low_ref[...] = part
            outs[k][:, :depth] = held[k, rank:, :]
            outs[k][:, depth:] = jnp.concatenate(
                [part.astype(BF16), jnp.zeros((rank, padded - slots), BF16)], axis=1
            )

    out = kernel_call(
        body,
        "choose",
        scalars,
        (*slot_list, *columns, *arrays),
        [shaped((rank, depth + padded))] * size + [shaped((rank, slots), F32)],
        2.0,
        after=after,
        scratch=[pltpu.VMEM((size, rows, depth), BF16)],
    )
    return out[:size], out[size]


def scene_sum(offsets, pieces, scene):
    total = jnp.zeros(pieces[0].shape, F32)
    for offset, piece in zip(offsets, pieces):
        total = total + jnp.where(offset == scene, piece, 0.0)
    return total


def first_refs(offsets, pieces, keep, sends, near, far, near_mul, far_mul):
    for f in range(far):
        keep[f] = scene_sum(offsets, pieces, f * far_mul)
        for s in range(1, near):
            sends[s - 1][f] = scene_sum(offsets, pieces, f * far_mul + s * near_mul).astype(BF16)


def second_refs(keep, received, final, sends, far):
    for f in range(far):
        total = keep[f]
        for ref in received:
            total = total + ref[f].astype(F32)
        if f == 0:
            final[...] = total
        else:
            sends[f - 1][...] = total.astype(BF16)


def make_chunked(frame_size, fsdp_size):
    chips = fsdp_size // 2
    outer, inner = split_axis(frame_size)
    along_inner = (inner, outer, 1, inner)
    along_outer = (outer, inner, inner, 1)

    def send_frames(arrays, step):
        return [xor_send(x, "frame", frame_size, (i + 1) * step) for i, x in enumerate(arrays)]

    def send_shards(arrays):
        return [arrays[0]] + [xor_send(x, "fsdp", fsdp_size, k) for k, x in enumerate(arrays) if k]

    def first_shapes(rank, w, order):
        near, far = order[:2]
        return [shaped((far, rank, w), F32)] + [shaped((far, rank, w))] * (near - 1)

    def second_shapes(rank, w, order):
        far = order[1]
        return [shaped((rank, w), F32)] + [shaped((rank, w))] * (far - 1)

    def per_device(
        queries,
        keys,
        values,
        residual,
        target,
        output_weight,
        down_adapter,
        up_adapter,
        scene_of_frame,
        scene_adapter_row,
        valid_token_count,
    ):
        depth = output_weight.shape[0]
        rank = down_adapter.shape[1]
        slots = queries.shape[1]
        shard = lax.axis_index("fsdp").astype(jnp.int32)
        group = lax.axis_index("frame").astype(jnp.int32)
        places = [shard, shard % 2, shard // 2, valid_token_count[0], group]
        scalars = jnp.stack(places)

        weight_near = xor_send(output_weight, "fsdp", fsdp_size, 1)

        attended = [attend_chip(valid_token_count, queries, keys, values, c, depth) for c in range(1, chips)]
        theirs = [xor_send(x, "fsdp", fsdp_size, 2 * (c + 1)) for c, x in enumerate(attended)]
        block = join_adapters(scalars, down_adapter, up_adapter, attended[:1])
        outer_blocks = {
            o: xor_send(block, "frame", frame_size, o * inner)
            for o in sorted(range(1, outer), key=lambda o: -o.bit_length())
        }
        own = attend_chip(valid_token_count, queries, keys, values, 0, depth, [block, weight_near])
        attended = [own] + attended

        weight_near, own_slot = bring_weight(
            scalars, weight_near, scene_of_frame, scene_adapter_row, [own]
        )
        near_slots = [own_slot] + [xor_send(own_slot, "fsdp", fsdp_size, 2 * c) for c in range(1, chips)]
        partials = []
        after = [own]
        for c, x in enumerate(theirs):
            part = project(scalars, x, output_weight, weight_near, c + 1, fsdp_size, after)
            partials.append(xor_send(part, "fsdp", fsdp_size, 2 * (c + 1)))
        stacked, others, near_slots = stack_blocks(
            scalars,
            [*outer_blocks.values(), block],
            [*outer_blocks, 0],
            [own, *theirs],
            near_slots,
            [part],
        )
        slot_list = [x for slot in near_slots for x in (slot, xor_send(slot, "fsdp", fsdp_size, 1))]
        far_blocks = [xor_send(stacked, "frame", frame_size, s) for s in range(1, inner)]
        base = base_error(
            scalars,
            own,
            output_weight,
            weight_near,
            residual,
            target,
            fsdp_size,
            [stacked],
        )
        blocks = [((stacked, *far_blocks)[s], o) for o in range(outer) for s in range(inner)]

        columns = [None] * fsdp_size
        for c, (x, other) in enumerate(zip([own] + theirs, others)):
            columns[2 * c] = x[0]
            columns[2 * c + 1] = xor_send(other, "fsdp", fsdp_size, 1)

        chosen, low_part = choose_adapters(scalars, slot_list, blocks, columns, [base])
        adapters = send_shards(chosen)
        pieces, loss = error_terms(scalars, base, partials, low_part, adapters)
        pieces = send_shards(pieces)

        cut = depth // 2 // LANES * LANES
        first_shape = first_shapes(rank, depth + cut, along_inner) + first_shapes(rank, depth - cut, along_outer)
        second_shape = second_shapes(rank, depth + cut, along_inner) + second_shapes(
            rank, depth - cut, along_outer
        )

        def first(sc, *refs):
            slot_refs, got, cols = (refs[i * fsdp_size : (i + 1) * fsdp_size] for i in range(3))
            got = got[::-1]
            outs = refs[3 * fsdp_size :]
            offsets = [slot_offset(sc, ref) for ref in slot_refs]
            downs = [dot(p[:, depth : depth + slots], c[...], 1, 0) for p, c in zip(got, cols)]
            down_outs = [ref.at[:, :, :depth] for ref in outs[:inner]]
            first_refs(offsets, downs, down_outs[0], down_outs[1:], *along_inner)
            ups = [p[:, :cut].astype(F32) for p in got]
            up_outs = [ref.at[:, :, depth:] for ref in outs[:inner]]
            first_refs(offsets, ups, up_outs[0], up_outs[1:], *along_inner)
            ups = [p[:, cut:depth].astype(F32) for p in got]
            first_refs(offsets, ups, outs[inner], outs[inner + 1 :], *along_outer)

        far = [o for o in range(1, outer) if 2 * o >= outer]
        near = [o for o in range(1, outer) if 2 * o < outer]
        order = [0, inner, *[inner + o for o in far], *range(1, inner), *[inner + o for o in near]]
        out = ordered_call(first, "first", scalars, (*slot_list, *pieces[::-1], *columns), first_shape, 2.0, order)
        keeps = out[0], out[inner]
        outer_got = send_frames(out[inner + 1 :], inner)
        inner_got = send_frames(out[1:inner], 1)

        ways = [("outer", o) for o in far] + [("inner", i) for i in range(1, inner)] + [("outer", o) for o in near]

        def second(sc, inner_keep, outer_keep, *refs):
            got = dict(zip(ways, refs))
            outs = refs[len(ways) :]
            inners = [got["inner", i] for i in range(1, inner)]
            outers = [got["outer", o] for o in range(1, outer)]
            second_refs(inner_keep, inners, outs[0], outs[1:outer], outer)
            second_refs(outer_keep, outers, outs[outer], outs[outer + 1 :], inner)

        order = [0, outer, *far, *near, *[outer + i for i in range(1, inner)]]
        sent = {"inner": inner_got, "outer": outer_got}
        operands = (*keeps, *[sent[way][i - 1] for way, i in ways])
        out = ordered_call(second, "second", scalars, operands, second_shape, 0.8, order)
        sent = send_frames(out[1:outer], inner)
        one = (out[0], *[sent[o - 1] for o in far + near])
        two = (out[outer], *send_frames(out[outer + 1 :], 1))

        def finish(sc, *refs):
            down_ref, up_ref = refs[-2:]
            for part, which in ((0, refs[: len(one)]), (1, refs[len(one) : -2])):
                total = which[0][...]
                for ref in which[1:]:
                    total = total + ref[...].astype(F32)
                if part == 0:
                    down_ref[0] = total[:, :depth]
                    up_ref[0, :, :cut] = total[:, depth:]
                else:
                    up_ref[0, :, cut:] = total

        grad = shaped((1, rank, depth), F32)
        grad_down, grad_up = kernel_call(finish, "finish", scalars, (*one, *two), [grad, grad], 1.3)
        return grad_down, grad_up, loss[0]

    return per_device


def solution(mesh):
    frame_size, fsdp_size = mesh.shape["frame"], mesh.shape["fsdp"]
    rows = P(("frame", "fsdp"), None, None)
    adapter = P("frame", None, "fsdp")
    vector = P(("frame", "fsdp"))
    placed = (rows, rows, rows, rows, rows, P("fsdp", None), adapter, adapter, vector, P(), vector)
    chunked = make_chunked(frame_size, fsdp_size)
    general = make_general(frame_size, fsdp_size)

    def per_device(*operands):
        depth = operands[5].shape[0]
        return (chunked if depth % (3 * LANES) == 0 else general)(*operands)

    return jax.shard_map(
        per_device,
        mesh=mesh,
        in_specs=placed,
        out_specs=(adapter, adapter, vector),
        check_vma=False,
    )
```

```python
import math

import jax
import jax.numpy as jnp
from jax import lax
from jax.experimental import pallas as pl
from jax.experimental.pallas import tpu as pltpu
from jax.sharding import PartitionSpec as P

HEADS = 24
ADAPTER_SCALE = 2.0
F32 = jnp.float32
BF16 = jnp.bfloat16


def xor_send(value, axis, size, offset):
    return lax.ppermute(value, axis, [(i, i ^ offset) for i in range(size)])


def split_axis(size):
    inner = 1 << ((size.bit_length() - 1) // 2)
    return size // inner, inner


def gather_scenes(block, size):
    outer, inner = split_axis(size)
    first = [block]
    for step in range(1, outer):
        first.append(xor_send(block, "frame", size, step * inner))
    out = [None] * size
    for step in range(outer):
        out[step * inner] = first[step]
    for step in range(1, inner):
        for lead in range(outer):
            out[lead * inner + step] = xor_send(first[lead], "frame", size, step)
    return jnp.stack(out)


def scatter_scenes(dense, size, inner_first):
    outer, inner = split_axis(size)
    near, far = (inner, outer) if inner_first else (outer, inner)
    near_mul, far_mul = (1, inner) if inner_first else (inner, 1)

    def at(f, s):
        return dense[f * far_mul + s * near_mul]

    staged = [at(f, 0) for f in range(far)]
    for step in range(1, near):
        sent = jnp.stack([at(f, step) for f in range(far)]).astype(BF16)
        got = xor_send(sent, "frame", size, step * near_mul)
        staged = [staged[f] + got[f].astype(F32) for f in range(far)]
    total = staged[0]
    for step in range(1, far):
        total = total + xor_send(staged[step].astype(BF16), "frame", size, step * far_mul).astype(F32)
    return total


def attend(queries, keys, values, valid):
    slots, width = queries.shape
    size = width // HEADS
    q = queries.reshape(slots, HEADS, size)
    k = keys.reshape(slots, HEADS, size)
    v = values.reshape(slots, HEADS, size)
    scores = jnp.einsum("qhd,khd->hqk", q, k, preferred_element_type=F32) * (1.0 / math.sqrt(size))
    scores = jnp.where(valid[None, None, :], scores, -jnp.inf)
    peak = jnp.max(scores, axis=-1, keepdims=True)
    exponent = jnp.exp(scores - peak)
    weights = (exponent / jnp.sum(exponent, axis=-1, keepdims=True)).astype(BF16)
    out = jnp.einsum("hqk,khd->qhd", weights, v, preferred_element_type=F32)
    return out.astype(BF16).reshape(slots, width)


def dot(a, b, ca, cb):
    return lax.dot_general(a, b, (((ca,), (cb,)), ((), ())), preferred_element_type=F32)


def make_general(frame_size, fsdp_size):
    chips = fsdp_size // 2

    def per_device(
        queries,
        keys,
        values,
        residual,
        target,
        output_weight,
        down_adapter,
        up_adapter,
        scene_of_frame,
        scene_adapter_row,
        valid_token_count,
    ):
        slots, width = queries.shape[1:]
        depth = output_weight.shape[0]
        shard = lax.axis_index("fsdp")
        group = lax.axis_index("frame")
        core = shard % 2
        chip = shard // 2

        weight_near = xor_send(output_weight, "fsdp", fsdp_size, 1)
        blocks = gather_scenes(jnp.concatenate([down_adapter, up_adapter], axis=0), frame_size)
        own_slot = scene_adapter_row[scene_of_frame[0]]
        offsets = [own_slot ^ group]
        for step in range(1, fsdp_size):
            offsets.append(xor_send(own_slot[None], "fsdp", fsdp_size, step)[0] ^ group)

        count = valid_token_count[0]
        valid = jnp.arange(slots, dtype=jnp.int32) < count
        attended = attend(queries[0], keys[0], values[0], valid)

        def partial(columns):
            mine = lax.dynamic_slice_in_dim(columns, core * depth, depth, 1)
            near = lax.dynamic_slice_in_dim(columns, (1 - core) * depth, depth, 1)
            return dot(mine, output_weight, 1, 0) + dot(near, weight_near, 1, 0)

        def chip_columns(which):
            return lax.dynamic_slice_in_dim(attended, which * 2 * depth, 2 * depth, 1)

        received = []
        for step in range(1, chips):
            theirs = xor_send(chip_columns(chip ^ step), "fsdp", fsdp_size, 2 * step)
            received.append(xor_send(partial(theirs).astype(BF16), "fsdp", fsdp_size, 2 * step))
        projected = partial(chip_columns(chip))
        for got in received:
            projected = projected + got.astype(F32)

        chosen = []
        for step in range(fsdp_size):
            pick = lax.dynamic_index_in_dim(blocks, offsets[step], 0, keepdims=False)
            chosen.append(pick if step == 0 else xor_send(pick, "fsdp", fsdp_size, step))
        adapters = jnp.zeros((2, down_adapter.shape[1], width), BF16)
        for step in range(fsdp_size):
            adapters = lax.dynamic_update_slice_in_dim(adapters, chosen[step], (shard ^ step) * depth, 2)
        down, up = adapters[0], adapters[1]

        low = dot(attended, down, 1, 1).astype(BF16)
        combined = (
            residual[0].astype(F32) + projected + ADAPTER_SCALE * dot(low, up, 1, 0) - target[0].astype(F32)
        )
        error = jnp.where(valid[:, None], combined, 0.0)
        tokens = count.astype(F32)
        loss = jnp.sum(error * error) / (tokens * width)
        cotangent = (2.0 * error / tokens).astype(BF16)
        up_terms = ADAPTER_SCALE * dot(low, cotangent, 0, 0)
        back = (ADAPTER_SCALE * dot(cotangent, up, 1, 1)).astype(BF16)
        down_terms = dot(back, attended, 0, 0)
        terms = jnp.concatenate([down_terms, up_terms], axis=0)

        pieces = []
        for step in range(fsdp_size):
            piece = lax.dynamic_slice_in_dim(terms, (shard ^ step) * depth, depth, 1)
            pieces.append(piece if step == 0 else xor_send(piece.astype(BF16), "fsdp", fsdp_size, step).astype(F32))
        dense = []
        for scene in range(frame_size):
            total = jnp.zeros_like(pieces[0])
            for offset, piece in zip(offsets, pieces):
                total = total + jnp.where(offset == scene, piece, 0.0)
            dense.append(total)
        dense = jnp.stack(dense)
        rank = down_adapter.shape[1]
        cut = 2 * rank * 5 // 8
        top = scatter_scenes(dense[:, :cut], frame_size, True)
        bottom = scatter_scenes(dense[:, cut:], frame_size, False)
        owned = jnp.concatenate([top, bottom], axis=0)
        return owned[None, :rank], owned[None, rank:], loss[None]

    return per_device


LANES = 128
VMEM = 20 * 1024 * 1024
COST = 7e8
ALONE = 52 * 1024 * 1024
SHARD, CORE, CHIP, COUNT, GROUP = range(5)


def kernel_call(
    body, name, scalars, operands, out_shape, micros, grid=None, in_specs=None, out_specs=None, after=(), scratch=(), vmem=VMEM
):
    whole = lambda shape: pl.BlockSpec(shape, lambda *_: (0,) * len(shape))
    inner_body = body
    ready = len(operands)

    def body(sc, *refs):
        inner_body(sc, *refs[:ready], *refs[ready + len(after) :])

    if in_specs is None:
        in_specs = [whole(x.shape) for x in operands]
    if out_specs is None:
        out_specs = jax.tree.map(lambda x: whole(x.shape), out_shape)
    return pl.pallas_call(
        body,
        out_shape=out_shape,
        grid_spec=pltpu.PrefetchScalarGridSpec(
            num_scalar_prefetch=1,
            grid=grid or (1,),
            in_specs=[*in_specs, *[pl.BlockSpec(memory_space=pl.ANY)] * len(after)],
            out_specs=out_specs,
            scratch_shapes=list(scratch),
        ),
        compiler_params=pltpu.CompilerParams(vmem_limit_bytes=vmem),
        cost_estimate=pl.CostEstimate(
            flops=int(micros * COST), bytes_accessed=0, transcendentals=0
        ),
        name=name,
    )(scalars, *operands, *after)


def ordered_call(body, name, scalars, operands, out_shape, micros, order):
    def inner_body(sc, *refs):
        outs = refs[len(operands) :]
        body(sc, *refs[: len(operands)], *[outs[order.index(i)] for i in range(len(order))])

    out = kernel_call(inner_body, name, scalars, operands, [out_shape[i] for i in order], micros)
    return [out[order.index(i)] for i in range(len(order))]


def fold_rows(rank, slots, depth):
    return rank * slots // depth


def fold_into(ref, rank, value):
    rows, depth = ref.shape[0] - rank, ref.shape[1]
    slots = value.shape[1]
    for i in range(depth // slots):
        ref[rank:, i * slots : (i + 1) * slots] = value[i * rows : (i + 1) * rows]


def unfold(ref, rank, slots):
    count = ref.shape[1] // slots
    return jnp.concatenate([ref[rank:, i * slots : (i + 1) * slots] for i in range(count)])


def shaped(shape, dtype=BF16):
    return jax.ShapeDtypeStruct(shape, dtype)


def attend_chip(counts, queries, keys, values, chip_offset, depth, after=()):
    slots, width = queries.shape[1:]
    size = width // HEADS
    heads = depth // size
    scale = math.log2(math.e) / math.sqrt(size)

    def body(sc, q_ref, k_ref, v_ref, out_ref, held, sems):
        def copy(c, i):
            shard = lax.axis_index("fsdp") ^ (2 * chip_offset + c)
            lanes = pl.ds(pl.multiple_of(shard * depth, LANES), depth)
            return pltpu.make_async_copy((q_ref, k_ref, v_ref)[i].at[0, :, lanes], held.at[c, i], sems.at[c, i])

        for i in range(3):
            copy(0, i).start()
        seen = lax.broadcasted_iota(jnp.int32, (1, slots), 1) < sc[0]
        at = [slice(h * size, (h + 1) * size) for h in range(heads)]
        for c in range(2):
            for i in range(3):
                copy(c, i).wait()
            if c == 0:
                for i in range(3):
                    copy(1, i).start()
            q, k, v = (held.at[c, i] for i in range(3))
            scores = [jnp.where(seen, dot(q[:, h], k[:, h], 1, 1), -1e30) for h in at]
            scores = [jnp.exp2((x - jnp.max(x, axis=1, keepdims=True)) * scale) for x in scores]
            weights = [(x * (1.0 / jnp.sum(x, axis=1, keepdims=True))).astype(BF16) for x in scores]
            for h, x in zip(at, weights):
                out_ref[c, :, h] = dot(x, v[:, h], 1, 0).astype(BF16)

    hbm, vmem = pl.BlockSpec(memory_space=pltpu.HBM), pl.BlockSpec(memory_space=pltpu.VMEM)
    return kernel_call(
        body,
        "attend",
        counts,
        (queries, keys, values),
        shaped((2, slots, depth)),
        4.0,
        in_specs=[hbm] * 3,
        out_specs=vmem,
        after=after,
        scratch=[pltpu.VMEM((2, 3, slots, depth), BF16), pltpu.SemaphoreType.DMA((2, 3))],
        vmem=ALONE,
    )


def bring_weight(scalars, weight, scene, rows_of, after):
    pieces = 4
    rows = weight.shape[0] // pieces

    def body(sc, in_ref, scene_ref, row_ref, out_ref, slot_ref, sems):
        copies = []
        for i in range(pieces):
            at = pl.ds(i * rows, rows)
            copies.append(pltpu.make_async_copy(in_ref.at[at], out_ref.at[at], sems.at[i]))
        for copy in copies:
            copy.start()
        slot_ref[...] = jnp.full(slot_ref.shape, row_ref[scene_ref[0]].astype(F32))
        for copy in copies:
            copy.wait()

    vmem, smem = pl.BlockSpec(memory_space=pltpu.VMEM), pl.BlockSpec(memory_space=pltpu.SMEM)
    return kernel_call(
        body,
        "bring_weight",
        scalars,
        (weight, scene, rows_of),
        [shaped(weight.shape), shaped((8, LANES), F32)],
        3.0,
        in_specs=[pl.BlockSpec(memory_space=pl.ANY), smem, smem],
        out_specs=[vmem, vmem],
        after=after,
        scratch=[pltpu.SemaphoreType.DMA((pieces,))],
    )


def project(scalars, columns, weight, weight_near, chip_offset, size, after):
    _, slots, depth = columns.shape

    def body(sc, x_ref, own_ref, near_ref, out_ref):
        for k in range(size):
            start = (sc[SHARD] ^ (2 * chip_offset) ^ k) * depth
            cols = pl.ds(pl.multiple_of(start, LANES), depth)
            out_ref[k] = (dot(x_ref[0], own_ref[:, cols], 1, 0) + dot(x_ref[1], near_ref[:, cols], 1, 0)).astype(BF16)

    vmem = pl.BlockSpec(memory_space=pltpu.VMEM)
    return kernel_call(
        body,
        "project",
        scalars,
        (columns, weight, weight_near),
        shaped((size, slots, depth)),
        3.0,
        in_specs=[vmem] * 3,
        out_specs=vmem,
        after=after,
    )


def base_error(scalars, columns, weight, weight_near, residual, target, size, after):
    _, slots, depth = columns.shape

    def body(sc, x_ref, own_ref, near_ref, r_ref, t_ref, out_ref):
        cols = pl.ds(pl.multiple_of((sc[SHARD] ^ pl.program_id(0)) * depth, LANES), depth)
        total = dot(x_ref[0], own_ref[:, cols], 1, 0) + dot(x_ref[1], near_ref[:, cols], 1, 0)
        out_ref[0] = total + (r_ref[0].astype(F32) - t_ref[0].astype(F32))

    tokens = pl.BlockSpec((1, slots, depth), lambda k, sc: (0, 0, sc[SHARD] ^ k))
    vmem = pl.BlockSpec(memory_space=pltpu.VMEM)
    return kernel_call(
        body,
        "base",
        scalars,
        (columns, weight, weight_near, residual, target),
        shaped((size, slots, depth), F32),
        7.0,
        grid=(size,),
        in_specs=[vmem, vmem, vmem, tokens, tokens],
        out_specs=pl.BlockSpec((1, slots, depth), lambda k, sc: (k, 0, 0)),
        after=after,
    )


def error_terms(scalars, base, received, low_part, adapters):
    size, slots, depth = base.shape
    rank = low_part.shape[0]
    peers = len(received)

    def body(sc, base_ref, low_ref, *refs):
        got, up_refs, pieces = refs[:peers], refs[peers : peers + size][::-1], refs[peers + size : -1]
        count = sc[COUNT]
        tokens = count.astype(F32)
        per_token = 2.0 / tokens
        valid = lax.broadcasted_iota(jnp.int32, (slots, 1), 0) < count
        low_wide = low_ref[...]
        for ref in up_refs[1:]:
            low_wide = low_wide + unfold(ref, rank, slots).astype(F32)
        low_turned = ADAPTER_SCALE * low_wide.astype(BF16)
        low_state = ADAPTER_SCALE * low_wide.T.astype(BF16)
        back = jnp.zeros((slots, rank), F32)
        squares = jnp.zeros((slots, depth), F32)
        for k in range(size):
            up = up_refs[k][:rank, :]
            error = base_ref[k] + dot(low_state, up, 1, 0)
            for ref in got:
                error = error + ref[k].astype(F32)
            error = jnp.where(valid, error, 0.0)
            squares = squares + error * error
            cotangent = (error * per_token).astype(BF16)
            back = back + dot(cotangent, up, 1, 1)
            pieces[k][:rank, :] = dot(low_turned, cotangent, 1, 0).astype(BF16)
        refs[-1][0, 0] = jnp.sum(squares) / (tokens * (size * depth))
        turned = (ADAPTER_SCALE * back).T.astype(BF16)
        for k in range(size):
            fold_into(pieces[k], rank, turned)

    whole = lambda x: pl.BlockSpec(x.shape, lambda k, sc: (0,) * len(x.shape))
    out_shape = [shaped((rank + fold_rows(rank, slots, depth), depth))] * size + [shaped((1, 1), F32)]
    out = kernel_call(
        body,
        "error",
        scalars,
        (base, low_part, *received, *adapters[::-1]),
        out_shape,
        3.0,
        in_specs=[whole(x) for x in (base, low_part, *received, *adapters[::-1])],
        out_specs=[whole(x) for x in out_shape[:-1]] + [pl.BlockSpec(memory_space=pltpu.SMEM)],
    )
    return out[:size], out[size]


def join_adapters(scalars, down, up, after):
    _, rank, depth = down.shape

    def body(sc, down_ref, up_ref, out_ref):
        out_ref[:rank, :] = down_ref[0]
        out_ref[rank:, :] = up_ref[0]

    return kernel_call(body, "join", scalars, (down, up), shaped((2 * rank, depth)), 1.0, after=after)


def stack_blocks(scalars, blocks, places, columns, slot_tiles, after):
    count, chips = len(blocks), len(columns)

    def body(sc, *refs):
        ins, out_ref, others = refs[: count + 2 * chips], refs[count + 2 * chips], refs[count + 2 * chips + 1 :]
        for i in range(count):
            out_ref[places[i]] = ins[i][...]
        for i in range(chips):
            others[i][...] = ins[count + i][1]
            others[chips + i][...] = ins[count + chips + i][...]

    out = kernel_call(
        body,
        "stack",
        scalars,
        (*blocks, *columns, *slot_tiles),
        [shaped((count, *blocks[0].shape))]
        + [shaped(x.shape[1:]) for x in columns]
        + [shaped(x.shape, F32) for x in slot_tiles],
        0.8,
        after=after,
    )
    return out[0], out[1 : 1 + chips], out[1 + chips :]


def slot_offset(sc, slot_ref):
    return jnp.max(slot_ref[...]).astype(jnp.int32) ^ sc[GROUP]


def choose_adapters(scalars, slot_list, blocks, columns, after):
    arrays = []
    for x, _ in blocks:
        if all(x is not y for y in arrays):
            arrays.append(x)
    where = [next(i for i, y in enumerate(arrays) if x is y) for x, _ in blocks]
    _, rows, depth = arrays[0].shape
    rank = rows // 2
    size = len(slot_list)
    slots = columns[0].shape[0]

    def body(sc, *refs):
        slot_refs, column_refs, refs = refs[:size], refs[size : 2 * size], refs[2 * size :]
        outs, low_ref, held = refs[len(arrays) : -2], refs[-2], refs[-1]
        for k in range(size):
            offset = slot_offset(sc, slot_refs[k])
            for scene, (_, place) in enumerate(blocks):

                @pl.when(offset == scene)
                def _():
                    held[k] = refs[where[scene]][place]

        for k in range(size):
            part = dot(held[k, :rank, :], column_refs[k][...], 1, 1)
            if k == 0:
                low_ref[...] = part
            outs[k][:rank, :] = held[k, rank:, :]
            fold_into(outs[k], rank, part.astype(BF16))

    out = kernel_call(
        body,
        "choose",
        scalars,
        (*slot_list, *columns, *arrays),
        [shaped((rank + fold_rows(rank, slots, depth), depth))] * size + [shaped((rank, slots), F32)],
        2.0,
        after=after,
        scratch=[pltpu.VMEM((size, rows, depth), BF16)],
    )
    return out[:size], out[size]


def scene_sum(offsets, pieces, scene):
    total = jnp.zeros(pieces[0].shape, F32)
    for offset, piece in zip(offsets, pieces):
        total = total + jnp.where(offset == scene, piece, 0.0)
    return total


def first_refs(offsets, pieces, keep, sends, near, far, near_mul, far_mul):
    for f in range(far):
        keep[f] = scene_sum(offsets, pieces, f * far_mul)
        for s in range(1, near):
            sends[s - 1][f] = scene_sum(offsets, pieces, f * far_mul + s * near_mul).astype(BF16)


def second_refs(keep, received, final, sends, far):
    for f in range(far):
        total = keep[f]
        for ref in received:
            total = total + ref[f].astype(F32)
        if f == 0:
            final[...] = total
        else:
            sends[f - 1][...] = total.astype(BF16)


def make_chunked(frame_size, fsdp_size):
    chips = fsdp_size // 2
    outer, inner = split_axis(frame_size)
    along_inner = (inner, outer, 1, inner)
    along_outer = (outer, inner, inner, 1)

    def send_frames(arrays, step):
        return [xor_send(x, "frame", frame_size, (i + 1) * step) for i, x in enumerate(arrays)]

    def send_shards(arrays):
        return [arrays[0]] + [xor_send(x, "fsdp", fsdp_size, k) for k, x in enumerate(arrays) if k]

    def first_shapes(rank, w, order):
        near, far = order[:2]
        return [shaped((far, rank, w), F32)] + [shaped((far, rank, w))] * (near - 1)

    def second_shapes(rank, w, order):
        far = order[1]
        return [shaped((rank, w), F32)] + [shaped((rank, w))] * (far - 1)

    def per_device(
        queries,
        keys,
        values,
        residual,
        target,
        output_weight,
        down_adapter,
        up_adapter,
        scene_of_frame,
        scene_adapter_row,
        valid_token_count,
    ):
        depth = output_weight.shape[0]
        rank = down_adapter.shape[1]
        slots = queries.shape[1]
        shard = lax.axis_index("fsdp").astype(jnp.int32)
        group = lax.axis_index("frame").astype(jnp.int32)
        places = [shard, shard % 2, shard // 2, valid_token_count[0], group]
        scalars = jnp.stack(places)

        weight_near = xor_send(output_weight, "fsdp", fsdp_size, 1)

        attended = [attend_chip(valid_token_count, queries, keys, values, c, depth) for c in range(1, chips)]
        theirs = [xor_send(x, "fsdp", fsdp_size, 2 * (c + 1)) for c, x in enumerate(attended)]
        block = join_adapters(scalars, down_adapter, up_adapter, attended[:1])
        outer_blocks = {
            o: xor_send(block, "frame", frame_size, o * inner)
            for o in sorted(range(1, outer), key=lambda o: -o.bit_length())
        }
        own = attend_chip(valid_token_count, queries, keys, values, 0, depth, [block, weight_near])
        attended = [own] + attended

        weight_near, own_slot = bring_weight(
            scalars, weight_near, scene_of_frame, scene_adapter_row, [own]
        )
        near_slots = [own_slot] + [xor_send(own_slot, "fsdp", fsdp_size, 2 * c) for c in range(1, chips)]
        partials = []
        after = [own]
        for c, x in enumerate(theirs):
            part = project(scalars, x, output_weight, weight_near, c + 1, fsdp_size, after)
            partials.append(xor_send(part, "fsdp", fsdp_size, 2 * (c + 1)))
        stacked, others, near_slots = stack_blocks(
            scalars,
            [*outer_blocks.values(), block],
            [*outer_blocks, 0],
            [own, *theirs],
            near_slots,
            [part],
        )
        slot_list = [x for slot in near_slots for x in (slot, xor_send(slot, "fsdp", fsdp_size, 1))]
        far_blocks = [xor_send(stacked, "frame", frame_size, s) for s in range(1, inner)]
        base = base_error(
            scalars,
            own,
            output_weight,
            weight_near,
            residual,
            target,
            fsdp_size,
            [stacked],
        )
        blocks = [((stacked, *far_blocks)[s], o) for o in range(outer) for s in range(inner)]

        columns = [None] * fsdp_size
        for c, (x, other) in enumerate(zip([own] + theirs, others)):
            columns[2 * c] = x[0]
            columns[2 * c + 1] = xor_send(other, "fsdp", fsdp_size, 1)

        chosen, low_part = choose_adapters(scalars, slot_list, blocks, columns, [base])
        adapters = send_shards(chosen)
        pieces, loss = error_terms(scalars, base, partials, low_part, adapters)
        pieces = send_shards(pieces)

        cut = depth // 2 // LANES * LANES
        first_shape = first_shapes(rank, depth + cut, along_inner) + first_shapes(rank, depth - cut, along_outer)
        second_shape = second_shapes(rank, depth + cut, along_inner) + second_shapes(
            rank, depth - cut, along_outer
        )

        def first(sc, *refs):
            slot_refs, got, cols = (refs[i * fsdp_size : (i + 1) * fsdp_size] for i in range(3))
            got = got[::-1]
            outs = refs[3 * fsdp_size :]
            offsets = [slot_offset(sc, ref) for ref in slot_refs]
            downs = [dot(unfold(p, rank, slots), c[...], 1, 0) for p, c in zip(got, cols)]
            down_outs = [ref.at[:, :, :depth] for ref in outs[:inner]]
            first_refs(offsets, downs, down_outs[0], down_outs[1:], *along_inner)
            ups = [p[:rank, :cut].astype(F32) for p in got]
            up_outs = [ref.at[:, :, depth:] for ref in outs[:inner]]
            first_refs(offsets, ups, up_outs[0], up_outs[1:], *along_inner)
            ups = [p[:rank, cut:depth].astype(F32) for p in got]
            first_refs(offsets, ups, outs[inner], outs[inner + 1 :], *along_outer)

        far = [o for o in range(1, outer) if 2 * o >= outer]
        near = [o for o in range(1, outer) if 2 * o < outer]
        order = [0, inner, *[inner + o for o in far], *range(1, inner), *[inner + o for o in near]]
        out = ordered_call(first, "first", scalars, (*slot_list, *pieces[::-1], *columns), first_shape, 2.0, order)
        keeps = out[0], out[inner]
        outer_got = send_frames(out[inner + 1 :], inner)
        inner_got = send_frames(out[1:inner], 1)

        ways = [("outer", o) for o in far] + [("inner", i) for i in range(1, inner)] + [("outer", o) for o in near]

        def second(sc, inner_keep, outer_keep, *refs):
            got = dict(zip(ways, refs))
            outs = refs[len(ways) :]
            inners = [got["inner", i] for i in range(1, inner)]
            outers = [got["outer", o] for o in range(1, outer)]
            second_refs(inner_keep, inners, outs[0], outs[1:outer], outer)
            second_refs(outer_keep, outers, outs[outer], outs[outer + 1 :], inner)

        order = [0, outer, *far, *near, *[outer + i for i in range(1, inner)]]
        sent = {"inner": inner_got, "outer": outer_got}
        operands = (*keeps, *[sent[way][i - 1] for way, i in ways])
        out = ordered_call(second, "second", scalars, operands, second_shape, 0.8, order)
        sent = send_frames(out[1:outer], inner)
        one = (out[0], *[sent[o - 1] for o in far + near])
        two = (out[outer], *send_frames(out[outer + 1 :], 1))

        def finish(sc, *refs):
            down_ref, up_ref = refs[-2:]
            for part, which in ((0, refs[: len(one)]), (1, refs[len(one) : -2])):
                total = which[0][...]
                for ref in which[1:]:
                    total = total + ref[...].astype(F32)
                if part == 0:
                    down_ref[0] = total[:, :depth]
                    up_ref[0, :, :cut] = total[:, depth:]
                else:
                    up_ref[0, :, cut:] = total

        grad = shaped((1, rank, depth), F32)
        grad_down, grad_up = kernel_call(finish, "finish", scalars, (*one, *two), [grad, grad], 1.3)
        return grad_down, grad_up, loss[0]

    return per_device


def solution(mesh):
    frame_size, fsdp_size = mesh.shape["frame"], mesh.shape["fsdp"]
    rows = P(("frame", "fsdp"), None, None)
    adapter = P("frame", None, "fsdp")
    vector = P(("frame", "fsdp"))
    placed = (rows, rows, rows, rows, rows, P("fsdp", None), adapter, adapter, vector, P(), vector)
    chunked = make_chunked(frame_size, fsdp_size)
    general = make_general(frame_size, fsdp_size)

    def per_device(*operands):
        depth = operands[5].shape[0]
        return (chunked if depth % (3 * LANES) == 0 and depth <= 4 * operands[0].shape[1] else general)(*operands)

    return jax.shard_map(
        per_device,
        mesh=mesh,
        in_specs=placed,
        out_specs=(adapter, adapter, vector),
        check_vma=False,
    )
```

```python
import math

import jax
import jax.numpy as jnp
from jax import lax
from jax.experimental import pallas as pl
from jax.experimental.pallas import tpu as pltpu
from jax.sharding import PartitionSpec as P

HEADS = 24
ADAPTER_SCALE = 2.0
F32 = jnp.float32
BF16 = jnp.bfloat16


def xor_send(value, axis, size, offset):
    return lax.ppermute(value, axis, [(i, i ^ offset) for i in range(size)])


def split_axis(size):
    inner = 1 << ((size.bit_length() - 1) // 2)
    return size // inner, inner


def gather_scenes(block, size):
    outer, inner = split_axis(size)
    first = [block]
    for step in range(1, outer):
        first.append(xor_send(block, "frame", size, step * inner))
    out = [None] * size
    for step in range(outer):
        out[step * inner] = first[step]
    for step in range(1, inner):
        for lead in range(outer):
            out[lead * inner + step] = xor_send(first[lead], "frame", size, step)
    return jnp.stack(out)


def scatter_scenes(dense, size, inner_first):
    outer, inner = split_axis(size)
    near, far = (inner, outer) if inner_first else (outer, inner)
    near_mul, far_mul = (1, inner) if inner_first else (inner, 1)

    def at(f, s):
        return dense[f * far_mul + s * near_mul]

    staged = [at(f, 0) for f in range(far)]
    for step in range(1, near):
        sent = jnp.stack([at(f, step) for f in range(far)]).astype(BF16)
        got = xor_send(sent, "frame", size, step * near_mul)
        staged = [staged[f] + got[f].astype(F32) for f in range(far)]
    total = staged[0]
    for step in range(1, far):
        total = total + xor_send(staged[step].astype(BF16), "frame", size, step * far_mul).astype(F32)
    return total


def attend(queries, keys, values, valid):
    slots, width = queries.shape
    size = width // HEADS
    q = queries.reshape(slots, HEADS, size)
    k = keys.reshape(slots, HEADS, size)
    v = values.reshape(slots, HEADS, size)
    scores = jnp.einsum("qhd,khd->hqk", q, k, preferred_element_type=F32) * (1.0 / math.sqrt(size))
    scores = jnp.where(valid[None, None, :], scores, -jnp.inf)
    peak = jnp.max(scores, axis=-1, keepdims=True)
    exponent = jnp.exp(scores - peak)
    weights = (exponent / jnp.sum(exponent, axis=-1, keepdims=True)).astype(BF16)
    out = jnp.einsum("hqk,khd->qhd", weights, v, preferred_element_type=F32)
    return out.astype(BF16).reshape(slots, width)


def dot(a, b, ca, cb):
    return lax.dot_general(a, b, (((ca,), (cb,)), ((), ())), preferred_element_type=F32)


def make_general(frame_size, fsdp_size):
    chips = fsdp_size // 2

    def per_device(
        queries,
        keys,
        values,
        residual,
        target,
        output_weight,
        down_adapter,
        up_adapter,
        scene_of_frame,
        scene_adapter_row,
        valid_token_count,
    ):
        slots, width = queries.shape[1:]
        depth = output_weight.shape[0]
        shard = lax.axis_index("fsdp")
        group = lax.axis_index("frame")
        core = shard % 2
        chip = shard // 2

        weight_near = xor_send(output_weight, "fsdp", fsdp_size, 1)
        blocks = gather_scenes(jnp.concatenate([down_adapter, up_adapter], axis=0), frame_size)
        own_slot = scene_adapter_row[scene_of_frame[0]]
        offsets = [own_slot ^ group]
        for step in range(1, fsdp_size):
            offsets.append(xor_send(own_slot[None], "fsdp", fsdp_size, step)[0] ^ group)

        count = valid_token_count[0]
        valid = jnp.arange(slots, dtype=jnp.int32) < count
        attended = attend(queries[0], keys[0], values[0], valid)

        def partial(columns):
            mine = lax.dynamic_slice_in_dim(columns, core * depth, depth, 1)
            near = lax.dynamic_slice_in_dim(columns, (1 - core) * depth, depth, 1)
            return dot(mine, output_weight, 1, 0) + dot(near, weight_near, 1, 0)

        def chip_columns(which):
            return lax.dynamic_slice_in_dim(attended, which * 2 * depth, 2 * depth, 1)

        received = []
        for step in range(1, chips):
            theirs = xor_send(chip_columns(chip ^ step), "fsdp", fsdp_size, 2 * step)
            received.append(xor_send(partial(theirs).astype(BF16), "fsdp", fsdp_size, 2 * step))
        projected = partial(chip_columns(chip))
        for got in received:
            projected = projected + got.astype(F32)

        chosen = []
        for step in range(fsdp_size):
            pick = lax.dynamic_index_in_dim(blocks, offsets[step], 0, keepdims=False)
            chosen.append(pick if step == 0 else xor_send(pick, "fsdp", fsdp_size, step))
        adapters = jnp.zeros((2, down_adapter.shape[1], width), BF16)
        for step in range(fsdp_size):
            adapters = lax.dynamic_update_slice_in_dim(adapters, chosen[step], (shard ^ step) * depth, 2)
        down, up = adapters[0], adapters[1]

        low = dot(attended, down, 1, 1).astype(BF16)
        combined = (
            residual[0].astype(F32) + projected + ADAPTER_SCALE * dot(low, up, 1, 0) - target[0].astype(F32)
        )
        error = jnp.where(valid[:, None], combined, 0.0)
        tokens = count.astype(F32)
        loss = jnp.sum(error * error) / (tokens * width)
        cotangent = (2.0 * error / tokens).astype(BF16)
        up_terms = ADAPTER_SCALE * dot(low, cotangent, 0, 0)
        back = (ADAPTER_SCALE * dot(cotangent, up, 1, 1)).astype(BF16)
        down_terms = dot(back, attended, 0, 0)
        terms = jnp.concatenate([down_terms, up_terms], axis=0)

        pieces = []
        for step in range(fsdp_size):
            piece = lax.dynamic_slice_in_dim(terms, (shard ^ step) * depth, depth, 1)
            pieces.append(piece if step == 0 else xor_send(piece.astype(BF16), "fsdp", fsdp_size, step).astype(F32))
        dense = []
        for scene in range(frame_size):
            total = jnp.zeros_like(pieces[0])
            for offset, piece in zip(offsets, pieces):
                total = total + jnp.where(offset == scene, piece, 0.0)
            dense.append(total)
        dense = jnp.stack(dense)
        rank = down_adapter.shape[1]
        cut = 2 * rank * 5 // 8
        top = scatter_scenes(dense[:, :cut], frame_size, True)
        bottom = scatter_scenes(dense[:, cut:], frame_size, False)
        owned = jnp.concatenate([top, bottom], axis=0)
        return owned[None, :rank], owned[None, rank:], loss[None]

    return per_device


LANES = 128
VMEM = 20 * 1024 * 1024
COST = 7e8
ALONE = 52 * 1024 * 1024
FIRST = 62 * 1024 * 1024
SHARD, CORE, CHIP, COUNT, GROUP = range(5)


def kernel_call(
    body, name, scalars, operands, out_shape, micros, grid=None, in_specs=None, out_specs=None, after=(), scratch=(), vmem=VMEM
):
    whole = lambda shape: pl.BlockSpec(shape, lambda *_: (0,) * len(shape))
    inner_body = body
    ready = len(operands)

    def body(sc, *refs):
        inner_body(sc, *refs[:ready], *refs[ready + len(after) :])

    if in_specs is None:
        in_specs = [whole(x.shape) for x in operands]
    if out_specs is None:
        out_specs = jax.tree.map(lambda x: whole(x.shape), out_shape)
    return pl.pallas_call(
        body,
        out_shape=out_shape,
        grid_spec=pltpu.PrefetchScalarGridSpec(
            num_scalar_prefetch=1,
            grid=grid or (1,),
            in_specs=[*in_specs, *[pl.BlockSpec(memory_space=pl.ANY)] * len(after)],
            out_specs=out_specs,
            scratch_shapes=list(scratch),
        ),
        compiler_params=pltpu.CompilerParams(vmem_limit_bytes=vmem),
        cost_estimate=pl.CostEstimate(
            flops=int(micros * COST), bytes_accessed=0, transcendentals=0
        ),
        name=name,
    )(scalars, *operands, *after)


def ordered_call(body, name, scalars, operands, out_shape, micros, order):
    def inner_body(sc, *refs):
        outs = refs[len(operands) :]
        body(sc, *refs[: len(operands)], *[outs[order.index(i)] for i in range(len(order))])

    out = kernel_call(inner_body, name, scalars, operands, [out_shape[i] for i in order], micros)
    return [out[order.index(i)] for i in range(len(order))]


def fold_rows(rank, slots, depth):
    return rank * slots // depth


def fold_into(ref, rank, value):
    rows, depth = ref.shape[0] - rank, ref.shape[1]
    slots = value.shape[1]
    for i in range(depth // slots):
        ref[rank:, i * slots : (i + 1) * slots] = value[i * rows : (i + 1) * rows]


def unfold(ref, rank, slots):
    count = ref.shape[1] // slots
    return jnp.concatenate([ref[rank:, i * slots : (i + 1) * slots] for i in range(count)])


def shaped(shape, dtype=BF16):
    return jax.ShapeDtypeStruct(shape, dtype)


def attend_chip(counts, queries, keys, values, chip_offset, depth, after=(), limit=ALONE):
    slots, width = queries.shape[1:]
    size = width // HEADS
    heads = depth // size
    scale = math.log2(math.e) / math.sqrt(size)

    def body(sc, q_ref, k_ref, v_ref, out_ref, held, sems):
        def copy(c, i):
            shard = lax.axis_index("fsdp") ^ (2 * chip_offset + c)
            lanes = pl.ds(pl.multiple_of(shard * depth, LANES), depth)
            return pltpu.make_async_copy((q_ref, k_ref, v_ref)[i].at[0, :, lanes], held.at[c, i], sems.at[c, i])

        for i in range(3):
            copy(0, i).start()
        seen = lax.broadcasted_iota(jnp.int32, (1, slots), 1) < sc[0]
        at = [slice(h * size, (h + 1) * size) for h in range(heads)]
        for c in range(2):
            for i in range(3):
                copy(c, i).wait()
            if c == 0:
                for i in range(3):
                    copy(1, i).start()
            q, k, v = (held.at[c, i] for i in range(3))
            scores = [jnp.where(seen, dot(q[:, h], k[:, h], 1, 1), -1e30) for h in at]
            scores = [jnp.exp2((x - jnp.max(x, axis=1, keepdims=True)) * scale) for x in scores]
            weights = [(x * (1.0 / jnp.sum(x, axis=1, keepdims=True))).astype(BF16) for x in scores]
            for h, x in zip(at, weights):
                out_ref[c, :, h] = dot(x, v[:, h], 1, 0).astype(BF16)

    hbm, vmem = pl.BlockSpec(memory_space=pltpu.HBM), pl.BlockSpec(memory_space=pltpu.VMEM)
    return kernel_call(
        body,
        "attend",
        counts,
        (queries, keys, values),
        shaped((2, slots, depth)),
        4.0,
        in_specs=[hbm] * 3,
        out_specs=vmem,
        after=after,
        scratch=[pltpu.VMEM((2, 3, slots, depth), BF16), pltpu.SemaphoreType.DMA((2, 3))],
        vmem=limit,
    )


def bring_weight(scalars, weight, scene, rows_of, after):
    pieces = 4
    rows = weight.shape[0] // pieces

    def body(sc, in_ref, scene_ref, row_ref, out_ref, slot_ref, sems):
        copies = []
        for i in range(pieces):
            at = pl.ds(i * rows, rows)
            copies.append(pltpu.make_async_copy(in_ref.at[at], out_ref.at[at], sems.at[i]))
        for copy in copies:
            copy.start()
        slot_ref[...] = jnp.full(slot_ref.shape, row_ref[scene_ref[0]].astype(F32))
        for copy in copies:
            copy.wait()

    vmem, smem = pl.BlockSpec(memory_space=pltpu.VMEM), pl.BlockSpec(memory_space=pltpu.SMEM)
    return kernel_call(
        body,
        "bring_weight",
        scalars,
        (weight, scene, rows_of),
        [shaped(weight.shape), shaped((8, LANES), F32)],
        3.0,
        in_specs=[pl.BlockSpec(memory_space=pl.ANY), smem, smem],
        out_specs=[vmem, vmem],
        after=after,
        scratch=[pltpu.SemaphoreType.DMA((pieces,))],
    )


def project(scalars, columns, weight, weight_near, chip_offset, size, after):
    _, slots, depth = columns.shape

    def body(sc, x_ref, own_ref, near_ref, out_ref):
        for k in range(size):
            start = (sc[SHARD] ^ (2 * chip_offset) ^ k) * depth
            cols = pl.ds(pl.multiple_of(start, LANES), depth)
            out_ref[k] = (dot(x_ref[0], own_ref[:, cols], 1, 0) + dot(x_ref[1], near_ref[:, cols], 1, 0)).astype(BF16)

    vmem = pl.BlockSpec(memory_space=pltpu.VMEM)
    return kernel_call(
        body,
        "project",
        scalars,
        (columns, weight, weight_near),
        shaped((size, slots, depth)),
        3.0,
        in_specs=[vmem] * 3,
        out_specs=vmem,
        after=after,
    )


def base_error(scalars, columns, weight, weight_near, residual, target, size, after):
    _, slots, depth = columns.shape

    def body(sc, x_ref, own_ref, near_ref, r_ref, t_ref, out_ref):
        cols = pl.ds(pl.multiple_of((sc[SHARD] ^ pl.program_id(0)) * depth, LANES), depth)
        total = dot(x_ref[0], own_ref[:, cols], 1, 0) + dot(x_ref[1], near_ref[:, cols], 1, 0)
        out_ref[0] = total + (r_ref[0].astype(F32) - t_ref[0].astype(F32))

    tokens = pl.BlockSpec((1, slots, depth), lambda k, sc: (0, 0, sc[SHARD] ^ k))
    vmem = pl.BlockSpec(memory_space=pltpu.VMEM)
    return kernel_call(
        body,
        "base",
        scalars,
        (columns, weight, weight_near, residual, target),
        shaped((size, slots, depth), F32),
        7.0,
        grid=(size,),
        in_specs=[vmem, vmem, vmem, tokens, tokens],
        out_specs=pl.BlockSpec((1, slots, depth), lambda k, sc: (k, 0, 0)),
        after=after,
    )


def error_terms(scalars, base, received, low_part, adapters):
    size, slots, depth = base.shape
    rank = low_part.shape[0]
    peers = len(received)

    def body(sc, base_ref, low_ref, *refs):
        got, up_refs, pieces = refs[:peers], refs[peers : peers + size][::-1], refs[peers + size : -1]
        count = sc[COUNT]
        tokens = count.astype(F32)
        per_token = 2.0 / tokens
        valid = lax.broadcasted_iota(jnp.int32, (slots, 1), 0) < count
        low_wide = low_ref[...]
        for ref in up_refs[1:]:
            low_wide = low_wide + unfold(ref, rank, slots).astype(F32)
        low_turned = ADAPTER_SCALE * low_wide.astype(BF16)
        low_state = ADAPTER_SCALE * low_wide.T.astype(BF16)
        back = jnp.zeros((slots, rank), F32)
        squares = jnp.zeros((slots, depth), F32)
        for k in range(size):
            up = up_refs[k][:rank, :]
            error = base_ref[k] + dot(low_state, up, 1, 0)
            for ref in got:
                error = error + ref[k].astype(F32)
            error = jnp.where(valid, error, 0.0)
            squares = squares + error * error
            cotangent = (error * per_token).astype(BF16)
            back = back + dot(cotangent, up, 1, 1)
            pieces[k][:rank, :] = dot(low_turned, cotangent, 1, 0).astype(BF16)
        refs[-1][0, 0] = jnp.sum(squares) / (tokens * (size * depth))
        turned = (ADAPTER_SCALE * back).T.astype(BF16)
        for k in range(size):
            fold_into(pieces[k], rank, turned)

    whole = lambda x: pl.BlockSpec(x.shape, lambda k, sc: (0,) * len(x.shape))
    out_shape = [shaped((rank + fold_rows(rank, slots, depth), depth))] * size + [shaped((1, 1), F32)]
    out = kernel_call(
        body,
        "error",
        scalars,
        (base, low_part, *received, *adapters[::-1]),
        out_shape,
        3.0,
        in_specs=[whole(x) for x in (base, low_part, *received, *adapters[::-1])],
        out_specs=[whole(x) for x in out_shape[:-1]] + [pl.BlockSpec(memory_space=pltpu.SMEM)],
    )
    return out[:size], out[size]


def join_adapters(scalars, down, up, after):
    _, rank, depth = down.shape

    def body(sc, down_ref, up_ref, out_ref):
        out_ref[:rank, :] = down_ref[0]
        out_ref[rank:, :] = up_ref[0]

    return kernel_call(body, "join", scalars, (down, up), shaped((2 * rank, depth)), 1.0, after=after)


def stack_blocks(scalars, blocks, places, columns, slot_tiles, after):
    count, chips = len(blocks), len(columns)

    def body(sc, *refs):
        ins, out_ref, others = refs[: count + 2 * chips], refs[count + 2 * chips], refs[count + 2 * chips + 1 :]
        for i in range(count):
            out_ref[places[i]] = ins[i][...]
        for i in range(chips):
            others[i][...] = ins[count + i][1]
            others[chips + i][...] = ins[count + chips + i][...]

    out = kernel_call(
        body,
        "stack",
        scalars,
        (*blocks, *columns, *slot_tiles),
        [shaped((count, *blocks[0].shape))]
        + [shaped(x.shape[1:]) for x in columns]
        + [shaped(x.shape, F32) for x in slot_tiles],
        0.8,
        after=after,
    )
    return out[0], out[1 : 1 + chips], out[1 + chips :]


def slot_offset(sc, slot_ref):
    return jnp.max(slot_ref[...]).astype(jnp.int32) ^ sc[GROUP]


def choose_adapters(scalars, slot_list, blocks, columns, after):
    arrays = []
    for x, _ in blocks:
        if all(x is not y for y in arrays):
            arrays.append(x)
    where = [next(i for i, y in enumerate(arrays) if x is y) for x, _ in blocks]
    _, rows, depth = arrays[0].shape
    rank = rows // 2
    size = len(slot_list)
    slots = columns[0].shape[0]

    def body(sc, *refs):
        slot_refs, column_refs, refs = refs[:size], refs[size : 2 * size], refs[2 * size :]
        outs, low_ref, held = refs[len(arrays) : -2], refs[-2], refs[-1]
        for k in range(size):
            offset = slot_offset(sc, slot_refs[k])
            for scene, (_, place) in enumerate(blocks):

                @pl.when(offset == scene)
                def _():
                    held[k] = refs[where[scene]][place]

        for k in range(size):
            part = dot(held[k, :rank, :], column_refs[k][...], 1, 1)
            if k == 0:
                low_ref[...] = part
            outs[k][:rank, :] = held[k, rank:, :]
            fold_into(outs[k], rank, part.astype(BF16))

    out = kernel_call(
        body,
        "choose",
        scalars,
        (*slot_list, *columns, *arrays),
        [shaped((rank + fold_rows(rank, slots, depth), depth))] * size + [shaped((rank, slots), F32)],
        2.0,
        after=after,
        scratch=[pltpu.VMEM((size, rows, depth), BF16)],
    )
    return out[:size], out[size]


def scene_sum(offsets, pieces, scene):
    total = jnp.zeros(pieces[0].shape, F32)
    for offset, piece in zip(offsets, pieces):
        total = total + jnp.where(offset == scene, piece, 0.0)
    return total


def first_refs(offsets, pieces, keep, sends, near, far, near_mul, far_mul):
    for f in range(far):
        keep[f] = scene_sum(offsets, pieces, f * far_mul)
        for s in range(1, near):
            sends[s - 1][f] = scene_sum(offsets, pieces, f * far_mul + s * near_mul).astype(BF16)


def second_refs(keep, received, final, sends, far):
    for f in range(far):
        total = keep[f]
        for ref in received:
            total = total + ref[f].astype(F32)
        if f == 0:
            final[...] = total
        else:
            sends[f - 1][...] = total.astype(BF16)


def make_chunked(frame_size, fsdp_size):
    chips = fsdp_size // 2
    outer, inner = split_axis(frame_size)
    along_inner = (inner, outer, 1, inner)
    along_outer = (outer, inner, inner, 1)

    def send_frames(arrays, step):
        return [xor_send(x, "frame", frame_size, (i + 1) * step) for i, x in enumerate(arrays)]

    def send_shards(arrays):
        return [arrays[0]] + [xor_send(x, "fsdp", fsdp_size, k) for k, x in enumerate(arrays) if k]

    def first_shapes(rank, w, order):
        near, far = order[:2]
        return [shaped((far, rank, w), F32)] + [shaped((far, rank, w))] * (near - 1)

    def second_shapes(rank, w, order):
        far = order[1]
        return [shaped((rank, w), F32)] + [shaped((rank, w))] * (far - 1)

    def per_device(
        queries,
        keys,
        values,
        residual,
        target,
        output_weight,
        down_adapter,
        up_adapter,
        scene_of_frame,
        scene_adapter_row,
        valid_token_count,
    ):
        depth = output_weight.shape[0]
        rank = down_adapter.shape[1]
        slots = queries.shape[1]
        shard = lax.axis_index("fsdp").astype(jnp.int32)
        group = lax.axis_index("frame").astype(jnp.int32)
        places = [shard, shard % 2, shard // 2, valid_token_count[0], group]
        scalars = jnp.stack(places)

        weight_near = xor_send(output_weight, "fsdp", fsdp_size, 1)

        attended = [attend_chip(valid_token_count, queries, keys, values, c, depth, limit=FIRST) for c in range(1, chips)]
        theirs = [xor_send(x, "fsdp", fsdp_size, 2 * (c + 1)) for c, x in enumerate(attended)]
        block = join_adapters(scalars, down_adapter, up_adapter, attended[:1])
        outer_blocks = {
            o: xor_send(block, "frame", frame_size, o * inner)
            for o in sorted(range(1, outer), key=lambda o: -o.bit_length())
        }
        own = attend_chip(valid_token_count, queries, keys, values, 0, depth, [block, weight_near])
        attended = [own] + attended

        weight_near, own_slot = bring_weight(
            scalars, weight_near, scene_of_frame, scene_adapter_row, [own]
        )
        near_slots = [own_slot] + [xor_send(own_slot, "fsdp", fsdp_size, 2 * c) for c in range(1, chips)]
        partials = []
        after = [own]
        for c, x in enumerate(theirs):
            part = project(scalars, x, output_weight, weight_near, c + 1, fsdp_size, after)
            partials.append(xor_send(part, "fsdp", fsdp_size, 2 * (c + 1)))
        stacked, others, near_slots = stack_blocks(
            scalars,
            [*outer_blocks.values(), block],
            [*outer_blocks, 0],
            [own, *theirs],
            near_slots,
            [part],
        )
        slot_list = [x for slot in near_slots for x in (slot, xor_send(slot, "fsdp", fsdp_size, 1))]
        far_blocks = [xor_send(stacked, "frame", frame_size, s) for s in range(1, inner)]
        base = base_error(
            scalars,
            own,
            output_weight,
            weight_near,
            residual,
            target,
            fsdp_size,
            [stacked],
        )
        blocks = [((stacked, *far_blocks)[s], o) for o in range(outer) for s in range(inner)]

        columns = [None] * fsdp_size
        for c, (x, other) in enumerate(zip([own] + theirs, others)):
            columns[2 * c] = x[0]
            columns[2 * c + 1] = xor_send(other, "fsdp", fsdp_size, 1)

        chosen, low_part = choose_adapters(scalars, slot_list, blocks, columns, [base])
        adapters = send_shards(chosen)
        pieces, loss = error_terms(scalars, base, partials, low_part, adapters)
        pieces = send_shards(pieces)

        cut = depth // 2 // LANES * LANES
        first_shape = first_shapes(rank, depth + cut, along_inner) + first_shapes(rank, depth - cut, along_outer)
        second_shape = second_shapes(rank, depth + cut, along_inner) + second_shapes(
            rank, depth - cut, along_outer
        )

        def first(sc, *refs):
            slot_refs, got, cols = (refs[i * fsdp_size : (i + 1) * fsdp_size] for i in range(3))
            got = got[::-1]
            outs = refs[3 * fsdp_size :]
            offsets = [slot_offset(sc, ref) for ref in slot_refs]
            downs = [dot(unfold(p, rank, slots), c[...], 1, 0) for p, c in zip(got, cols)]
            down_outs = [ref.at[:, :, :depth] for ref in outs[:inner]]
            first_refs(offsets, downs, down_outs[0], down_outs[1:], *along_inner)
            ups = [p[:rank, :cut].astype(F32) for p in got]
            up_outs = [ref.at[:, :, depth:] for ref in outs[:inner]]
            first_refs(offsets, ups, up_outs[0], up_outs[1:], *along_inner)
            ups = [p[:rank, cut:depth].astype(F32) for p in got]
            first_refs(offsets, ups, outs[inner], outs[inner + 1 :], *along_outer)

        far = [o for o in range(1, outer) if 2 * o >= outer]
        near = [o for o in range(1, outer) if 2 * o < outer]
        order = [0, inner, *[inner + o for o in far], *range(1, inner), *[inner + o for o in near]]
        out = ordered_call(first, "first", scalars, (*slot_list, *pieces[::-1], *columns), first_shape, 2.0, order)
        keeps = out[0], out[inner]
        outer_got = send_frames(out[inner + 1 :], inner)
        inner_got = send_frames(out[1:inner], 1)

        ways = [("outer", o) for o in far] + [("inner", i) for i in range(1, inner)] + [("outer", o) for o in near]

        def second(sc, inner_keep, outer_keep, *refs):
            got = dict(zip(ways, refs))
            outs = refs[len(ways) :]
            inners = [got["inner", i] for i in range(1, inner)]
            outers = [got["outer", o] for o in range(1, outer)]
            second_refs(inner_keep, inners, outs[0], outs[1:outer], outer)
            second_refs(outer_keep, outers, outs[outer], outs[outer + 1 :], inner)

        order = [0, outer, *far, *near, *[outer + i for i in range(1, inner)]]
        sent = {"inner": inner_got, "outer": outer_got}
        operands = (*keeps, *[sent[way][i - 1] for way, i in ways])
        out = ordered_call(second, "second", scalars, operands, second_shape, 0.8, order)
        sent = send_frames(out[1:outer], inner)
        one = (out[0], *[sent[o - 1] for o in far + near])
        two = (out[outer], *send_frames(out[outer + 1 :], 1))

        def finish(sc, *refs):
            down_ref, up_ref = refs[-2:]
            for part, which in ((0, refs[: len(one)]), (1, refs[len(one) : -2])):
                total = which[0][...]
                for ref in which[1:]:
                    total = total + ref[...].astype(F32)
                if part == 0:
                    down_ref[0] = total[:, :depth]
                    up_ref[0, :, :cut] = total[:, depth:]
                else:
                    up_ref[0, :, cut:] = total

        grad = shaped((1, rank, depth), F32)
        grad_down, grad_up = kernel_call(finish, "finish", scalars, (*one, *two), [grad, grad], 1.3)
        return grad_down, grad_up, loss[0]

    return per_device


def solution(mesh):
    frame_size, fsdp_size = mesh.shape["frame"], mesh.shape["fsdp"]
    rows = P(("frame", "fsdp"), None, None)
    adapter = P("frame", None, "fsdp")
    vector = P(("frame", "fsdp"))
    placed = (rows, rows, rows, rows, rows, P("fsdp", None), adapter, adapter, vector, P(), vector)
    chunked = make_chunked(frame_size, fsdp_size)
    general = make_general(frame_size, fsdp_size)

    def per_device(*operands):
        depth = operands[5].shape[0]
        return (chunked if depth % (3 * LANES) == 0 and depth <= 4 * operands[0].shape[1] else general)(*operands)

    return jax.shard_map(
        per_device,
        mesh=mesh,
        in_specs=placed,
        out_specs=(adapter, adapter, vector),
        check_vma=False,
    )
```
